32 devices in a mesh: dp: 8 (over y, x, core), tensor: 4 (over z).
Axes of the slice: x: 2, y: 2, z: 4, core: 2. Of those that a mesh axis runs over, the one named last changes fastest.
Arguments:
- hidden_in: bfloat16 [8192, 768], P('dp'), may hold values from -6 to 6
- visual_feats: bfloat16 [128, 257, 1408], P('dp'), may hold values from -6 to 6
- caption_lengths: int32 [128, 4], P('dp'), may hold values from 1 to 16, 32 in all within a row
- self_qkv: bfloat16 [3, 768, 768], P(None, None, 'tensor'), may hold values from -0.21875 to 0.21875
- self_out: bfloat16 [768, 768], P('tensor'), may hold values from -0.875 to 0.875
- cross_query: bfloat16 [768, 768], P(None, 'tensor'), may hold values from -0.21875 to 0.21875
- cross_kv: bfloat16 [2, 1408, 768], P(None, None, 'tensor'), may hold values from -0.15625 to 0.15625
- cross_out: bfloat16 [768, 768], P('tensor'), may hold values from -1.25 to 1.25
- ffn_in: bfloat16 [2, 768, 3072], P(None, None, 'tensor'), may hold values from -0.21875 to 0.21875
- ffn_out: bfloat16 [2, 3072, 768], P(None, 'tensor'), may hold values from -0.109375 to 0.109375
- norm_gain: float32 [4, 768], replicated, may hold values from 0.5 to 1.5
- norm_shift: float32 [4, 768], replicated, may hold values from -3 to 3
- out_grad: bfloat16 [8192, 768], P('dp'), may hold values from -6 to 6
Outputs:
- block_out: bfloat16 [8192, 768], P('dp')
- grad_hidden: float32 [8192, 768], P('dp')
- grad_self_qkv: float32 [3, 768, 768], P(None, None, 'tensor')
- grad_self_out: float32 [768, 768], P('tensor')
- grad_cross_query: float32 [768, 768], P(None, 'tensor')
- grad_cross_kv: float32 [2, 1408, 768], P(None, None, 'tensor')
- grad_cross_out: float32 [768, 768], P('tensor')
- grad_ffn_in: float32 [2, 768, 3072], P(None, None, 'tensor')
- grad_ffn_out: float32 [2, 3072, 768], P(None, 'tensor')
- grad_norm_gain: float32 [4, 768], replicated
- grad_norm_shift: float32 [4, 768], replicated
The draws below stay inside these ranges and needn't reach their ends.
Inputs may be any that keep to these rules, and one draw needn't show every extreme that they name: `caption_lengths`: each item's 4 caption lengths sum to 32, and the longest caption of every item has exactly 16 tokens.
All inputs are finite; a program needn't handle non-finite values.
Results may differ from the reference program's by a relative error of at most 0.028.
Values may be sent and summed in bfloat16 or wider, within the bound.
A program may use at most 128 MiB of HBM per device.

```python
import math
import jax
import jax.numpy as jnp
import numpy as np
from jax import lax

D = 768
HEADS = 12
HEAD = 64
FF = 3072
NQ = 32
VIS = 257
VD = 1408
TXT = 32
CAPS = 4
CAP_MOST = 16
ITEMS_DEV = 16
ITEMS = 128
ROWS = 8192
N_DP = 8
N_TENSOR = 4


def block_scale(key, dims, cuts, smallest, top_value):
    factor_of = 1.0
    for axis_at, blocks in cuts:
        heights = jax.random.uniform(jax.random.fold_in(jax.random.fold_in(key, 6), axis_at), (blocks,), jnp.float32, smallest / len(cuts), top_value / len(cuts))
        factor_of = factor_of * jnp.repeat(jnp.exp(heights), dims[axis_at] // blocks).reshape((-1,) + (1,) * (len(dims) - 1 - axis_at))
    return factor_of


def profile(amount, total, most, skew):
    weights = [(1 << 20) // math.isqrt(rank ** skew) + 1 for rank in range(2, amount + 1)]
    spare, given = total - most - (amount - 1), [1] * (amount - 1)
    while spare > 0:
        movable = [i for i in range(amount - 1) if given[i] < most]
        mass, left = sum([weights[i] for i in movable]), spare
        for i in movable:
            more = min(most - given[i], max(1, left * weights[i] // mass), spare)
            given[i] = given[i] + more
            spare = spare - more
    return np.array([most] + given)


def ragged(rng, amount, total, limit, lean):
    if amount == 2:
        one = jax.random.randint(rng, (), max(1, total - limit), min(limit, total - 1) + 1)
        return jnp.stack([one, total - one])
    sizes = jnp.asarray(profile(amount, total, limit, lean), jnp.int32)
    twos = (amount - 1) // 2
    donor, receiver = sizes[1:1 + 2 * twos:2], sizes[2:2 + 2 * twos:2]
    margin = jnp.minimum(donor - 1, limit - receiver)
    shifted = jax.random.randint(jax.random.fold_in(rng, 1), (twos,), 0, 1 << 20) % (margin + 1)
    sizes = sizes.at[1:1 + 2 * twos:2].set(donor - shifted).at[2:2 + 2 * twos:2].set(receiver + shifted)
    return sizes[jax.random.permutation(jax.random.fold_in(rng, 2), amount)]


def bell_draw(key, dims, scale, limit, cuts=(), kind=jnp.bfloat16):
    entries = jax.random.normal(key, dims, jnp.float32) * scale
    if len(cuts) > 0:
        entries = block_scale(key, dims, cuts, -0.22, 0.18) * entries
    return jnp.clip(entries, min=-limit, max=limit).astype(kind)


def setup_inputs(seed: int = 0) -> dict:
    key_of = jax.random.split(jax.random.key(seed), 14)
    return {
        "hidden_in": bell_draw(key_of[0], (ROWS, D), 1.0, 6.0, ((0, 8),)),
        "visual_feats": bell_draw(key_of[1], (ITEMS, VIS, VD), 1.0, 6.0, ((0, 8),)),
        "caption_lengths": jax.vmap(lambda own: ragged(own, CAPS, TXT, CAP_MOST, 0))(jax.random.split(key_of[2], ITEMS)).reshape((ITEMS, CAPS)).astype(jnp.int32),
        "self_qkv": bell_draw(key_of[3], (3, D, D), D ** -0.5, 0.21875, ((2, 4),)),
        "self_out": bell_draw(key_of[4], (D, D), (D // 16) ** -0.5, 0.875, ((0, 4),)),
        "cross_query": bell_draw(key_of[5], (D, D), D ** -0.5, 0.21875, ((1, 4),)),
        "cross_kv": bell_draw(key_of[6], (2, VD, D), VD ** -0.5, 0.15625, ((2, 4),)),
        "cross_out": bell_draw(key_of[7], (D, D), (D // 32) ** -0.5, 1.25, ((0, 4),)),
        "ffn_in": bell_draw(key_of[8], (2, D, FF), D ** -0.5, 0.21875, ((2, 4),)),
        "ffn_out": bell_draw(key_of[9], (2, FF, D), FF ** -0.5, 0.109375, ((1, 4),)),
        "norm_gain": jnp.clip(1.0 + 0.1 * jax.random.normal(key_of[10], (4, D), jnp.float32), 0.5, 1.5),
        "norm_shift": bell_draw(key_of[11], (4, D), 0.5, 3.0, (), jnp.float32),
        "out_grad": bell_draw(key_of[12], (ROWS, D), 1.0, 6.0, ((0, 8),)),
    }


EPSILON = 1e-06
PRECISE = lax.Precision.HIGHEST
MASKED_SCORE = -1e+30

@jax.custom_vjp
def low(v):
    return lax.optimization_barrier(v.astype(jnp.bfloat16)).astype(jnp.float32)

@jax.custom_vjp
def low_back(v):
    return v

def low_keep(v):
    return (low(v), None)

def low_pass(kept, grad):
    return (grad,)

def back_keep(v):
    return (v, None)

def back_low(kept, grad):
    return (low(grad),)
low.defvjp(low_keep, low_pass)
low_back.defvjp(back_keep, back_low)

def normalize(residue, gain_row, shift_row):
    row_mean = lax.optimization_barrier(jnp.mean(residue, axis=-1, keepdims=True))
    centered = residue - row_mean
    variance = lax.optimization_barrier(jnp.mean(centered * centered, axis=-1, keepdims=True))
    return centered * lax.rsqrt(variance + EPSILON) * gain_row + shift_row

def allowed_of(lengths):
    caption_ends = jnp.cumsum(lengths, axis=-1, dtype=jnp.int32)
    places = jnp.arange(TXT, dtype=jnp.int32)
    segment = lax.optimization_barrier(jnp.sum((places[None, :, None] >= caption_ends[:, None, :]).astype(jnp.int32), axis=-1, dtype=jnp.int32))
    query_marks = jnp.full((lengths.shape[0], NQ), -1, dtype=jnp.int32)
    labels = jnp.concatenate([query_marks, segment], axis=1)
    return (labels[:, :, None] == labels[:, None, :]) | (labels[:, None, :] == -1)

def copies(value):
    return low_back(jnp.broadcast_to(value, (N_TENSOR,) + value.shape))

def split_in(spread, weight):
    shaped = weight.reshape(weight.shape[0], N_TENSOR, weight.shape[1] // N_TENSOR)
    result = jnp.einsum('gnrd,dgk->nrgk', spread, shaped, precision=PRECISE)
    return result.reshape(result.shape[0], result.shape[1], weight.shape[1])

def split_out(inputs, weight):
    shaped_in = inputs.reshape(inputs.shape[0], inputs.shape[1], N_TENSOR, inputs.shape[2] // N_TENSOR)
    shaped_w = weight.reshape(N_TENSOR, weight.shape[0] // N_TENSOR, weight.shape[1])
    partial_value = jnp.einsum('nrgk,gkd->gnrd', shaped_in, shaped_w, precision=PRECISE)
    return low_back(lax.optimization_barrier(jnp.sum(low(partial_value), axis=0)))

def heads_of(tensor):
    return tensor.reshape(tensor.shape[0], tensor.shape[1], HEADS, HEAD)

def attend(queries, key_heads, value_heads, allowed):
    scale_factor = 1.0 / math.sqrt(HEAD)
    scores = low_back(jnp.einsum('nrhe,nshe->nhrs', queries, key_heads, precision=PRECISE) * scale_factor)
    if allowed is not None:
        scores = jnp.where(allowed[:, None], scores, MASKED_SCORE)
    chances = low(jax.nn.softmax(scores, axis=-1))
    context = jnp.einsum('nhrs,nshe->nrhe', chances, value_heads, precision=PRECISE)
    context = low_back(low(context))
    return context.reshape(context.shape[0], context.shape[1], D)

def feed_forward(row_block, weight_in, weight_out):
    spread = copies(low(row_block))
    pre_act = low_back(split_in(spread, weight_in))
    active = low(jax.nn.gelu(pre_act, approximate=False))
    return split_out(active, weight_out)

def forward(hidden, visual, allowed, self_qkv, self_out, cross_query, cross_kv, cross_out, ffn_in, ffn_out, norm_gain, norm_shift):
    shared = copies(hidden)
    query_self = low_back(low(split_in(shared, self_qkv[0])))
    key_self = low_back(low(split_in(shared, self_qkv[1])))
    value_self = low_back(low(split_in(shared, self_qkv[2])))
    self_context = attend(heads_of(query_self), heads_of(key_self), heads_of(value_self), allowed)
    first_norm = normalize(hidden + split_out(self_context, self_out), norm_gain[0], norm_shift[0])
    query_rows = first_norm[:, :NQ]
    text_rows = first_norm[:, NQ:]
    query_in = copies(low(query_rows))
    cross_q = low_back(low(split_in(query_in, cross_query)))
    cross_keys = low_back(low(jnp.einsum('nvc,cd->nvd', visual, cross_kv[0], precision=PRECISE)))
    cross_values = low_back(low(jnp.einsum('nvc,cd->nvd', visual, cross_kv[1], precision=PRECISE)))
    cross_context = attend(heads_of(cross_q), heads_of(cross_keys), heads_of(cross_values), None)
    second_norm = normalize(query_rows + split_out(cross_context, cross_out), norm_gain[1], norm_shift[1])
    out_query = normalize(second_norm + feed_forward(second_norm, ffn_in[0], ffn_out[0]), norm_gain[2], norm_shift[2])
    out_text = normalize(text_rows + feed_forward(text_rows, ffn_in[1], ffn_out[1]), norm_gain[3], norm_shift[3])
    return jnp.concatenate([out_query, out_text], axis=1)

def to_wide(source):
    return source.astype(jnp.float32)

def reference(hidden_in, visual_feats, caption_lengths, self_qkv, self_out, cross_query, cross_kv, cross_out, ffn_in, ffn_out, norm_gain, norm_shift, out_grad):
    row_span = NQ + TXT
    params = tuple(map(to_wide, (self_qkv, self_out, cross_query, cross_kv, cross_out, ffn_in, ffn_out, norm_gain, norm_shift)))
    hidden = to_wide(hidden_in).reshape(N_DP, ITEMS_DEV, row_span, D)
    visual = to_wide(visual_feats).reshape(N_DP, ITEMS_DEV, VIS, VD)
    lengths = caption_lengths.reshape(N_DP, ITEMS_DEV, CAPS)
    cotangent = to_wide(out_grad).reshape(N_DP, ITEMS_DEV, row_span, D)

    def group_step(totals, pieces):
        item_block, visual_block, length_block, grad_block = pieces
        allowed = allowed_of(length_block)

        def run_block(block_in, *weights):
            return forward(block_in, visual_block, allowed, *weights)
        result, pullback = jax.vjp(run_block, item_block, *params)
        gradients = pullback(grad_block)
        totals = tuple((total_item + grad_item for total_item, grad_item in zip(totals, gradients[1:])))
        return (totals, (result.astype(jnp.bfloat16), gradients[0]))
    start = tuple((jnp.zeros_like(weight_item) for weight_item in params))
    totals, (outputs, grad_rows) = lax.scan(group_step, start, (hidden, visual, lengths, cotangent))
    all_rows = N_DP * ITEMS_DEV * row_span
    return (outputs.reshape(all_rows, D), grad_rows.reshape(all_rows, D), totals[0], totals[1], totals[2], totals[3], totals[4], totals[5], totals[6], totals[7], totals[8])
```

```python
import functools
import math

import jax
import jax.numpy as jnp
from jax import lax
from jax.experimental import pallas as pl
from jax.experimental.pallas import tpu as pltpu
from jax.sharding import PartitionSpec as P

HEAD = 64
NQ = 32
TXT = 32
QUAD = 4
EPSILON = 1e-06
MASKED_SCORE = -1e30
SCALE = 1.0 / math.sqrt(HEAD)
WIDE = jnp.float32
NARROW = jnp.bfloat16
VMEM_BYTES = 56 * 2**20


def mm(a, b):
    return lax.dot_general(a, b, (((1,), (0,)), ((), ())), preferred_element_type=WIDE)


def mm_nt(a, b):
    return lax.dot_general(a, b, (((1,), (1,)), ((), ())), preferred_element_type=WIDE)


def mm_tn(a, b):
    return lax.dot_general(a, b, (((0,), (0,)), ((), ())), preferred_element_type=WIDE)


def lane_group(rows, lanes, size):
    return lax.broadcasted_iota(jnp.int32, (rows, lanes), 1) // size


def spread_heads(block, count):
    rows, lanes = block.shape
    group = lane_group(rows, lanes, HEAD)
    wide = block.astype(WIDE)
    return jnp.concatenate(
        [jnp.where(group == h, wide, 0.0).astype(NARROW) for h in range(count)], axis=0
    )


def gather_heads(block, count):
    rows, lanes = block.shape[0] // count, block.shape[1]
    group = lane_group(rows, lanes, HEAD)
    out = block[:rows]
    for h in range(1, count):
        out = jnp.where(group == h, block[h * rows : (h + 1) * rows], out)
    return out


def norm_parts(residue):
    mean = jnp.mean(residue, axis=-1, keepdims=True)
    centered = residue - mean
    variance = jnp.mean(centered * centered, axis=-1, keepdims=True)
    inverse = lax.rsqrt(variance + EPSILON)
    return centered * inverse, inverse


def norm_back(unit, inverse, gain_row, cotangent):
    scaled = gain_row * cotangent
    first = jnp.mean(scaled, axis=-1, keepdims=True)
    second = jnp.mean(scaled * unit, axis=-1, keepdims=True)
    return inverse * (scaled - first - unit * second)


def column_sums(unit, cotangent):
    return (
        jnp.sum(cotangent * unit, axis=0, keepdims=True),
        jnp.sum(cotangent, axis=0, keepdims=True),
    )


def gelu_parts(pre):
    bell = jnp.exp(-0.5 * pre * pre)
    half = 0.5 * lax.erf(pre * math.sqrt(0.5)) + 0.5
    return pre * half, half + pre * bell * (1.0 / math.sqrt(2.0 * math.pi))


def labels_of(position, ends):
    place = position - NQ
    label = jnp.zeros_like(position)
    for end in ends:
        label = label + jnp.where(place >= end, 1, 0)
    return jnp.where(position < NQ, -1, label)


def allowed_pairs(lens_ref, item, span, lanes):
    ends = []
    total = jnp.int32(0)
    for c in range(lens_ref.shape[1]):
        total = total + lens_ref[item, c]
        ends.append(total)
    key_label = labels_of(lax.broadcasted_iota(jnp.int32, (span, lanes), 0), ends)
    query_label = labels_of(lax.broadcasted_iota(jnp.int32, (span, lanes), 1) % span, ends)
    return (key_label == query_label) | (key_label == -1)


def self_forward_kernel(
    lens_ref, x_ref, w_ref, gain_ref, shift_ref,
    q_ref, k_ref, v_ref, p_ref, ctx_ref, res_ref, fq_ref, ft_ref,
):
    span = NQ + TXT
    items = x_ref.shape[0] // span
    lanes = QUAD * HEAD
    x = x_ref[...]
    q_ref[...] = (mm_nt(x, w_ref[0]) .astype(NARROW).astype(WIDE) * SCALE).astype(NARROW)
    k_ref[...] = mm_nt(x, w_ref[1]).astype(NARROW)
    v_ref[...] = mm_nt(x, w_ref[2]).astype(NARROW)

    @pl.loop(0, items)
    def _(item):
        rows = pl.ds(pl.multiple_of(item * span, span), span)
        allowed = allowed_pairs(lens_ref, pl.program_id(0) * items + item, span, lanes)
        for quad in range(x_ref.shape[1] // lanes):
            cols = slice(quad * lanes, (quad + 1) * lanes)
            scores = mm_nt(k_ref[rows, cols], spread_heads(q_ref[rows, cols], QUAD))
            scores = jnp.where(allowed, scores, MASKED_SCORE)
            lifted = jnp.exp(scores - jnp.max(scores, axis=0, keepdims=True))
            chances = lifted * (1.0 / jnp.sum(lifted, axis=0, keepdims=True))
            low = chances.astype(NARROW)
            p_ref[rows, cols] = low
            ctx_ref[rows, cols] = gather_heads(mm_tn(low, v_ref[rows, cols]), QUAD).astype(NARROW)

    residue = x.astype(WIDE) + mm(ctx_ref[...], w_ref[3])
    res_ref[...] = residue
    unit, _ = norm_parts(residue)
    first = unit * gain_ref[0:1] + shift_ref[0:1]
    for item in range(items):
        fq_ref[item * NQ : (item + 1) * NQ] = first[item * span : item * span + NQ]
        ft_ref[item * TXT : (item + 1) * TXT] = first[item * span + NQ : (item + 1) * span]


def self_forward(hidden, lens, weights, gain, shift):
    rows, width = hidden.shape
    block = min(rows, 256)
    half = block // 2
    full = pl.BlockSpec((block, width), lambda i: (i, 0))
    halves = pl.BlockSpec((half, width), lambda i: (i, 0))
    low = jax.ShapeDtypeStruct((rows, width), NARROW)
    return pl.pallas_call(
        self_forward_kernel,
        grid=(rows // block,),
        in_specs=[
            pl.BlockSpec(memory_space=pltpu.SMEM),
            full,
            pl.BlockSpec(weights.shape, lambda i: (0, 0, 0)),
            pl.BlockSpec(gain.shape, lambda i: (0, 0)),
            pl.BlockSpec(shift.shape, lambda i: (0, 0)),
        ],
        out_specs=[full, full, full, full, full, full, halves, halves],
        out_shape=[
            low, low, low, low, low,
            jax.ShapeDtypeStruct((rows, width), WIDE),
            jax.ShapeDtypeStruct((rows // 2, width), WIDE),
            jax.ShapeDtypeStruct((rows // 2, width), WIDE),
        ],
        compiler_params=pltpu.CompilerParams(vmem_limit_bytes=VMEM_BYTES),
        name="self_forward",
    )(lens, hidden, weights, gain, shift)


def self_backward_kernel(
    own_ref, x_ref, w_ref, gain_ref, res_ref, gq_ref, gt_ref, q_ref, k_ref, v_ref, p_ref, ctx_ref,
    grad_ref, gqkv_ref, gout_ref, gain_out, shift_out,
    down, dctx, dq, dk, dv, acc,
):
    span = NQ + TXT
    block = res_ref.shape[0]
    items = block // span
    lanes = QUAD * HEAD
    step = pl.program_id(0)
    unit, inverse = norm_parts(res_ref[...])
    pieces = []
    for item in range(items):
        pieces.append(gq_ref[item * NQ : (item + 1) * NQ])
        pieces.append(gt_ref[item * TXT : (item + 1) * TXT])
    cotangent = jnp.concatenate(pieces, axis=0)
    grad_res = norm_back(unit, inverse, gain_ref[0:1], cotangent)
    gain_sum, shift_sum = column_sums(unit, cotangent)

    @pl.when(step == 0)
    def _():
        gain_out[...] = gain_sum
        shift_out[...] = shift_sum

    @pl.when(step > 0)
    def _():
        gain_out[...] += gain_sum
        shift_out[...] += shift_sum

    grad_ref[...] = grad_res
    low = grad_res.astype(NARROW)
    down[...] = low
    dctx[...] = mm_nt(low, w_ref[3]).astype(NARROW)

    @pl.loop(0, items)
    def _(item):
        rows = pl.ds(pl.multiple_of(item * span, span), span)
        for quad in range(w_ref.shape[2] // lanes):
            cols = slice(quad * lanes, (quad + 1) * lanes)
            chances = p_ref[rows, cols]
            spread = spread_heads(dctx[rows, cols], QUAD)
            grad_chances = mm_nt(v_ref[rows, cols], spread)
            weighted = chances.astype(WIDE)
            inner = jnp.sum(grad_chances * weighted, axis=0, keepdims=True)
            scores = (weighted * (grad_chances - inner)).astype(NARROW)
            dk[rows, cols] = mm(scores, spread_heads(q_ref[rows, cols], QUAD)).astype(NARROW)
            dv[rows, cols] = mm(chances, spread).astype(NARROW)
            dq[rows, cols] = (gather_heads(mm_tn(scores, k_ref[rows, cols]), QUAD) * SCALE).astype(
                NARROW
            )

    grad_ref[...] += mm(dq[...], w_ref[0]) + mm(dk[...], w_ref[1]) + mm(dv[...], w_ref[2])

    own = own_ref[0]
    cols = gqkv_ref.shape[1]
    window = acc.shape[1]
    start = pl.multiple_of((own * cols) // 128 * 128, 128)
    here = pl.ds(start, window)
    x = x_ref[...]
    parts = (
        mm_tn(dq[:, here], x), mm_tn(dk[:, here], x), mm_tn(dv[:, here], x),
        mm_tn(ctx_ref[:, here], down[...]),
    )

    @pl.when(step == 0)
    def _():
        for c, part in enumerate(parts):
            acc[c] = part

    @pl.when(step > 0)
    def _():
        for c, part in enumerate(parts):
            acc[c] += part

    @pl.when(step == pl.num_programs(0) - 1)
    def _():
        offset = pl.multiple_of(own * cols - start, 64)
        for c in range(3):
            gqkv_ref[c] = acc[c, pl.ds(offset, cols), :].astype(gqkv_ref.dtype)
        gout_ref[...] = acc[3, pl.ds(offset, cols), :].astype(gout_ref.dtype)


def self_backward(own, hidden, weights, gain, residue, grad_q, grad_t, q, k, v, p, ctx, cols):
    rows, width = hidden.shape
    block = min(rows, 256)
    half = block // 2
    full = pl.BlockSpec((block, width), lambda i: (i, 0))
    halves = pl.BlockSpec((half, width), lambda i: (i, 0))
    row = pl.BlockSpec((1, width), lambda i: (0, 0))
    return pl.pallas_call(
        self_backward_kernel,
        grid=(rows // block,),
        in_specs=[
            pl.BlockSpec(memory_space=pltpu.SMEM),
            full,
            pl.BlockSpec(weights.shape, lambda i: (0, 0, 0)),
            pl.BlockSpec(gain.shape, lambda i: (0, 0)),
            full, halves, halves, full, full, full, full, full,
        ],
        out_specs=[
            full,
            pl.BlockSpec((3, cols, width), lambda i: (0, 0, 0)),
            pl.BlockSpec((cols, width), lambda i: (0, 0)),
            row, row,
        ],
        out_shape=[
            jax.ShapeDtypeStruct((rows, width), WIDE),
            jax.ShapeDtypeStruct((3, cols, width), NARROW),
            jax.ShapeDtypeStruct((cols, width), NARROW),
            jax.ShapeDtypeStruct((1, width), WIDE),
            jax.ShapeDtypeStruct((1, width), WIDE),
        ],
        scratch_shapes=[pltpu.VMEM((block, width), NARROW)] * 5
        + [pltpu.VMEM((4, (cols + 64 + 127) // 128 * 128, width), WIDE)],
        compiler_params=pltpu.CompilerParams(vmem_limit_bytes=VMEM_BYTES),
        name="self_backward",
    )(own, hidden, weights, gain, residue, grad_q, grad_t, q, k, v, p, ctx)


def visual_forward_kernel(x_ref, w_ref, k_ref, v_ref):
    x = x_ref[0]
    k_ref[0] = mm_nt(x, w_ref[0]).astype(NARROW)
    v_ref[0] = mm_nt(x, w_ref[1]).astype(NARROW)


def visual_forward(visual, weights):
    items, span, depth = visual.shape
    cols = weights.shape[1]
    out = pl.BlockSpec((1, span, cols), lambda i: (i, 0, 0))
    shape = jax.ShapeDtypeStruct((items, span, cols), NARROW)
    return pl.pallas_call(
        visual_forward_kernel,
        grid=(items,),
        in_specs=[
            pl.BlockSpec((1, span, depth), lambda i: (i, 0, 0)),
            pl.BlockSpec(weights.shape, lambda i: (0, 0, 0)),
        ],
        out_specs=[out, out],
        out_shape=[shape, shape],
        compiler_params=pltpu.CompilerParams(vmem_limit_bytes=VMEM_BYTES),
        name="visual_forward",
    )(visual, weights)


def cross_forward_kernel(x_ref, wq_ref, wo_ref, k_ref, v_ref, q_ref, p_ref, ctx_ref, part_ref):
    items = k_ref.shape[0]
    heads = q_ref.shape[1] // HEAD
    q_ref[...] = (
        mm_nt(x_ref[...].astype(NARROW), wq_ref[...]).astype(NARROW).astype(WIDE) * SCALE
    ).astype(NARROW)
    for item in range(items):
        rows = slice(item * NQ, (item + 1) * NQ)
        scores = mm_nt(k_ref[item], spread_heads(q_ref[rows], heads))
        lifted = jnp.exp(scores - jnp.max(scores, axis=0, keepdims=True))
        chances = (lifted * (1.0 / jnp.sum(lifted, axis=0, keepdims=True))).astype(NARROW)
        p_ref[item] = chances
        ctx_ref[rows] = gather_heads(mm_tn(chances, v_ref[item]), heads).astype(NARROW)
    part_ref[...] = mm(ctx_ref[...], wo_ref[...]).astype(NARROW)


def cross_forward(rows_q, wq, wo, k, v):
    rows, width = rows_q.shape
    items, span, cols = k.shape
    step = min(items, 4)
    heads = cols // HEAD
    block = step * NQ

    def by_rows(lanes):
        return pl.BlockSpec((block, lanes), lambda i: (i, 0))

    def by_items(lanes):
        return pl.BlockSpec((step, span, lanes), lambda i: (i, 0, 0))

    return pl.pallas_call(
        cross_forward_kernel,
        grid=(items // step,),
        in_specs=[
            by_rows(width),
            pl.BlockSpec(wq.shape, lambda i: (0, 0)),
            pl.BlockSpec(wo.shape, lambda i: (0, 0)),
            by_items(cols), by_items(cols),
        ],
        out_specs=[by_rows(cols), by_items(heads * NQ), by_rows(cols), by_rows(width)],
        out_shape=[
            jax.ShapeDtypeStruct((rows, cols), NARROW),
            jax.ShapeDtypeStruct((items, span, heads * NQ), NARROW),
            jax.ShapeDtypeStruct((rows, cols), NARROW),
            jax.ShapeDtypeStruct((rows, width), NARROW),
        ],
        compiler_params=pltpu.CompilerParams(vmem_limit_bytes=VMEM_BYTES),
        name="cross_forward",
    )(rows_q, wq, wo, k, v)


def cross_backward_kernel(
    down_ref, fq_ref, wq_ref, wo_ref, q_ref, k_ref, v_ref, p_ref, ctx_ref,
    part_ref, dk_ref, dv_ref, gq_ref, go_ref, dctx, dq, acc,
):
    items = k_ref.shape[0]
    heads = q_ref.shape[1] // HEAD
    step = pl.program_id(0)
    dctx[...] = mm_nt(down_ref[...], wo_ref[...]).astype(NARROW)
    for item in range(items):
        rows = slice(item * NQ, (item + 1) * NQ)
        chances = p_ref[item]
        spread = spread_heads(dctx[rows], heads)
        grad_chances = mm_nt(v_ref[item], spread)
        weighted = chances.astype(WIDE)
        inner = jnp.sum(grad_chances * weighted, axis=0, keepdims=True)
        scores = (weighted * (grad_chances - inner)).astype(NARROW)
        dk_ref[item] = mm(scores, spread_heads(q_ref[rows], heads)).astype(NARROW)
        dv_ref[item] = mm(chances, spread).astype(NARROW)
        dq[rows] = (gather_heads(mm_tn(scores, k_ref[item]), heads) * SCALE).astype(NARROW)
    part_ref[...] = mm(dq[...], wq_ref[...]).astype(NARROW)
    grad_q = mm_tn(dq[...], fq_ref[...].astype(NARROW))
    grad_o = mm_tn(ctx_ref[...], down_ref[...])

    @pl.when(step == 0)
    def _():
        acc[0] = grad_q
        acc[1] = grad_o

    @pl.when(step > 0)
    def _():
        acc[0] += grad_q
        acc[1] += grad_o

    @pl.when(step == pl.num_programs(0) - 1)
    def _():
        gq_ref[...] = acc[0].astype(gq_ref.dtype)
        go_ref[...] = acc[1].astype(go_ref.dtype)


def cross_backward(down, rows_q, wq, wo, q, k, v, p, ctx):
    rows, width = down.shape
    items, span, cols = k.shape
    step = min(items, 4)
    heads = cols // HEAD
    block = step * NQ

    def by_rows(lanes):
        return pl.BlockSpec((block, lanes), lambda i: (i, 0))

    def by_items(lanes):
        return pl.BlockSpec((step, span, lanes), lambda i: (i, 0, 0))

    whole = pl.BlockSpec(wq.shape, lambda i: (0, 0))
    low = jax.ShapeDtypeStruct((items, span, cols), NARROW)
    grads = jax.ShapeDtypeStruct((cols, width), NARROW)
    return pl.pallas_call(
        cross_backward_kernel,
        grid=(items // step,),
        in_specs=[
            by_rows(width), by_rows(width), whole, whole,
            by_rows(cols), by_items(cols), by_items(cols), by_items(heads * NQ), by_rows(cols),
        ],
        out_specs=[by_rows(width), by_items(cols), by_items(cols), whole, whole],
        out_shape=[jax.ShapeDtypeStruct((rows, width), NARROW), low, low, grads, grads],
        scratch_shapes=[
            pltpu.VMEM((block, cols), NARROW),
            pltpu.VMEM((block, cols), NARROW),
            pltpu.VMEM((2, cols, width), WIDE),
        ],
        compiler_params=pltpu.CompilerParams(vmem_limit_bytes=VMEM_BYTES),
        name="cross_backward",
    )(down, rows_q, wq, wo, q, k, v, p, ctx)


def visual_backward_kernel(x_ref, dk_ref, dv_ref, out_ref, acc, tail_x, tail_k, tail_v):
    step = pl.program_id(0)
    span = x_ref.shape[1]
    even = span // 128 * 128
    x = x_ref[0, :even]
    part_k = mm_tn(dk_ref[0, :even], x)
    part_v = mm_tn(dv_ref[0, :even], x)

    @pl.when(step == 0)
    def _():
        acc[0] = part_k
        acc[1] = part_v
        tail_x[...] = jnp.zeros_like(tail_x)
        tail_k[...] = jnp.zeros_like(tail_k)
        tail_v[...] = jnp.zeros_like(tail_v)

    @pl.when(step > 0)
    def _():
        acc[0] += part_k
        acc[1] += part_v

    if span > even:
        here = pl.ds(step * (span - even), span - even)
        tail_x[here] = x_ref[0, even:].astype(WIDE)
        tail_k[here] = dk_ref[0, even:].astype(WIDE)
        tail_v[here] = dv_ref[0, even:].astype(WIDE)

    @pl.when(step == pl.num_programs(0) - 1)
    def _():
        x = tail_x[...].astype(NARROW)
        out_ref[0] = (acc[0] + mm_tn(tail_k[...].astype(NARROW), x)).astype(out_ref.dtype)
        out_ref[1] = (acc[1] + mm_tn(tail_v[...].astype(NARROW), x)).astype(out_ref.dtype)


def visual_backward(visual, dk, dv):
    items, span, depth = visual.shape
    cols = dk.shape[2]
    tail = max(16, (items * (span % 128) + 15) // 16 * 16)
    return pl.pallas_call(
        visual_backward_kernel,
        grid=(items,),
        in_specs=[
            pl.BlockSpec((1, span, depth), lambda i: (i, 0, 0)),
            pl.BlockSpec((1, span, cols), lambda i: (i, 0, 0)),
            pl.BlockSpec((1, span, cols), lambda i: (i, 0, 0)),
        ],
        out_specs=pl.BlockSpec((2, cols, depth), lambda i: (0, 0, 0)),
        out_shape=jax.ShapeDtypeStruct((2, cols, depth), NARROW),
        scratch_shapes=[
            pltpu.VMEM((2, cols, depth), WIDE),
            pltpu.VMEM((tail, depth), WIDE),
            pltpu.VMEM((tail, cols), WIDE),
            pltpu.VMEM((tail, cols), WIDE),
        ],
        compiler_params=pltpu.CompilerParams(vmem_limit_bytes=VMEM_BYTES),
        name="visual_backward",
    )(visual, dk, dv)


def feed_kernel(
    own_ref, fq_ref, cross_ref, win_ref, wout_ref, gain_ref, shift_ref, cot_ref,
    out_ref, grad_ref, down_ref, low_ref, top_ref, act_ref, dpre_ref, gain_out, shift_out,
    unit1, inverse1, second, slopes, total,
):
    step = pl.program_id(0)
    chunks = slopes.shape[0]
    width = slopes.shape[2]
    per = act_ref.shape[1] // width
    chunk = lax.rem(step, chunks)
    mine = chunk // per == own_ref[0]
    place = pl.ds(pl.multiple_of(lax.rem(chunk, per) * width, width), width)

    @pl.when(step == 0)
    def _():
        unit, inverse = norm_parts(fq_ref[...] + cross_ref[...].astype(WIDE))
        unit1[...] = unit
        inverse1[...] = inverse
        value = unit * gain_ref[1:2] + shift_ref[1:2]
        second[...] = value
        low_ref[...] = value.astype(NARROW)
        total[...] = jnp.zeros_like(total)

    @pl.when(step < chunks)
    def _():
        act, slope = gelu_parts(mm(low_ref[...], win_ref[0]))
        slopes[chunk] = slope
        act = act.astype(NARROW)
        total[...] += mm(act, wout_ref[0])

        @pl.when(mine)
        def _():
            act_ref[:, place] = act

    @pl.when(step == chunks)
    def _():
        unit, inverse = norm_parts(second[...] + total[...])
        out_ref[...] = (unit * gain_ref[2:3] + shift_ref[2:3]).astype(NARROW)
        cotangent = cot_ref[...].astype(WIDE)
        gain_sum, shift_sum = column_sums(unit, cotangent)
        gain_out[1:2] = gain_sum
        shift_out[1:2] = shift_sum
        grad = norm_back(unit, inverse, gain_ref[2:3], cotangent)
        total[...] = grad
        top_ref[...] = grad.astype(NARROW)

    @pl.when(step >= chunks)
    def _():
        dpre = (mm_nt(top_ref[...], wout_ref[0]) * slopes[chunk]).astype(NARROW)
        total[...] += mm_nt(dpre, win_ref[0])

        @pl.when(mine)
        def _():
            dpre_ref[:, place] = dpre

    @pl.when(step == 2 * chunks - 1)
    def _():
        grad_second = total[...]
        gain_sum, shift_sum = column_sums(unit1[...], grad_second)
        gain_out[0:1] = gain_sum
        shift_out[0:1] = shift_sum
        grad = norm_back(unit1[...], inverse1[...], gain_ref[1:2], grad_second)
        grad_ref[...] = grad
        down_ref[...] = grad.astype(NARROW)


def feed_forward_back(own, rows_q, cross, win, wout, gain, shift, cotangent):
    rows, width = rows_q.shape
    shards, _, hidden = win.shape
    tile = 256 if hidden % 256 == 0 else hidden
    per = hidden // tile
    chunks = shards * per
    whole = pl.BlockSpec((rows, width), lambda i: (0, 0))
    owned = pl.BlockSpec((rows, hidden), lambda i: (0, 0))
    pair = pl.BlockSpec((2, width), lambda i: (0, 0))
    low = jax.ShapeDtypeStruct((rows, width), NARROW)
    mine = jax.ShapeDtypeStruct((rows, hidden), NARROW)
    two = jax.ShapeDtypeStruct((2, width), WIDE)
    return pl.pallas_call(
        feed_kernel,
        grid=(2 * chunks,),
        in_specs=[
            pl.BlockSpec(memory_space=pltpu.SMEM),
            whole, whole,
            pl.BlockSpec((1, width, tile), lambda i: ((i % chunks) // per, 0, (i % chunks) % per)),
            pl.BlockSpec((1, tile, width), lambda i: ((i % chunks) // per, (i % chunks) % per, 0)),
            pl.BlockSpec(gain.shape, lambda i: (0, 0)),
            pl.BlockSpec(shift.shape, lambda i: (0, 0)),
            whole,
        ],
        out_specs=[whole, whole, whole, whole, whole, owned, owned, pair, pair],
        out_shape=[
            low, jax.ShapeDtypeStruct((rows, width), WIDE), low, low, low, mine, mine, two, two,
        ],
        scratch_shapes=[
            pltpu.VMEM((rows, width), WIDE),
            pltpu.VMEM((rows, 1), WIDE),
            pltpu.VMEM((rows, width), WIDE),
            pltpu.VMEM((chunks, rows, tile), WIDE),
            pltpu.VMEM((rows, width), WIDE),
        ],
        compiler_params=pltpu.CompilerParams(vmem_limit_bytes=VMEM_BYTES),
        name="feed_query",
    )(own, rows_q, cross, win, wout, gain, shift, cotangent)


MESH = pl.DeviceIdType.MESH
PEERS = 8


def flip(index, bit):
    return index + bit - 2 * bit * ((index // bit) % 2)


def greet(targets):
    barrier = pltpu.get_barrier_semaphore()
    for target in targets:
        pl.semaphore_signal(barrier, inc=1, device_id=target, device_id_type=MESH)
    pl.semaphore_wait(barrier, len(targets))


def remote(src, dst, send, recv, target):
    return pltpu.make_async_remote_copy(
        src_ref=src, dst_ref=dst, send_sem=send, recv_sem=recv, device_id=target, device_id_type=MESH
    )


class Spread:
    def __init__(self, at, own_at, send, recv):
        self.at, self.own_at, self.send, self.recv = at, own_at, send, recv
        self.dp, self.tensor = lax.axis_index("dp"), lax.axis_index("tensor")
        self.shards = lax.axis_size("tensor")
        self.peer = self.dp % PEERS
        self.index = 0
        self.open = []

    def targets(self):
        along = [(self.dp, (self.tensor + s) % self.shards) for s in range(1, self.shards)]
        return along + [(flip(self.dp, bit), self.tensor) for bit in (2, 4, 1)]

    def copy(self, src, dst, target):
        self.index += 1
        made = remote(src, dst, self.send.at[self.index - 1], self.recv.at[self.index - 1], target)
        made.start()
        self.open.append(made)
        return made

    def along_tensor(self):
        return [
            self.copy(
                self.own_at(self.peer),
                self.at(self.tensor, self.peer, None),
                (self.dp, (self.tensor + s) % self.shards),
            )
            for s in range(1, self.shards)
        ]

    def others(self):
        return [(self.tensor + self.shards - s) % self.shards for s in range(1, self.shards)]

    def exchange(self, bit, peers, half, shards=None):
        target = (flip(self.dp, bit), self.tensor)
        return [
            self.copy(self.at(shard, peer, half), self.at(shard, peer, half), target)
            for shard in (self.others() if shards is None else shards)
            for peer in peers
        ]

    @staticmethod
    def arrived(copies):
        for made in copies:
            made.wait_recv()

    def finish(self):
        for made in self.open:
            made.wait_send()


def spread_copies(shards):
    return (shards - 1) * (1 + 2 + 4 + 4)


def reduce_chain(part, out, buf_in, buf_mid, sems, steps):
    send_pair, send_mid, send_out, recv_pair, recv_mid, recv_out = sems
    dp, tensor = lax.axis_index("dp"), lax.axis_index("tensor")
    side = tensor // 2
    other = 1 - side
    pair = (dp, tensor + 1 - 2 * (tensor % 2))
    across = (dp, 3 - tensor)
    middle = (tensor + side) % 2 == 1

    def to_pair(half, c):
        return remote(part.at[half, c], buf_in.at[half, c], send_pair.at[half, c], recv_pair.at[half, c], pair)

    def to_mid(c):
        return remote(buf_mid.at[0, c], buf_mid.at[1, c], send_mid.at[c], recv_mid.at[c], across)

    def final_across(half, c):
        return remote(out.at[half, c], out.at[half, c], send_out.at[0, c], recv_out.at[half, c], across)

    def final_pair(half, c):
        return remote(out.at[half, c], out.at[half, c], send_out.at[1 + (0 if half is side else 1), c], recv_out.at[half, c], pair)

    def wide(ref, *at):
        return ref[at].astype(WIDE)

    def begin():
        @pl.when(middle)
        def _():
            greet([pair, across])

        @pl.when(jnp.logical_not(middle))
        def _():
            greet([pair])
            for c in range(steps):
                to_pair(other, c).start()
                to_pair(side, c).start()

    def first(c):
        to_pair(other, c).wait_recv()
        buf_mid[0, c] = (wide(buf_in, other, c) + wide(part, other, c)).astype(buf_mid.dtype)
        to_mid(c).start()

    def second(c):
        to_pair(side, c).wait_recv()
        to_mid(c).wait_recv()
        out[side, c] = (wide(buf_in, side, c) + wide(buf_mid, 1, c) + wide(part, side, c)).astype(out.dtype)
        final_across(side, c).start()
        final_pair(side, c).start()

    def third(c):
        final_across(other, c).wait_recv()
        final_pair(other, c).start()

    def step(t):
        @pl.when(middle)
        def _():
            if t < steps:
                first(t)
            if 0 <= t - 1 < steps:
                second(t - 1)
            if 0 <= t - 2 < steps:
                third(t - 2)

    def end():
        @pl.when(middle)
        def _():
            for c in range(steps):
                to_mid(c).wait_send()
                final_across(side, c).wait_send()
                final_pair(side, c).wait_send()
                final_pair(other, c).wait_send()

        @pl.when(jnp.logical_not(middle))
        def _():
            for c in range(steps):
                to_pair(other, c).wait_send()
                to_pair(side, c).wait_send()
                final_pair(other, c).wait_recv()
                final_pair(side, c).wait_recv()

    return [begin] + [functools.partial(step, t) for t in range(steps + 2)] + [end]


def chain_scratch(steps, rows, width):
    dma = pltpu.SemaphoreType.DMA
    return [
        pltpu.VMEM((2, steps, rows, width), NARROW),
        pltpu.VMEM((2, steps, rows, width), NARROW),
        dma((2, steps)), dma((steps,)), dma((3, steps)),
        dma((2, steps)), dma((steps,)), dma((2, steps)),
    ]


def sum_shards_kernel(part, out, buf_in, buf_mid, *sems):
    for run in reduce_chain(part, out, buf_in, buf_mid, sems, part.shape[1]):
        run()


def sum_shards(part, ident):
    rows, width = part.shape
    steps = 8
    shape = (2, steps, rows // (2 * steps), width)
    vmem = pl.BlockSpec(memory_space=pltpu.VMEM)
    return pl.pallas_call(
        sum_shards_kernel,
        in_specs=[vmem],
        out_specs=vmem,
        out_shape=jax.ShapeDtypeStruct(shape, NARROW),
        scratch_shapes=chain_scratch(steps, shape[2], width),
        compiler_params=pltpu.CompilerParams(
            collective_id=ident, has_side_effects=True, vmem_limit_bytes=VMEM_BYTES
        ),
        name="sum_shards",
    )(part.reshape(shape)).reshape(rows, width)


def gather_shards(shard):
    peers = lax.axis_size("dp")
    rows = shard.shape[0] // peers
    own = lax.dynamic_slice_in_dim(shard, lax.axis_index("dp") * rows, rows, axis=0)
    whole = lax.all_gather(own, ("tensor", "dp"), axis=0, tiled=True)
    return whole.reshape((whole.shape[0] // shard.shape[0],) + shard.shape)


def sum_items(values):
    return lax.psum([v.astype(NARROW) for v in values], "dp")


def on_device(
    hidden_in,
    visual_feats,
    caption_lengths,
    self_qkv,
    self_out,
    cross_query,
    cross_kv,
    cross_out,
    ffn_in,
    ffn_out,
    norm_gain,
    norm_shift,
    out_grad,
):
    items = visual_feats.shape[0]
    rows, width = hidden_in.shape
    span = rows // items
    cols = self_qkv.shape[2]
    hidden = ffn_in.shape[2]
    own = lax.axis_index("tensor").reshape((1,)).astype(jnp.int32)
    shards = lax.axis_size("tensor")

    attn_own = jnp.concatenate([jnp.swapaxes(self_qkv, 1, 2), self_out[None]], axis=0)
    attn = gather_shards(attn_own.reshape(4 * cols, width)).reshape(shards, 4, cols, width)
    attn = jnp.swapaxes(attn, 0, 1).reshape(4, shards * cols, width)
    feed = gather_shards(jnp.concatenate([ffn_in[0], ffn_out[0]], axis=0))
    win_q, wout_q = feed[:, :width], feed[:, width:]

    cross_wq = jnp.swapaxes(cross_query, 0, 1)
    cross_k, cross_v = visual_forward(visual_feats, jnp.swapaxes(cross_kv, 1, 2))
    q, k, v, p, ctx, residue, first_q, first_t = self_forward(
        hidden_in, caption_lengths, attn, norm_gain, norm_shift
    )
    cq, cp, cctx, cross_part = cross_forward(first_q, cross_wq, cross_out, cross_k, cross_v)
    cross_sum = sum_shards(cross_part, 1)

    cot = out_grad.reshape(items, span, width)
    cot_q = cot[:, :NQ].reshape(items * NQ, width)
    cot_t = cot[:, NQ:].reshape(items * TXT, width)

    low_t = first_t.astype(NARROW)
    act_t, slope_t = gelu_parts(jnp.dot(low_t, ffn_in[1], preferred_element_type=WIDE))
    act_t = act_t.astype(NARROW)
    ffn_t = lax.psum(mm(act_t, ffn_out[1]).astype(NARROW), "tensor").astype(WIDE)
    unit, inverse = norm_parts(first_t + ffn_t)
    out_t = (unit * norm_gain[3:4] + norm_shift[3:4]).astype(NARROW)
    cot_t = cot_t.astype(WIDE)
    gain_t, shift_t = column_sums(unit, cot_t)
    grad_t = norm_back(unit, inverse, norm_gain[3:4], cot_t)
    top_t = grad_t.astype(NARROW)
    dpre_t = (mm_nt(top_t, ffn_out[1]) * slope_t).astype(NARROW)
    grad_t = grad_t + lax.psum(mm_nt(dpre_t, ffn_in[1]).astype(NARROW), "tensor").astype(WIDE)

    out_q, grad_second, down_q, low_q, top_q, act_q, dpre_q, gain_pair, shift_pair = feed_forward_back(
        own, first_q, cross_sum, win_q, wout_q, norm_gain, norm_shift, cot_q
    )
    back_part, dk, dv, g_cq, g_co = cross_backward(
        down_q, first_q, cross_wq, cross_out, cq, cross_k, cross_v, cp, cctx
    )
    grad_q = grad_second + sum_shards(back_part, 2).astype(WIDE)
    g_in = jnp.stack([mm_tn(low_q, dpre_q), mm_tn(low_t, dpre_t)])
    g_out = jnp.stack([mm_tn(act_q, top_q), mm_tn(act_t, top_t)])
    g_kv = visual_backward(visual_feats, dk, dv)
    grad_hidden, g_qkv, g_so, gain_first, shift_first = self_backward(
        own, hidden_in, attn, norm_gain, residue, grad_q, grad_t, q, k, v, p, ctx, cols
    )
    out = jnp.concatenate(
        [out_q.reshape(items, NQ, width), out_t.reshape(items, TXT, width)], axis=1
    ).reshape(rows, width)
    gains = jnp.concatenate([gain_first, gain_pair, gain_t, shift_first, shift_pair, shift_t])
    sums = sum_items([g_in, g_out, g_kv, g_cq, g_co, g_qkv, g_so, gains])
    g_in, g_out, g_kv, g_cq, g_co, g_qkv, g_so, gains = [s.astype(WIDE) for s in sums]
    return (
        out,
        grad_hidden,
        jnp.swapaxes(g_qkv, 1, 2),
        g_so,
        jnp.swapaxes(g_cq, 0, 1),
        jnp.swapaxes(g_kv, 1, 2),
        g_co,
        g_in,
        g_out,
        gains[:4],
        gains[4:],
    )


def solution(mesh):
    placed = (
        P("dp", None),
        P("dp", None, None),
        P("dp", None),
        P(None, None, "tensor"),
        P("tensor", None),
        P(None, "tensor"),
        P(None, None, "tensor"),
        P("tensor", None),
        P(None, None, "tensor"),
        P(None, "tensor", None),
        P(),
        P(),
        P("dp", None),
    )
    return jax.shard_map(
        on_device,
        mesh=mesh,
        in_specs=placed,
        out_specs=(
            P("dp", None),
            P("dp", None),
            P(None, None, "tensor"),
            P("tensor", None),
            P(None, "tensor"),
            P(None, None, "tensor"),
            P("tensor", None),
            P(None, None, "tensor"),
            P(None, "tensor", None),
            P(),
            P(),
        ),
        check_vma=False,
    )
```

```python
import functools
import math

import jax
import jax.numpy as jnp
from jax import lax
from jax.experimental import pallas as pl
from jax.experimental.pallas import tpu as pltpu
from jax.sharding import PartitionSpec as P

HEAD = 64
NQ = 32
TXT = 32
QUAD = 4
EPSILON = 1e-06
MASKED_SCORE = -1e30
SCALE = 1.0 / math.sqrt(HEAD)
WIDE = jnp.float32
NARROW = jnp.bfloat16
VMEM_BYTES = 56 * 2**20


def mm(a, b):
    return lax.dot_general(a, b, (((1,), (0,)), ((), ())), preferred_element_type=WIDE)


def mm_nt(a, b):
    return lax.dot_general(a, b, (((1,), (1,)), ((), ())), preferred_element_type=WIDE)


def mm_tn(a, b):
    return lax.dot_general(a, b, (((0,), (0,)), ((), ())), preferred_element_type=WIDE)


def lane_group(rows, lanes, size):
    return lax.broadcasted_iota(jnp.int32, (rows, lanes), 1) // size


def spread_heads(block, count):
    rows, lanes = block.shape
    group = lane_group(rows, lanes, HEAD)
    wide = block.astype(WIDE)
    return jnp.concatenate(
        [jnp.where(group == h, wide, 0.0).astype(NARROW) for h in range(count)], axis=0
    )


def gather_heads(block, count):
    rows, lanes = block.shape[0] // count, block.shape[1]
    group = lane_group(rows, lanes, HEAD)
    out = block[:rows]
    for h in range(1, count):
        out = jnp.where(group == h, block[h * rows : (h + 1) * rows], out)
    return out


def norm_parts(residue):
    mean = jnp.mean(residue, axis=-1, keepdims=True)
    centered = residue - mean
    variance = jnp.mean(centered * centered, axis=-1, keepdims=True)
    inverse = lax.rsqrt(variance + EPSILON)
    return centered * inverse, inverse


def norm_back(unit, inverse, gain_row, cotangent):
    scaled = gain_row * cotangent
    first = jnp.mean(scaled, axis=-1, keepdims=True)
    second = jnp.mean(scaled * unit, axis=-1, keepdims=True)
    return inverse * (scaled - first - unit * second)


def column_sums(unit, cotangent):
    return (
        jnp.sum(cotangent * unit, axis=0, keepdims=True),
        jnp.sum(cotangent, axis=0, keepdims=True),
    )


def gelu_parts(pre):
    bell = jnp.exp(-0.5 * pre * pre)
    half = 0.5 * lax.erf(pre * math.sqrt(0.5)) + 0.5
    return pre * half, half + pre * bell * (1.0 / math.sqrt(2.0 * math.pi))


MESH = pl.DeviceIdType.MESH
PEERS = 8


def flip(index, bit):
    return index + bit - 2 * bit * ((index // bit) % 2)


def greet(targets):
    barrier = pltpu.get_barrier_semaphore()
    for target in targets:
        pl.semaphore_signal(barrier, inc=1, device_id=target, device_id_type=MESH)
    pl.semaphore_wait(barrier, len(targets))


def remote(src, dst, send, recv, target):
    return pltpu.make_async_remote_copy(
        src_ref=src, dst_ref=dst, send_sem=send, recv_sem=recv, device_id=target, device_id_type=MESH
    )


class Spread:
    COPIES = 9

    def __init__(self, at, send, recv, base):
        self.at, self.send, self.recv, self.base = at, send, recv, base
        self.dp, self.tensor = lax.axis_index("dp"), lax.axis_index("tensor")
        self.shards = lax.axis_size("tensor")
        self.peer = self.dp % PEERS

    def hop(self, slot, s, src, dst, target):
        index = self.base + (s - 1) * self.COPIES + slot
        return remote(src, dst, self.send.at[index], self.recv.at[index], target)

    def came(self, s):
        return (self.tensor + self.shards - s) % self.shards

    def along(self, s, own):
        return self.hop(0, s, own, self.at(self.tensor, self.peer, None), (self.dp, (self.tensor + s) % self.shards))

    def hand(self, slot, s, bit, peer, half):
        place = self.at(self.came(s), peer, half)
        return self.hop(slot, s, place, place, (flip(self.dp, bit), self.tensor))

    def across(self, s):
        return [self.hand(1, s, 2, self.peer, None), self.hand(2, s, 4, self.peer, None), self.hand(3, s, 1, self.peer, None)]

    def onward(self, s):
        x, y = flip(self.peer, 2), flip(self.peer, 4)
        return (
            [self.hand(4, s, 4, x, 0), self.hand(5, s, 1, x, None)],
            [self.hand(6, s, 2, y, 1), self.hand(7, s, 1, y, None)],
        )

    def last(self, s):
        return self.hand(8, s, 1, flip(flip(self.peer, 2), 4), None)

    def start_across(self, s):
        for made in self.across(s):
            made.start()

    def start_onward(self, s):
        over_x, over_y, _ = self.across(s)
        by_x, by_y = self.onward(s)
        over_x.wait_recv()
        for made in by_x:
            made.start()
        over_y.wait_recv()
        for made in by_y:
            made.start()

    def start_last(self, s):
        by_x, by_y = self.onward(s)
        by_x[0].wait_recv()
        by_y[0].wait_recv()
        self.last(s).start()

    def finish(self, s):
        over = self.across(s)
        by_x, by_y = self.onward(s)
        final = self.last(s)
        for made in (over[2], by_x[1], by_y[1], final):
            made.wait_recv()
        for made in over + by_x + by_y + [final]:
            made.wait_send()

    def targets(self):
        return self.along_targets() + self.peer_targets()

    def along_targets(self):
        return [(self.dp, (self.tensor + s) % self.shards) for s in range(1, self.shards)]

    def peer_targets(self):
        return [(flip(self.dp, bit), self.tensor) for bit in (2, 4, 1)]


def eighth(ref, offset=0):
    rows = ref.shape[1] // PEERS

    def at(shard, peer, half):
        first = peer * rows + (0 if half is None else half * (rows // 2))
        return ref.at[shard, pl.ds(pl.multiple_of(first, 16), rows if half is None else rows // 2)]

    return at


def reduce_chain(part, out, buf_in, buf_mid, sems, steps):
    send_pair, send_mid, send_out, recv_pair, recv_mid, recv_out = sems
    dp, tensor = lax.axis_index("dp"), lax.axis_index("tensor")
    side = tensor // 2
    other = 1 - side
    pair = (dp, tensor + 1 - 2 * (tensor % 2))
    across = (dp, 3 - tensor)
    middle = (tensor + side) % 2 == 1

    def to_pair(half, c):
        return remote(part.at[half, c], buf_in.at[half, c], send_pair.at[half, c], recv_pair.at[half, c], pair)

    def to_mid(c):
        return remote(buf_mid.at[0, c], buf_mid.at[1, c], send_mid.at[c], recv_mid.at[c], across)

    def final_across(half, c):
        return remote(out.at[half, c], out.at[half, c], send_out.at[0, c], recv_out.at[half, c], across)

    def final_pair(half, c):
        return remote(out.at[half, c], out.at[half, c], send_out.at[1 + (0 if half is side else 1), c], recv_out.at[half, c], pair)

    def wide(ref, *at):
        return ref[at].astype(WIDE)

    def begin(more=()):
        @pl.when(middle)
        def _():
            greet([pair, across, *more])

        @pl.when(jnp.logical_not(middle))
        def _():
            greet([pair, *more])
            for c in range(steps):
                to_pair(other, c).start()
                to_pair(side, c).start()

    def first(c):
        to_pair(other, c).wait_recv()
        buf_mid[0, c] = (wide(buf_in, other, c) + wide(part, other, c)).astype(buf_mid.dtype)
        to_mid(c).start()

    def second(c):
        to_pair(side, c).wait_recv()
        to_mid(c).wait_recv()
        out[side, c] = (wide(buf_in, side, c) + wide(buf_mid, 1, c) + wide(part, side, c)).astype(out.dtype)
        final_across(side, c).start()
        final_pair(side, c).start()

    def third(c):
        final_across(other, c).wait_recv()
        final_pair(other, c).start()

    def step(t):
        @pl.when(middle)
        def _():
            if t < steps:
                first(t)
            if 0 <= t - 1 < steps:
                second(t - 1)
            if 0 <= t - 2 < steps:
                third(t - 2)

    def end():
        @pl.when(middle)
        def _():
            for c in range(steps):
                to_mid(c).wait_send()
                final_across(side, c).wait_send()
                final_pair(side, c).wait_send()
                final_pair(other, c).wait_send()

        @pl.when(jnp.logical_not(middle))
        def _():
            for c in range(steps):
                to_pair(other, c).wait_send()
                to_pair(side, c).wait_send()
                final_pair(other, c).wait_recv()
                final_pair(side, c).wait_recv()

    return [begin] + [functools.partial(step, t) for t in range(steps + 2)] + [end]


def chain_scratch(steps, rows, width):
    dma = pltpu.SemaphoreType.DMA
    return [
        pltpu.VMEM((2, steps, rows, width), NARROW),
        pltpu.VMEM((2, steps, rows, width), NARROW),
        dma((2, steps)), dma((steps,)), dma((3, steps)),
        dma((2, steps)), dma((steps,)), dma((2, steps)),
    ]


def sum_shards_kernel(part, out, buf_in, buf_mid, *sems):
    for run in reduce_chain(part, out, buf_in, buf_mid, sems, part.shape[1]):
        run()


def sum_shards(part, ident):
    rows, width = part.shape
    steps = 8
    shape = (2, steps, rows // (2 * steps), width)
    vmem = pl.BlockSpec(memory_space=pltpu.VMEM)
    return pl.pallas_call(
        sum_shards_kernel,
        in_specs=[vmem],
        out_specs=vmem,
        out_shape=jax.ShapeDtypeStruct(shape, NARROW),
        scratch_shapes=chain_scratch(steps, shape[2], width),
        compiler_params=pltpu.CompilerParams(
            collective_id=ident, has_side_effects=True, vmem_limit_bytes=VMEM_BYTES
        ),
        name="sum_shards",
    )(part.reshape(shape)).reshape(rows, width)


PIECES = 8


class PeerSum:
    def __init__(self, parts, source, work, total, land, higher, send, recv, base=0):
        self.parts, self.source, self.work, self.land, self.higher = parts, source, work, land, higher
        self.total = total
        self.send, self.recv, self.base = send, recv, base
        self.dp, self.tensor = lax.axis_index("dp"), lax.axis_index("tensor")
        self.bits = [(self.dp // b) % 2 for b in (1, 2, 4)]

    @staticmethod
    def far_bits():
        return [PEERS << k for k in range((lax.axis_size("dp") // PEERS - 1).bit_length())]

    @staticmethod
    def copies(parts, far):
        return len(parts) * (6 + far)

    def way(self, part):
        order = ((2, self.bits[1]), (4, self.bits[2]))
        return order if part[5] == 0 else order[::-1]

    def rows(self, refs, part, piece, count):
        array, first, size, column, columns, _ = part
        start = pl.multiple_of(first + piece * size, 16)
        return refs[array].at[pl.ds(start, count * size), pl.ds(column, columns)]

    def hop(self, n, stage, src, dst, bit):
        index = self.base + n * (6 + len(self.far_bits())) + stage
        return remote(src, dst, self.send.at[index], self.recv.at[index], (flip(self.dp, bit), self.tensor))

    def halving(self, n, stage):
        part = self.parts[n]
        core = self.bits[0]
        if stage == 0:
            away, kept, count, bit = (1 - core) * 4, core * 4, 4, 1
        else:
            (bit_1, own_1), (bit_2, own_2) = self.way(part)
            if stage == 1:
                away, kept, count, bit = core * 4 + (1 - own_1) * 2, core * 4 + own_1 * 2, 2, bit_1
            else:
                at = core * 4 + own_1 * 2
                away, kept, count, bit = at + 1 - own_2, at + own_2, 1, bit_2
        landed = self.land[n].at[pl.ds((0, 4, 6)[stage] * part[2], count * part[2])]
        out = self.rows(self.source if stage == 0 else self.work, part, away, count)
        return self.hop(n, stage, out, landed, bit), kept, count, landed

    def final_piece(self, part):
        (_, own_1), (_, own_2) = self.way(part)
        return self.bits[0] * 4 + own_1 * 2 + own_2

    def gathering(self, n, stage):
        part = self.parts[n]
        core = self.bits[0]
        (bit_1, own_1), (bit_2, _) = self.way(part)
        piece, count, bit = (
            (self.final_piece(part), 1, bit_2), (core * 4 + own_1 * 2, 2, bit_1), (core * 4, 4, 1),
        )[stage]
        place = self.rows(self.total, part, piece, count)
        return self.hop(n, 3 + stage, place, place, bit)

    def targets(self):
        return [(flip(self.dp, bit), self.tensor) for bit in [1, 2, 4] + self.far_bits()]

    def start_halving(self, stage):
        for n in range(len(self.parts)):
            self.halving(n, stage)[0].start()

    def end_halving(self, stage):
        for n, part in enumerate(self.parts):
            made, kept, count, landed = self.halving(n, stage)
            made.wait_recv()
            source = self.rows(self.source if stage == 0 else self.work, part, kept, count)
            place = self.rows(self.total if stage == 2 else self.work, part, kept, count)
            place[...] = (source[...].astype(WIDE) + landed[...].astype(WIDE)).astype(place.dtype)
        for n in range(len(self.parts)):
            self.halving(n, stage)[0].wait_send()

    def far(self):
        for k, bit in enumerate(self.far_bits()):
            for n, part in enumerate(self.parts):
                place = self.rows(self.total, part, self.final_piece(part), 1)
                made = self.hop(n, 6 + k, place, self.higher[n].at[k], bit)
                made.start()
                made.wait()
                place[...] = (place[...].astype(WIDE) + self.higher[n][k].astype(WIDE)).astype(place.dtype)

    def start_gathering(self, stage):
        for n in range(len(self.parts)):
            self.gathering(n, stage).start()

    def end_gathering(self, stage):
        for n in range(len(self.parts)):
            self.gathering(n, stage).wait()


def peer_scratch(parts, shapes, far):
    dma = pltpu.SemaphoreType.DMA
    count = PeerSum.copies(parts, far)
    land = [pltpu.VMEM((7 * p[2], p[4]), NARROW) for p in parts]
    higher = [pltpu.VMEM((max(far, 1), p[2], p[4]), NARROW) for p in parts]
    return [pltpu.VMEM(shape, NARROW) for shape in shapes * 2] + land + higher + [dma((count,)), dma((count,))]


def sum_rows(values, out, land, send, recv):
    dp, tensor = lax.axis_index("dp"), lax.axis_index("tensor")
    bits = [1, 2, 4] + PeerSum.far_bits()
    for k, bit in enumerate(bits):
        source = values if k == 0 else out.at[k - 1]
        made = remote(source, land.at[k], send.at[k], recv.at[k], (flip(dp, bit), tensor))
        made.start()
        made.wait()
        out[k] = source[...] + land[k]


def last_sums_kernel(parts, kv_ref, cross_ref, self_ref, rows_ref, kv_out, cq_out, co_out, qkv_out, so_out, rows_out, *rest):
    work, total, rest = rest[:3], rest[3:6], rest[6:]
    land, rest = rest[: len(parts)], rest[len(parts) :]
    higher, rest = rest[: len(parts)], rest[len(parts) :]
    send, recv, few, few_land, few_send, few_recv = rest
    peers = PeerSum(parts, (kv_ref, cross_ref, self_ref), work, total, land, higher, send, recv)
    greet(peers.targets())
    for stage in range(3):
        peers.start_halving(stage)
        peers.end_halving(stage)
    peers.far()
    for stage in range(3):
        peers.start_gathering(stage)
        if stage == 0:
            sum_rows(rows_ref, few, few_land, few_send, few_recv)
            rows_out[...] = few[few.shape[0] - 1]
        peers.end_gathering(stage)
    kv, cross, own = total
    cols = co_out.shape[0]
    kv_out[0] = kv[:cols].astype(WIDE)
    kv_out[1, 128:] = kv[cols : 2 * cols - 128].astype(WIDE)
    kv_out[1, :128] = kv[2 * cols - 128 :].astype(WIDE)
    cq_out[...] = cross[:cols].astype(WIDE)
    co_out[...] = cross[cols:].astype(WIDE)
    for c in range(3):
        qkv_out[c] = own[c * cols : (c + 1) * cols].astype(WIDE)
    so_out[...] = own[3 * cols :].astype(WIDE)


def last_sums(kv, cross, own, rows, peers):
    cols = cross.shape[0] // 2
    width, depth = cross.shape[1], kv.shape[1]
    third = own.shape[0] // 3
    parts = (
        (0, 0, kv.shape[0] // PIECES, 0, width, 0),
        (0, 0, kv.shape[0] // PIECES, width, depth - width, 1),
        (1, 0, cross.shape[0] // PIECES, 0, width, 0),
        (2, 0, third // PIECES, 0, width, 0),
        (2, third, 2 * third // PIECES, 0, width, 1),
    )
    far = (peers // PEERS - 1).bit_length()
    vmem = pl.BlockSpec(memory_space=pltpu.VMEM)
    steps = 3 + far
    dma = pltpu.SemaphoreType.DMA

    def wide(*shape):
        return jax.ShapeDtypeStruct(shape, WIDE)

    return pl.pallas_call(
        functools.partial(last_sums_kernel, parts),
        in_specs=[vmem] * 4,
        out_specs=[vmem] * 6,
        out_shape=[
            wide(2, cols, depth), wide(cols, width), wide(cols, width),
            wide(3, cols, width), wide(cols, width), wide(*rows.shape),
        ],
        scratch_shapes=peer_scratch(parts, [kv.shape, cross.shape, own.shape], far)
        + [pltpu.VMEM((steps,) + rows.shape, WIDE)] * 2
        + [dma((steps,)), dma((steps,))],
        compiler_params=pltpu.CompilerParams(
            collective_id=4, has_side_effects=True, vmem_limit_bytes=VMEM_BYTES
        ),
        name="last_sums",
    )(kv, cross, own, rows)


def start_kernel(x_ref, tail_ref, wkv_ref, own_ref, k_ref, v_ref, attn_ref, w_ref, y_ref, send, recv, local):
    step = pl.program_id(0)
    last = pl.num_programs(0) - 1
    block, items, depth = x_ref.shape
    cols = own_ref.shape[1]
    kinds = own_ref.shape[0]
    rows = kinds * cols // PEERS

    def at(shard, peer, half):
        per = cols // rows
        first = shard * cols + (peer % per) * rows + (0 if half is None else half * (rows // 2))
        return attn_ref.at[peer // per, pl.ds(pl.multiple_of(first, 16), rows if half is None else rows // 2)]

    spread = Spread(at, send, recv, 0)
    per = cols // rows
    mine = own_ref.at[spread.peer // per, pl.ds(pl.multiple_of((spread.peer % per) * rows, 16), rows)]
    steps = range(1, spread.shards)
    here = pl.ds(pl.multiple_of(spread.tensor * cols, 16), cols)
    own_copies = [
        pltpu.make_async_copy(own_ref.at[c], attn_ref.at[c, here], local.at[c]) for c in range(kinds)
    ]

    @pl.when(step == 0)
    def _():
        greet(spread.targets())
        for s in steps:
            spread.along(s, mine).start()
        for made in own_copies:
            made.start()

    @pl.when(step == 0)
    def _():
        low = 128
        w_ref[:cols] = wkv_ref[0]
        w_ref[cols : 2 * cols - low] = wkv_ref[1, low:]
        w_ref[2 * cols - low :] = wkv_ref[1, :low]

    def project(x, first, count):
        y = mm_nt(x, w_ref[...])
        for tile in range(y_ref.shape[0]):
            y_ref[tile, : count * items] = y[:, tile * 128 : (tile + 1) * 128]
        for item in range(items):
            k_low, high, v_low = [
                y_ref[tile, pl.ds(item, count, stride=items)].astype(NARROW) for tile in range(3)
            ]
            k_ref[item, first, :128] = k_low
            k_ref[item, first, 128:] = high[:, : cols - 128]
            v_ref[item, first, :128] = v_low
            v_ref[item, first, 128:] = high[:, cols - 128 :]

    project(
        x_ref[...].reshape(block * items, depth),
        pl.ds(pl.multiple_of(step * block, block), block),
        block,
    )

    @pl.when(step == last)
    def _():
        count = tail_ref.shape[0]
        project(
            tail_ref[...].reshape(count * items, depth),
            pl.ds(k_ref.shape[1] - count, count),
            count,
        )
        for s in steps:
            spread.along(s, mine).wait_recv()
            spread.start_across(s)
        for s in steps:
            spread.start_onward(s)
        for s in steps:
            spread.start_last(s)
        for s in steps:
            spread.finish(s)
            spread.along(s, mine).wait_send()
        for made in own_copies:
            made.wait()


def start_layer(visual, wkv, own, shards):
    span, items, depth = visual.shape
    kinds, cols, width = own.shape
    steps = 4
    tail = span % (16 * steps)
    block = (span - tail) // steps
    out = pl.BlockSpec((items, span, cols), lambda i: (0, 0, 0))
    shape = jax.ShapeDtypeStruct((items, span, cols), NARROW)
    copies = Spread.COPIES * (shards - 1)
    dma = pltpu.SemaphoreType.DMA
    return pl.pallas_call(
        start_kernel,
        grid=(steps,),
        in_specs=[
            pl.BlockSpec((block, items, depth), lambda i: (i, 0, 0)),
            pl.BlockSpec((tail, items, depth), lambda i: (span // tail - 1, 0, 0)),
            pl.BlockSpec(wkv.shape, lambda i: (0, 0, 0)),
            pl.BlockSpec(own.shape, lambda i: (0, 0, 0)),
        ],
        out_specs=[out, out, pl.BlockSpec(memory_space=pl.ANY)],
        out_shape=[shape, shape, jax.ShapeDtypeStruct((kinds, shards * cols, width), NARROW)],
        scratch_shapes=[
            pltpu.VMEM((2 * cols, depth), NARROW),
            pltpu.VMEM((2 * cols // 128, block * items, 128), WIDE),
            dma((copies,)), dma((copies,)), dma((kinds,)),
        ],
        compiler_params=pltpu.CompilerParams(
            collective_id=0, has_side_effects=True, vmem_limit_bytes=VMEM_BYTES
        ),
        name="start_layer",
    )(visual, visual, wkv, own)


def feed_copies(shards):
    return 2 * Spread.COPIES * (shards - 1)


def sum_and_spread_kernel(part, in_ref, out_ref, out, win_ref, wout_ref, buf_in, buf_mid, *rest):
    sems, (send, recv) = rest[:6], rest[6:]
    del in_ref, out_ref
    chain = reduce_chain(part, out, buf_in, buf_mid, sems, part.shape[1])
    shards = lax.axis_size("tensor")
    base = Spread.COPIES * (shards - 1)
    spreads = [
        (Spread(eighth(ref), send, recv, n * base), s)
        for s in range(1, shards)
        for n, ref in enumerate((win_ref, wout_ref))
    ]
    chain[0](spreads[0][0].peer_targets())
    for spread, s in spreads:
        spread.start_across(s)
    todo = list(spreads)
    for t, run in enumerate(chain[1:-1]):
        run()
        if t >= 2 and t % 3 != 1 and todo:
            spread, s = todo.pop(0)
            spread.start_onward(s)
    for spread, s in todo:
        spread.start_onward(s)
    chain[-1]()
    for spread, s in spreads:
        spread.start_last(s)
    for spread, s in spreads:
        spread.finish(s)


def sum_and_spread(part, win, wout, ident):
    rows, width = part.shape
    steps = 8
    shape = (2, steps, rows // (2 * steps), width)
    vmem = pl.BlockSpec(memory_space=pltpu.VMEM)
    hbm = pl.BlockSpec(memory_space=pl.ANY)
    copies = feed_copies(win.shape[0])
    dma = pltpu.SemaphoreType.DMA
    total, win, wout = pl.pallas_call(
        sum_and_spread_kernel,
        in_specs=[vmem, hbm, hbm],
        out_specs=[vmem, hbm, hbm],
        out_shape=[
            jax.ShapeDtypeStruct(shape, NARROW),
            jax.ShapeDtypeStruct(win.shape, NARROW),
            jax.ShapeDtypeStruct(wout.shape, NARROW),
        ],
        input_output_aliases={1: 1, 2: 2},
        scratch_shapes=chain_scratch(steps, shape[2], width) + [dma((copies,)), dma((copies,))],
        compiler_params=pltpu.CompilerParams(
            collective_id=ident, has_side_effects=True, vmem_limit_bytes=VMEM_BYTES
        ),
        name="sum_and_spread",
    )(part.reshape(shape), win, wout)
    return total.reshape(rows, width), win, wout


def labels_of(position, ends):
    place = position - NQ
    label = jnp.zeros_like(position)
    for end in ends:
        label = label + jnp.where(place >= end, 1, 0)
    return jnp.where(position < NQ, -1, label)


def allowed_pairs(lens_ref, item, span, lanes):
    ends = []
    total = jnp.int32(0)
    for c in range(lens_ref.shape[1]):
        total = total + lens_ref[item, c]
        ends.append(total)
    key_label = labels_of(lax.broadcasted_iota(jnp.int32, (span, lanes), 0), ends)
    query_label = labels_of(lax.broadcasted_iota(jnp.int32, (span, lanes), 1) % span, ends)
    return (key_label == query_label) | (key_label == -1)


def self_forward_kernel(
    lens_ref, x_ref, w_ref, gain_ref, shift_ref, in_ref, out_ref,
    q_ref, k_ref, v_ref, p_ref, ctx_ref, res_ref, fq_ref, ft_ref, win_ref, wout_ref,
    bounce, send, recv, local,
):
    step = pl.program_id(0)
    tensor = lax.axis_index("tensor")
    shards = lax.axis_size("tensor")
    hops, load = [], []
    for n, (own, gathered) in enumerate(((in_ref, win_ref), (out_ref, wout_ref))):
        spread = Spread(eighth(gathered), send, recv, n * Spread.COPIES * (shards - 1))
        rows = own.shape[1] // PEERS
        mine = own.at[0, pl.ds(pl.multiple_of(spread.peer * rows, 16), rows)]
        hops += [spread.along(s, mine) for s in range(1, shards)]
        load.append(pltpu.make_async_copy(own.at[0], bounce.at[n], local.at[n]))
        hops.append(pltpu.make_async_copy(bounce.at[n], gathered.at[tensor], local.at[n]))

    @pl.when(step == 0)
    def _():
        for made in load:
            made.start()
        greet(spread.along_targets())
        for made in hops[: shards - 1] + hops[shards : 2 * shards - 1]:
            made.start()
        for made in load:
            made.wait()
        for made in (hops[shards - 1], hops[2 * shards - 1]):
            made.start()

    span = NQ + TXT
    items = x_ref.shape[0] // span
    lanes = QUAD * HEAD
    x = x_ref[...]
    q_ref[...] = (mm_nt(x, w_ref[0]) .astype(NARROW).astype(WIDE) * SCALE).astype(NARROW)
    k_ref[...] = mm_nt(x, w_ref[1]).astype(NARROW)
    v_ref[...] = mm_nt(x, w_ref[2]).astype(NARROW)

    @pl.loop(0, items)
    def _(item):
        rows = pl.ds(pl.multiple_of(item * span, span), span)
        allowed = allowed_pairs(lens_ref, pl.program_id(0) * items + item, span, lanes)
        for quad in range(x_ref.shape[1] // lanes):
            cols = slice(quad * lanes, (quad + 1) * lanes)
            scores = mm_nt(k_ref[rows, cols], spread_heads(q_ref[rows, cols], QUAD))
            scores = jnp.where(allowed, scores, MASKED_SCORE)
            lifted = jnp.exp(scores - jnp.max(scores, axis=0, keepdims=True))
            chances = lifted * (1.0 / jnp.sum(lifted, axis=0, keepdims=True))
            low = chances.astype(NARROW)
            p_ref[rows, cols] = low
            ctx_ref[rows, cols] = gather_heads(mm_tn(low, v_ref[rows, cols]), QUAD).astype(NARROW)

    residue = x.astype(WIDE) + mm(ctx_ref[...], w_ref[3])
    res_ref[...] = residue
    unit, _ = norm_parts(residue)
    first = unit * gain_ref[0:1] + shift_ref[0:1]
    for item in range(items):
        fq_ref[item * NQ : (item + 1) * NQ] = first[item * span : item * span + NQ]
        ft_ref[item * TXT : (item + 1) * TXT] = first[item * span + NQ : (item + 1) * span]

    @pl.when(step == pl.num_programs(0) - 1)
    def _():
        for made in hops:
            made.wait()


def self_forward(hidden, lens, weights, gain, shift, ffn_in, ffn_out, shards):
    rows, width = hidden.shape
    block = min(rows, 256)
    half = block // 2
    full = pl.BlockSpec((block, width), lambda i: (i, 0))
    halves = pl.BlockSpec((half, width), lambda i: (i, 0))
    low = jax.ShapeDtypeStruct((rows, width), NARROW)
    hbm = pl.BlockSpec(memory_space=pl.ANY)
    dma = pltpu.SemaphoreType.DMA
    return pl.pallas_call(
        self_forward_kernel,
        grid=(rows // block,),
        in_specs=[
            pl.BlockSpec(memory_space=pltpu.SMEM),
            full,
            pl.BlockSpec(weights.shape, lambda i: (0, 0, 0)),
            pl.BlockSpec(gain.shape, lambda i: (0, 0)),
            pl.BlockSpec(shift.shape, lambda i: (0, 0)),
            hbm, hbm,
        ],
        out_specs=[full, full, full, full, full, full, halves, halves, hbm, hbm],
        out_shape=[
            low, low, low, low, low,
            jax.ShapeDtypeStruct((rows, width), WIDE),
            jax.ShapeDtypeStruct((rows // 2, width), WIDE),
            jax.ShapeDtypeStruct((rows // 2, width), WIDE),
            jax.ShapeDtypeStruct((shards,) + ffn_in.shape[1:], NARROW),
            jax.ShapeDtypeStruct((shards,) + ffn_out.shape[1:], NARROW),
        ],
        scratch_shapes=[
            pltpu.VMEM((2,) + ffn_in.shape[1:], NARROW),
            dma((feed_copies(shards),)), dma((feed_copies(shards),)), dma((2,)),
        ],
        compiler_params=pltpu.CompilerParams(
            collective_id=3, has_side_effects=True, vmem_limit_bytes=VMEM_BYTES
        ),
        name="self_forward",
    )(lens, hidden, weights, gain, shift, ffn_in, ffn_out)


def self_backward_kernel(
    own_ref, x_ref, w_ref, gain_ref, res_ref, gq_ref, gt_ref, q_ref, k_ref, v_ref, p_ref, ctx_ref,
    grad_ref, grads_ref, gain_out, shift_out,
    down, dctx, dq, dk, dv, acc,
):
    span = NQ + TXT
    block = res_ref.shape[0]
    items = block // span
    lanes = QUAD * HEAD
    step = pl.program_id(0)
    unit, inverse = norm_parts(res_ref[...])
    pieces = []
    for item in range(items):
        pieces.append(gq_ref[item * NQ : (item + 1) * NQ])
        pieces.append(gt_ref[item * TXT : (item + 1) * TXT])
    cotangent = jnp.concatenate(pieces, axis=0)
    grad_res = norm_back(unit, inverse, gain_ref[0:1], cotangent)
    gain_sum, shift_sum = column_sums(unit, cotangent)

    @pl.when(step == 0)
    def _():
        gain_out[...] = gain_sum
        shift_out[...] = shift_sum

    @pl.when(step > 0)
    def _():
        gain_out[...] += gain_sum
        shift_out[...] += shift_sum

    grad_ref[...] = grad_res
    low = grad_res.astype(NARROW)
    down[...] = low
    dctx[...] = mm_nt(low, w_ref[3]).astype(NARROW)

    @pl.loop(0, items)
    def _(item):
        rows = pl.ds(pl.multiple_of(item * span, span), span)
        for quad in range(w_ref.shape[2] // lanes):
            cols = slice(quad * lanes, (quad + 1) * lanes)
            chances = p_ref[rows, cols]
            spread = spread_heads(dctx[rows, cols], QUAD)
            grad_chances = mm_nt(v_ref[rows, cols], spread)
            weighted = chances.astype(WIDE)
            inner = jnp.sum(grad_chances * weighted, axis=0, keepdims=True)
            scores = (weighted * (grad_chances - inner)).astype(NARROW)
            dk[rows, cols] = mm(scores, spread_heads(q_ref[rows, cols], QUAD)).astype(NARROW)
            dv[rows, cols] = mm(chances, spread).astype(NARROW)
            dq[rows, cols] = (gather_heads(mm_tn(scores, k_ref[rows, cols]), QUAD) * SCALE).astype(
                NARROW
            )

    grad_ref[...] += mm(dq[...], w_ref[0]) + mm(dk[...], w_ref[1]) + mm(dv[...], w_ref[2])

    own = own_ref[0]
    cols = grads_ref.shape[0] // 4
    window = acc.shape[1]
    start = pl.multiple_of((own * cols) // 128 * 128, 128)
    here = pl.ds(start, window)
    x = x_ref[...]
    parts = (
        mm_tn(dq[:, here], x), mm_tn(dk[:, here], x), mm_tn(dv[:, here], x),
        mm_tn(ctx_ref[:, here], down[...]),
    )

    @pl.when(step == 0)
    def _():
        for c, part in enumerate(parts):
            acc[c] = part

    @pl.when(step > 0)
    def _():
        for c, part in enumerate(parts):
            acc[c] += part

    @pl.when(step == pl.num_programs(0) - 1)
    def _():
        offset = pl.multiple_of(own * cols - start, 64)
        for c in range(4):
            grads_ref[c * cols : (c + 1) * cols] = acc[c, pl.ds(offset, cols), :].astype(NARROW)


def self_backward(own, hidden, weights, gain, residue, grad_q, grad_t, q, k, v, p, ctx, cols):
    rows, width = hidden.shape
    block = min(rows, 256)
    half = block // 2
    full = pl.BlockSpec((block, width), lambda i: (i, 0))
    halves = pl.BlockSpec((half, width), lambda i: (i, 0))
    row = pl.BlockSpec((1, width), lambda i: (0, 0))
    return pl.pallas_call(
        self_backward_kernel,
        grid=(rows // block,),
        in_specs=[
            pl.BlockSpec(memory_space=pltpu.SMEM),
            full,
            pl.BlockSpec(weights.shape, lambda i: (0, 0, 0)),
            pl.BlockSpec(gain.shape, lambda i: (0, 0)),
            full, halves, halves, full, full, full, full, full,
        ],
        out_specs=[
            full,
            pl.BlockSpec((4 * cols, width), lambda i: (0, 0)),
            row, row,
        ],
        out_shape=[
            jax.ShapeDtypeStruct((rows, width), WIDE),
            jax.ShapeDtypeStruct((4 * cols, width), NARROW),
            jax.ShapeDtypeStruct((1, width), WIDE),
            jax.ShapeDtypeStruct((1, width), WIDE),
        ],
        scratch_shapes=[pltpu.VMEM((block, width), NARROW)] * 5
        + [pltpu.VMEM((4, (cols + 64 + 127) // 128 * 128, width), WIDE)],
        compiler_params=pltpu.CompilerParams(vmem_limit_bytes=VMEM_BYTES),
        name="self_backward",
    )(own, hidden, weights, gain, residue, grad_q, grad_t, q, k, v, p, ctx)


def cross_forward_kernel(x_ref, wq_ref, wo_ref, k_ref, v_ref, q_ref, p_ref, ctx_ref, part_ref):
    items = k_ref.shape[0]
    heads = q_ref.shape[1] // HEAD
    q_ref[...] = (
        mm_nt(x_ref[...].astype(NARROW), wq_ref[...]).astype(NARROW).astype(WIDE) * SCALE
    ).astype(NARROW)
    for item in range(items):
        rows = slice(item * NQ, (item + 1) * NQ)
        scores = mm_nt(k_ref[item], spread_heads(q_ref[rows], heads))
        lifted = jnp.exp(scores - jnp.max(scores, axis=0, keepdims=True))
        chances = (lifted * (1.0 / jnp.sum(lifted, axis=0, keepdims=True))).astype(NARROW)
        p_ref[item] = chances
        ctx_ref[rows] = gather_heads(mm_tn(chances, v_ref[item]), heads).astype(NARROW)
    part_ref[...] = mm(ctx_ref[...], wo_ref[...]).astype(NARROW)


def cross_forward(rows_q, wq, wo, k, v):
    rows, width = rows_q.shape
    items, span, cols = k.shape
    step = min(items, 4)
    heads = cols // HEAD
    block = step * NQ

    def by_rows(lanes):
        return pl.BlockSpec((block, lanes), lambda i: (i, 0))

    def by_items(lanes):
        return pl.BlockSpec((step, span, lanes), lambda i: (i, 0, 0))

    return pl.pallas_call(
        cross_forward_kernel,
        grid=(items // step,),
        in_specs=[
            by_rows(width),
            pl.BlockSpec(wq.shape, lambda i: (0, 0)),
            pl.BlockSpec(wo.shape, lambda i: (0, 0)),
            by_items(cols), by_items(cols),
        ],
        out_specs=[by_rows(cols), by_items(heads * NQ), by_rows(cols), by_rows(width)],
        out_shape=[
            jax.ShapeDtypeStruct((rows, cols), NARROW),
            jax.ShapeDtypeStruct((items, span, heads * NQ), NARROW),
            jax.ShapeDtypeStruct((rows, cols), NARROW),
            jax.ShapeDtypeStruct((rows, width), NARROW),
        ],
        compiler_params=pltpu.CompilerParams(vmem_limit_bytes=VMEM_BYTES),
        name="cross_forward",
    )(rows_q, wq, wo, k, v)


def cross_backward_kernel(
    down_ref, fq_ref, wq_ref, wo_ref, q_ref, k_ref, v_ref, p_ref, ctx_ref,
    part_ref, dkv_ref, grads_ref, dctx, dq, acc,
):
    items, span, cols = k_ref.shape
    all_items = items * pl.num_programs(0)
    heads = q_ref.shape[1] // HEAD
    step = pl.program_id(0)
    dctx[...] = mm_nt(down_ref[...], wo_ref[...]).astype(NARROW)
    for item in range(items):
        rows = slice(item * NQ, (item + 1) * NQ)
        chances = p_ref[item]
        spread = spread_heads(dctx[rows], heads)
        grad_chances = mm_nt(v_ref[item], spread)
        weighted = chances.astype(WIDE)
        inner = jnp.sum(grad_chances * weighted, axis=0, keepdims=True)
        scores = (weighted * (grad_chances - inner)).astype(NARROW)
        spread_q = spread_heads(q_ref[rows], heads)
        none = jnp.zeros((heads * NQ, cols), NARROW)
        both = mm(
            jnp.concatenate([scores, chances], axis=1),
            jnp.concatenate(
                [
                    jnp.concatenate([spread_q, none], axis=1),
                    jnp.concatenate([none, spread[:, 128:], spread[:, :128]], axis=1),
                ],
                axis=0,
            ),
        )
        for tile in range(dkv_ref.shape[0]):
            dkv_ref[tile, pl.ds(step * items + item, span, stride=all_items)] = both[
                :, tile * 128 : (tile + 1) * 128
            ]
        dq[rows] = (gather_heads(mm_tn(scores, k_ref[item]), heads) * SCALE).astype(NARROW)
    part_ref[...] = mm(dq[...], wq_ref[...]).astype(NARROW)
    grad_q = mm_tn(dq[...], fq_ref[...].astype(NARROW))
    grad_o = mm_tn(ctx_ref[...], down_ref[...])

    @pl.when(step == 0)
    def _():
        acc[0] = grad_q
        acc[1] = grad_o

    @pl.when(step > 0)
    def _():
        acc[0] += grad_q
        acc[1] += grad_o

    @pl.when(step == pl.num_programs(0) - 1)
    def _():
        grads_ref[:cols] = acc[0].astype(grads_ref.dtype)
        grads_ref[cols:] = acc[1].astype(grads_ref.dtype)


def cross_backward(down, rows_q, wq, wo, q, k, v, p, ctx):
    rows, width = down.shape
    items, span, cols = k.shape
    step = min(items, 4)
    heads = cols // HEAD
    block = step * NQ

    def by_rows(lanes):
        return pl.BlockSpec((block, lanes), lambda i: (i, 0))

    def by_items(lanes):
        return pl.BlockSpec((step, span, lanes), lambda i: (i, 0, 0))

    whole = pl.BlockSpec(wq.shape, lambda i: (0, 0))
    tiles = (2 * cols // 128, items * span, 128)
    keyed = pl.BlockSpec(tiles, lambda i: (0, 0, 0))
    wide = jax.ShapeDtypeStruct(tiles, WIDE)
    return pl.pallas_call(
        cross_backward_kernel,
        grid=(items // step,),
        in_specs=[
            by_rows(width), by_rows(width), whole, whole,
            by_rows(cols), by_items(cols), by_items(cols), by_items(heads * NQ), by_rows(cols),
        ],
        out_specs=[by_rows(width), keyed, pl.BlockSpec((2 * cols, width), lambda i: (0, 0))],
        out_shape=[
            jax.ShapeDtypeStruct((rows, width), NARROW),
            wide,
            jax.ShapeDtypeStruct((2 * cols, width), NARROW),
        ],
        scratch_shapes=[
            pltpu.VMEM((block, cols), NARROW),
            pltpu.VMEM((block, cols), NARROW),
            pltpu.VMEM((2, cols, width), WIDE),
        ],
        compiler_params=pltpu.CompilerParams(vmem_limit_bytes=VMEM_BYTES),
        name="cross_backward",
    )(down, rows_q, wq, wo, q, k, v, p, ctx)


def visual_backward_kernel(x_ref, tail_ref, d_ref, rest_ref, out_ref, acc):
    step = pl.program_id(0)
    block, items, depth = x_ref.shape

    def product(ref, x):
        grads = jnp.concatenate([ref[tile].astype(NARROW) for tile in range(ref.shape[0])], axis=1)
        return mm_tn(grads, x.reshape(-1, depth))

    part = product(d_ref, x_ref[...])

    @pl.when(step == 0)
    def _():
        acc[...] = part + product(rest_ref, tail_ref[...])

    @pl.when(step > 0)
    def _():
        acc[...] += part

    @pl.when(step == pl.num_programs(0) - 1)
    def _():
        out_ref[...] = acc[...].astype(out_ref.dtype)


def visual_backward(visual, grads):
    span, items, depth = visual.shape
    tiles = grads.shape[0]
    steps = 4
    tail = span % (16 * steps)
    block = (span - tail) // steps
    return pl.pallas_call(
        visual_backward_kernel,
        grid=(steps,),
        in_specs=[
            pl.BlockSpec((block, items, depth), lambda i: (i, 0, 0)),
            pl.BlockSpec((tail, items, depth), lambda i: (span // tail - 1, 0, 0)),
            pl.BlockSpec((tiles, block * items, 128), lambda i: (0, i, 0)),
            pl.BlockSpec((tiles, tail * items, 128), lambda i: (0, span // tail - 1, 0)),
        ],
        out_specs=pl.BlockSpec((tiles * 128, depth), lambda i: (0, 0)),
        out_shape=jax.ShapeDtypeStruct((tiles * 128, depth), NARROW),
        scratch_shapes=[pltpu.VMEM((tiles * 128, depth), WIDE)],
        compiler_params=pltpu.CompilerParams(vmem_limit_bytes=VMEM_BYTES),
        name="visual_backward",
    )(visual, visual, grads, grads)


def feed_kernel(
    own_ref, fq_ref, cross_ref, win_ref, wout_ref, gain_ref, shift_ref, cot_ref,
    out_ref, grad_ref, down_ref, low_ref, top_ref, act_ref, dpre_ref, gain_out, shift_out,
    unit1, inverse1, second, slopes, total,
):
    step = pl.program_id(0)
    chunks = slopes.shape[0]
    width = slopes.shape[2]
    per = act_ref.shape[1] // width
    chunk = lax.rem(step, chunks)
    mine = chunk // per == own_ref[0]
    place = pl.ds(pl.multiple_of(lax.rem(chunk, per) * width, width), width)

    @pl.when(step == 0)
    def _():
        unit, inverse = norm_parts(fq_ref[...] + cross_ref[...].astype(WIDE))
        unit1[...] = unit
        inverse1[...] = inverse
        value = unit * gain_ref[1:2] + shift_ref[1:2]
        second[...] = value
        low_ref[...] = value.astype(NARROW)
        total[...] = jnp.zeros_like(total)

    @pl.when(step < chunks)
    def _():
        act, slope = gelu_parts(mm(low_ref[...], win_ref[0]))
        slopes[chunk] = slope
        act = act.astype(NARROW)
        total[...] += mm(act, wout_ref[0])

        @pl.when(mine)
        def _():
            act_ref[:, place] = act

    @pl.when(step == chunks)
    def _():
        unit, inverse = norm_parts(second[...] + total[...])
        out_ref[...] = (unit * gain_ref[2:3] + shift_ref[2:3]).astype(NARROW)
        cotangent = cot_ref[...].astype(WIDE)
        gain_sum, shift_sum = column_sums(unit, cotangent)
        gain_out[1:2] = gain_sum
        shift_out[1:2] = shift_sum
        grad = norm_back(unit, inverse, gain_ref[2:3], cotangent)
        total[...] = grad
        top_ref[...] = grad.astype(NARROW)

    @pl.when(step >= chunks)
    def _():
        dpre = (mm_nt(top_ref[...], wout_ref[0]) * slopes[chunk]).astype(NARROW)
        total[...] += mm_nt(dpre, win_ref[0])

        @pl.when(mine)
        def _():
            dpre_ref[:, place] = dpre

    @pl.when(step == 2 * chunks - 1)
    def _():
        grad_second = total[...]
        gain_sum, shift_sum = column_sums(unit1[...], grad_second)
        gain_out[0:1] = gain_sum
        shift_out[0:1] = shift_sum
        grad = norm_back(unit1[...], inverse1[...], gain_ref[1:2], grad_second)
        grad_ref[...] = grad
        down_ref[...] = grad.astype(NARROW)


def feed_forward_back(own, rows_q, cross, win, wout, gain, shift, cotangent):
    rows, width = rows_q.shape
    shards, _, hidden = win.shape
    tile = 256 if hidden % 256 == 0 else hidden
    per = hidden // tile
    chunks = shards * per
    whole = pl.BlockSpec((rows, width), lambda i: (0, 0))
    owned = pl.BlockSpec((rows, hidden), lambda i: (0, 0))
    pair = pl.BlockSpec((2, width), lambda i: (0, 0))
    low = jax.ShapeDtypeStruct((rows, width), NARROW)
    mine = jax.ShapeDtypeStruct((rows, hidden), NARROW)
    two = jax.ShapeDtypeStruct((2, width), WIDE)
    return pl.pallas_call(
        feed_kernel,
        grid=(2 * chunks,),
        in_specs=[
            pl.BlockSpec(memory_space=pltpu.SMEM),
            whole, whole,
            pl.BlockSpec((1, width, tile), lambda i: ((i % chunks) // per, 0, (i % chunks) % per)),
            pl.BlockSpec((1, tile, width), lambda i: ((i % chunks) // per, (i % chunks) % per, 0)),
            pl.BlockSpec(gain.shape, lambda i: (0, 0)),
            pl.BlockSpec(shift.shape, lambda i: (0, 0)),
            whole,
        ],
        out_specs=[whole, whole, whole, whole, whole, owned, owned, pair, pair],
        out_shape=[
            low, jax.ShapeDtypeStruct((rows, width), WIDE), low, low, low, mine, mine, two, two,
        ],
        scratch_shapes=[
            pltpu.VMEM((rows, width), WIDE),
            pltpu.VMEM((rows, 1), WIDE),
            pltpu.VMEM((rows, width), WIDE),
            pltpu.VMEM((chunks, rows, tile), WIDE),
            pltpu.VMEM((rows, width), WIDE),
        ],
        compiler_params=pltpu.CompilerParams(vmem_limit_bytes=VMEM_BYTES),
        name="feed_query",
    )(own, rows_q, cross, win, wout, gain, shift, cotangent)


def sum_items(values):
    return lax.psum([v.astype(NARROW) for v in values], "dp")


def on_device(
    hidden_in,
    visual_feats,
    caption_lengths,
    self_qkv,
    self_out,
    cross_query,
    cross_kv,
    cross_out,
    ffn_in,
    ffn_out,
    norm_gain,
    norm_shift,
    out_grad,
):
    items = visual_feats.shape[0]
    rows, width = hidden_in.shape
    span = rows // items
    cols = self_qkv.shape[2]
    hidden = ffn_in.shape[2]
    own = lax.axis_index("tensor").reshape((1,)).astype(jnp.int32)
    shards = lax.axis_size("tensor")

    visual = jnp.swapaxes(visual_feats, 0, 1)
    cross_wq = jnp.swapaxes(cross_query, 0, 1)
    attn_own = jnp.concatenate([jnp.swapaxes(self_qkv, 1, 2), self_out[None]], axis=0)
    cross_k, cross_v, attn = start_layer(visual, jnp.swapaxes(cross_kv, 1, 2), attn_own, shards)
    q, k, v, p, ctx, residue, first_q, first_t, win_q, wout_q = self_forward(
        hidden_in, caption_lengths, attn, norm_gain, norm_shift, ffn_in, ffn_out, shards
    )
    cq, cp, cctx, cross_part = cross_forward(first_q, cross_wq, cross_out, cross_k, cross_v)
    cross_sum, win_q, wout_q = sum_and_spread(cross_part, win_q, wout_q, 1)

    cot = out_grad.reshape(items, span, width)
    cot_q = cot[:, :NQ].reshape(items * NQ, width)
    cot_t = cot[:, NQ:].reshape(items * TXT, width)

    low_t = first_t.astype(NARROW)
    act_t, slope_t = gelu_parts(jnp.dot(low_t, ffn_in[1], preferred_element_type=WIDE))
    act_t = act_t.astype(NARROW)
    ffn_t = lax.psum(mm(act_t, ffn_out[1]).astype(NARROW), "tensor").astype(WIDE)
    unit, inverse = norm_parts(first_t + ffn_t)
    out_t = (unit * norm_gain[3:4] + norm_shift[3:4]).astype(NARROW)
    cot_t = cot_t.astype(WIDE)
    gain_t, shift_t = column_sums(unit, cot_t)
    grad_t = norm_back(unit, inverse, norm_gain[3:4], cot_t)
    top_t = grad_t.astype(NARROW)
    dpre_t = (mm_nt(top_t, ffn_out[1]) * slope_t).astype(NARROW)
    back_t = mm_nt(dpre_t, ffn_in[1]).astype(NARROW)
    back_t, cross_sum = lax.optimization_barrier((back_t, cross_sum))
    back_t = lax.psum(back_t, "tensor")

    out_q, grad_second, down_q, low_q, top_q, act_q, dpre_q, gain_pair, shift_pair = feed_forward_back(
        own, first_q, cross_sum, win_q, wout_q, norm_gain, norm_shift, cot_q
    )
    back_part, dkv, g_cross = cross_backward(
        down_q, first_q, cross_wq, cross_out, cq, cross_k, cross_v, cp, cctx
    )
    grad_q = grad_second + sum_shards(back_part, 2).astype(WIDE)
    g_in = jnp.stack([mm_tn(low_q, dpre_q), mm_tn(low_t, dpre_t)])
    g_out = jnp.stack([mm_tn(act_q, top_q), mm_tn(act_t, top_t)])
    g_in, g_out = sum_items([g_in, g_out])
    g_kv = visual_backward(visual, dkv)
    grad_t = grad_t + back_t.astype(WIDE)
    grad_hidden, g_self, gain_first, shift_first = self_backward(
        own, hidden_in, attn, norm_gain, residue, grad_q, grad_t, q, k, v, p, ctx, cols
    )
    out = jnp.concatenate(
        [out_q.reshape(items, NQ, width), out_t.reshape(items, TXT, width)], axis=1
    ).reshape(rows, width)
    gains = jnp.concatenate([gain_first, gain_pair, gain_t, shift_first, shift_pair, shift_t])
    g_kv, g_cq, g_co, g_qkv, g_so, gains = last_sums(g_kv, g_cross, g_self, gains, lax.axis_size("dp"))
    g_in, g_out = g_in.astype(WIDE), g_out.astype(WIDE)
    return (
        out,
        grad_hidden,
        jnp.swapaxes(g_qkv, 1, 2),
        g_so,
        jnp.swapaxes(g_cq, 0, 1),
        jnp.swapaxes(g_kv, 1, 2),
        g_co,
        g_in,
        g_out,
        gains[:4],
        gains[4:],
    )


def solution(mesh):
    placed = (
        P("dp", None),
        P("dp", None, None),
        P("dp", None),
        P(None, None, "tensor"),
        P("tensor", None),
        P(None, "tensor"),
        P(None, None, "tensor"),
        P("tensor", None),
        P(None, None, "tensor"),
        P(None, "tensor", None),
        P(),
        P(),
        P("dp", None),
    )
    return jax.shard_map(
        on_device,
        mesh=mesh,
        in_specs=placed,
        out_specs=(
            P("dp", None),
            P("dp", None),
            P(None, None, "tensor"),
            P("tensor", None),
            P(None, "tensor"),
            P(None, None, "tensor"),
            P("tensor", None),
            P(None, None, "tensor"),
            P(None, "tensor", None),
            P(),
            P(),
        ),
        check_vma=False,
    )
```

```python
import functools
import math
import types

import jax
import jax.numpy as jnp
from jax import lax
from jax.experimental import pallas as pl
from jax.experimental.pallas import tpu as pltpu
from jax.sharding import PartitionSpec as P

HEAD = 64
NQ = 32
TXT = 32
QUAD = 4
UNITS = 12
VISUAL_STEPS = 16
EPSILON = 1e-06
MASKED_SCORE = -1e30
SCALE = 1.0 / math.sqrt(HEAD)
WIDE = jnp.float32
NARROW = jnp.bfloat16
VMEM_BYTES = 60 * 2**20


def mm(a, b):
    return lax.dot_general(a, b, (((1,), (0,)), ((), ())), preferred_element_type=WIDE)


def mm_nt(a, b):
    return lax.dot_general(a, b, (((1,), (1,)), ((), ())), preferred_element_type=WIDE)


def mm_tn(a, b):
    return lax.dot_general(a, b, (((0,), (0,)), ((), ())), preferred_element_type=WIDE)


def lane_group(rows, lanes, size):
    return lax.broadcasted_iota(jnp.int32, (rows, lanes), 1) // size


def spread_heads(block, count):
    group = lane_group(1, block.shape[1], HEAD)
    return jnp.concatenate(
        [block * jnp.where(group == h, 1.0, 0.0).astype(NARROW) for h in range(QUAD)], axis=0
    )


def gather_heads(block, count):
    rows, lanes = block.shape[0] // QUAD, block.shape[1]
    group = lane_group(rows, lanes, HEAD)
    out = block[:rows]
    for h in range(1, count):
        out = jnp.where(group == h, block[h * rows : (h + 1) * rows], out)
    return out


def norm_parts(residue):
    mean = jnp.mean(residue, axis=-1, keepdims=True)
    centered = residue - mean
    variance = jnp.mean(centered * centered, axis=-1, keepdims=True)
    inverse = lax.rsqrt(variance + EPSILON)
    return centered * inverse, inverse


def norm_back(unit, inverse, gain_row, cotangent):
    scaled = gain_row * cotangent
    first = jnp.mean(scaled, axis=-1, keepdims=True)
    second = jnp.mean(scaled * unit, axis=-1, keepdims=True)
    return inverse * (scaled - first - unit * second)


def column_sums(unit, cotangent):
    return (
        jnp.sum(cotangent * unit, axis=0, keepdims=True),
        jnp.sum(cotangent, axis=0, keepdims=True),
    )


def gelu_parts(pre):
    bell = jnp.exp(-0.5 * pre * pre)
    half = 0.5 * lax.erf(pre * math.sqrt(0.5)) + 0.5
    return pre * half, half + pre * bell * (1.0 / math.sqrt(2.0 * math.pi))


MESH = pl.DeviceIdType.MESH
PEERS = 8


def flip(index, bit):
    return index + bit - 2 * bit * ((index // bit) % 2)


def greet(targets):
    barrier = pltpu.get_barrier_semaphore()
    for target in targets:
        pl.semaphore_signal(barrier, inc=1, device_id=target, device_id_type=MESH)
    pl.semaphore_wait(barrier, len(targets))


def remote(src, dst, send, recv, target):
    return pltpu.make_async_remote_copy(
        src_ref=src, dst_ref=dst, send_sem=send, recv_sem=recv, device_id=target, device_id_type=MESH
    )


class Spread:
    COPIES = 9

    def __init__(self, at, send, recv, base):
        self.at, self.send, self.recv, self.base = at, send, recv, base
        self.dp, self.tensor = lax.axis_index("dp"), lax.axis_index("tensor")
        self.shards = lax.axis_size("tensor")
        self.peer = self.dp % PEERS

    def hop(self, slot, s, src, dst, target):
        index = self.base + (s - 1) * self.COPIES + slot
        return remote(src, dst, self.send.at[index], self.recv.at[index], target)

    def came(self, s):
        return (self.tensor + self.shards - s) % self.shards

    def along(self, s, own):
        return self.hop(0, s, own, self.at(self.tensor, self.peer, None), (self.dp, (self.tensor + s) % self.shards))

    def hand(self, slot, s, bit, peer, half):
        place = self.at(self.came(s), peer, half)
        return self.hop(slot, s, place, place, (flip(self.dp, bit), self.tensor))

    def across(self, s):
        return [self.hand(1, s, 2, self.peer, None), self.hand(2, s, 4, self.peer, None), self.hand(3, s, 1, self.peer, None)]

    def onward(self, s):
        x, y = flip(self.peer, 2), flip(self.peer, 4)
        return (
            [self.hand(4, s, 4, x, 0), self.hand(5, s, 1, x, None)],
            [self.hand(6, s, 2, y, 1), self.hand(7, s, 1, y, None)],
        )

    def last(self, s):
        return self.hand(8, s, 1, flip(flip(self.peer, 2), 4), None)

    def start_across(self, s):
        for made in self.across(s):
            made.start()

    def wait_across(self, s):
        for made in self.across(s):
            made.wait()

    def start_onward(self, s, arrived=False):
        over_x, over_y, _ = self.across(s)
        by_x, by_y = self.onward(s)
        if not arrived:
            over_x.wait_recv()
        for made in by_x:
            made.start()
        if not arrived:
            over_y.wait_recv()
        for made in by_y:
            made.start()

    def start_last(self, s):
        by_x, by_y = self.onward(s)
        by_x[0].wait_recv()
        by_y[0].wait_recv()
        self.last(s).start()

    def finish(self, s, arrived=False):
        over = self.across(s)
        by_x, by_y = self.onward(s)
        final = self.last(s)
        for made in ([] if arrived else [over[2]]) + [by_x[1], by_y[1], final]:
            made.wait_recv()
        for made in ([] if arrived else over) + by_x + by_y + [final]:
            made.wait_send()

    def targets(self):
        return self.along_targets() + self.peer_targets()

    def along_targets(self):
        return [(self.dp, (self.tensor + s) % self.shards) for s in range(1, self.shards)]

    def peer_targets(self):
        return [(flip(self.dp, bit), self.tensor) for bit in (2, 4, 1)]


FAR = 2


def one_shard(ref):
    rows = ref.shape[0] // PEERS

    def at(shard, peer, half):
        return ref.at[half_rows(peer * rows, rows, half)]

    return at


def half_rows(first, rows, half):
    split = (rows // 2 + 15) // 16 * 16
    start, count = {None: (0, rows), 0: (0, split), 1: (split, rows - split)}[half]
    return pl.ds(pl.multiple_of(first + start, 16), count)


def eighth(ref):
    rows = ref.shape[1] // PEERS

    def at(shard, peer, half):
        return ref.at[shard, half_rows(peer * rows, rows, half)]

    return at


class HeadGather:
    def __init__(self, buffer, send, recv):
        self.buffer, self.send, self.recv = buffer, send, recv
        self.dp, self.tensor = lax.axis_index("dp"), lax.axis_index("tensor")
        self.shards = lax.axis_size("tensor")

    def copies(self, half):
        count = self.buffer.shape[1] // 2
        place = self.buffer.at[self.tensor, pl.ds(half * count, count)]
        return [
            remote(place, place, self.send.at[half, s], self.recv.at[half, s], (self.dp, (self.tensor + s) % self.shards))
            for s in range(1, self.shards)
        ]

    def start(self, half):
        for made in self.copies(half):
            made.start()

    def wait(self, half):
        for made in self.copies(half):
            made.wait()

    def product(self, weights):
        total = mm(self.buffer[0], weights[0])
        for shard in range(1, self.shards):
            total += mm(self.buffer[shard], weights[shard])
        return total


PIECES = 8


class PeerSum:
    def __init__(self, parts, source, total, land, higher, send, recv, base=0, pieces=None):
        self.parts, self.source, self.total, self.land, self.higher = parts, source, total, land, higher
        self.pieces = pieces
        self.send, self.recv, self.base = send, recv, base
        self.dp, self.tensor = lax.axis_index("dp"), lax.axis_index("tensor")
        self.bits = [(self.dp // b) % 2 for b in (1, 2, 4)]

    @staticmethod
    def far_bits():
        return [PEERS << k for k in range((lax.axis_size("dp") // PEERS - 1).bit_length())]

    @staticmethod
    def copies(parts, far):
        return len(parts) * (6 + far)

    def way(self, part):
        order = ((2, self.bits[1]), (4, self.bits[2]))
        return order if part[5] == 0 else order[::-1]

    def rows(self, refs, part, piece, count):
        array, first, size, column, columns, _ = part
        start = pl.multiple_of(first + piece * size, 16)
        return refs[array].at[pl.ds(start, count * size), pl.ds(column, columns)]

    def hop(self, n, stage, src, dst, bit):
        index = self.base + n * (6 + len(self.far_bits())) + stage
        return remote(src, dst, self.send.at[index], self.recv.at[index], (flip(self.dp, bit), self.tensor))

    def landed(self, n, piece, count):
        size = self.parts[n][2]
        return self.land[n].at[pl.ds(pl.multiple_of(piece * size, 16), count * size)]

    def halving(self, n, stage):
        part = self.parts[n]
        core = self.bits[0]
        (bit_1, own_1), (bit_2, own_2) = self.way(part)
        if stage == 0:
            bit, place = 1, self.landed(n, 0, 4)
            out = self.rows(self.source, part, (1 - core) * 4, 4)
            kept = self.rows(self.source, part, core * 4, 4)
        elif stage == 1:
            bit, place = bit_1, self.landed(n, 4, 2)
            out, kept = self.landed(n, (1 - own_1) * 2, 2), self.landed(n, own_1 * 2, 2)
        else:
            bit, place = bit_2, self.landed(n, 6, 1)
            out, kept = self.landed(n, 4 + 1 - own_2, 1), self.landed(n, 4 + own_2, 1)
        goal = self.final_place(n) if stage == 2 else place
        return self.hop(n, stage, out, place, bit), kept, place, goal

    def final_place(self, n):
        if self.pieces is not None:
            return self.pieces[n]
        return self.rows(self.total, self.parts[n], self.final_piece(self.parts[n]), 1)

    def final_piece(self, part):
        (_, own_1), (_, own_2) = self.way(part)
        return self.bits[0] * 4 + own_1 * 2 + own_2

    def gathering(self, n, stage):
        part = self.parts[n]
        core = self.bits[0]
        (bit_1, own_1), (bit_2, _) = self.way(part)
        piece, count, bit = (
            (self.final_piece(part), 1, bit_2), (core * 4 + own_1 * 2, 2, bit_1), (core * 4, 4, 1),
        )[stage]
        place = self.rows(self.total, part, piece, count)
        return self.hop(n, 3 + stage, place, place, bit)

    def targets(self):
        return [(flip(self.dp, bit), self.tensor) for bit in [1, 2, 4] + self.far_bits()]

    def start_halving(self, stage):
        for n in range(len(self.parts)):
            self.halving(n, stage)[0].start()

    def end_halving(self, stage):
        for n in range(len(self.parts)):
            made, kept, place, goal = self.halving(n, stage)
            made.wait_recv()
            goal[...] = (kept[...].astype(WIDE) + place[...].astype(WIDE)).astype(goal.dtype)
        for n in range(len(self.parts)):
            self.halving(n, stage)[0].wait_send()

    def far(self):
        for k, bit in enumerate(self.far_bits()):
            for n in range(len(self.parts)):
                place = self.final_place(n)
                made = self.hop(n, 6 + k, place, self.higher[n].at[k], bit)
                made.start()
                made.wait()
                place[...] = (place[...].astype(WIDE) + self.higher[n][k].astype(WIDE)).astype(place.dtype)

    def start_gathering(self, stage):
        for n in range(len(self.parts)):
            self.gathering(n, stage).start()

    def end_gathering(self, stage):
        for n in range(len(self.parts)):
            self.gathering(n, stage).wait()


def peer_scratch(parts, shapes, far):
    dma = pltpu.SemaphoreType.DMA
    count = PeerSum.copies(parts, far)
    land = [pltpu.VMEM((7 * p[2], p[4]), NARROW) for p in parts]
    higher = [pltpu.VMEM((far, p[2], p[4]) if far else (1, 16, 128), NARROW) for p in parts]
    return [pltpu.VMEM(shape, NARROW) for shape in shapes] + land + higher + [dma((count,)), dma((count,))]


def sum_rows(values, out, land, send, recv):
    dp, tensor = lax.axis_index("dp"), lax.axis_index("tensor")
    bits = [1, 2, 4] + PeerSum.far_bits()

    def hop(k):
        source = values if k == 0 else out.at[k - 1]
        return remote(source, land.at[k], send.at[k], recv.at[k], (flip(dp, bits[k]), tensor))

    def run(k):
        if k > 0:
            hop(k - 1).wait()
            out[k - 1] = (values if k == 1 else out.at[k - 2])[...] + land[k - 1]
        if k < len(bits):
            hop(k).start()

    return [functools.partial(run, k) for k in range(len(bits) + 1)]


def cross_parts(kv, cross):
    width = cross[1]
    return (
        (0, 0, kv[0] // PIECES, 0, width, 0),
        (0, 0, kv[0] // PIECES, width, kv[1] - width, 1),
        (1, 0, cross[0] // PIECES, 0, width, 0),
    )


def self_parts(own):
    third, width = own[0] // 3, own[1]
    return ((0, 0, third // PIECES, 0, width, 0), (0, third, 2 * third // PIECES, 0, width, 1))


def last_sums_kernel(
    own_ref, kv_low, kv_high, cross_piece, first_gain, first_shift, other_gain, other_shift, feed_ref,
    kv_out, cq_out, co_out, qkv_out, so_out, rows_out, feed_total, *rest,
):
    parts = self_parts(own_ref.shape)
    kv_total, cross_total, total = rest[:3]
    land, higher = rest[3:5], rest[5:7]
    send, recv, cross_send, cross_recv, few, few_land, few_send, few_recv, few_in, feed_send, feed_recv = rest[7:]
    del feed_ref
    feed = PeerSum(feed_parts(own_ref.shape[1]), (), (feed_total,), (), (), feed_send, feed_recv)
    late_parts = cross_parts(kv_total.shape, cross_total.shape)
    late = PeerSum(late_parts, (), (kv_total, cross_total), (), (), cross_send, cross_recv)
    peers = PeerSum(parts, (own_ref,), (total,), land, higher, send, recv)
    cols = co_out.shape[0]
    greet(peers.targets())
    peers.start_halving(0)
    feed.start_gathering(2)
    for piece, part in zip((kv_low, kv_high, cross_piece), late_parts):
        late.rows(late.total, part, late.final_piece(part), 1)[...] = piece[...]
    few_in[0:1] = first_gain[...]
    few_in[1:4] = other_gain[...]
    few_in[4:5] = first_shift[...]
    few_in[5:8] = other_shift[...]
    late.start_gathering(0)
    few_steps = sum_rows(few_in, few, few_land, few_send, few_recv)
    few_steps[0]()
    peers.end_halving(0)
    peers.start_halving(1)
    late.end_gathering(0)
    peers.end_halving(1)
    peers.start_halving(2)
    late.start_gathering(1)
    for run in few_steps[1:]:
        run()
    rows_out[...] = few[few.shape[0] - 1]
    peers.end_halving(2)
    peers.far()
    peers.start_gathering(0)
    late.end_gathering(1)
    late.start_gathering(2)
    peers.end_gathering(0)
    peers.start_gathering(1)
    late.end_gathering(2)
    kv_out[0] = kv_total[:cols].astype(WIDE)
    kv_out[1, 128:] = kv_total[cols : 2 * cols - 128].astype(WIDE)
    kv_out[1, :128] = kv_total[2 * cols - 128 :].astype(WIDE)
    cq_out[...] = cross_total[:cols].astype(WIDE)
    co_out[...] = cross_total[cols:].astype(WIDE)
    peers.end_gathering(1)
    peers.start_gathering(2)
    peers.end_gathering(2)
    feed.end_gathering(2)
    for c in range(3):
        qkv_out[c] = total[c * cols : (c + 1) * cols].astype(WIDE)
    so_out[...] = total[3 * cols :].astype(WIDE)


def last_sums(own, pieces, norms, feed, kv, cross, ident, peers):
    cols = own.shape[0] // 4
    width, depth = cross[1], kv[1]
    far = (peers // PEERS - 1).bit_length()
    vmem = pl.BlockSpec(memory_space=pltpu.VMEM)
    steps = 3 + far
    dma = pltpu.SemaphoreType.DMA
    count = PeerSum.copies(cross_parts(kv, cross), far)
    more = PeerSum.copies(feed_parts(width), far)
    hbm = pl.BlockSpec(memory_space=pl.ANY)
    rows = (8, width)

    def wide(*shape):
        return jax.ShapeDtypeStruct(shape, WIDE)

    return pl.pallas_call(
        last_sums_kernel,
        in_specs=[vmem] * (4 + len(norms)) + [hbm],
        out_specs=[vmem] * 6 + [hbm],
        out_shape=[
            wide(2, cols, depth), wide(cols, width), wide(cols, width),
            wide(3, cols, width), wide(cols, width), wide(*rows), jax.ShapeDtypeStruct(feed.shape, feed.dtype),
        ],
        input_output_aliases={4 + len(norms): 6},
        scratch_shapes=[pltpu.VMEM(kv, NARROW), pltpu.VMEM(cross, NARROW)]
        + peer_scratch(self_parts(own.shape), [own.shape], far)
        + [dma((count,)), dma((count,))]
        + [pltpu.VMEM((steps,) + rows, WIDE)] * 2
        + [dma((steps,)), dma((steps,)), pltpu.VMEM(rows, WIDE), dma((more,)), dma((more,))],
        compiler_params=pltpu.CompilerParams(
            collective_id=ident, has_side_effects=True, vmem_limit_bytes=VMEM_BYTES
        ),
        name="last_sums",
    )(own, *pieces, *norms, feed)


def start_kernel(
    x_ref, tail_ref, wkv_ref, qkv_ref, so_ref, cq_ref, co_ref, in_ref,
    k_ref, v_ref, attn_ref, win_ref, cross_ref, w_ref, y_ref, send, recv, local,
):
    step = pl.program_id(0)
    last = pl.num_programs(0) - 1
    block, items, depth = x_ref.shape
    cols = so_ref.shape[0]
    per = PEERS // 4
    rows = cols // per

    def at(shard, peer, half):
        return attn_ref.at[peer // per, half_rows(shard * cols + (peer % per) * rows, rows, half)]

    spread = Spread(at, send, recv, 0)
    peer, tensor = spread.peer, spread.tensor
    steps = range(1, spread.shards)
    base = Spread.COPIES * (spread.shards - 1)
    feed = Spread(eighth(win_ref), send, recv, base)
    cross = Spread(eighth(cross_ref), send, recv, 2 * base)
    few = 2 * cols // PEERS

    def eighth_of(ref, first, count):
        return ref.at[pl.ds(pl.multiple_of(first, 16), count)]

    def start_self(s):
        @pl.when(peer < 3 * per)
        def _():
            spread.along(s, eighth_of(qkv_ref.at[peer // per], (peer % per) * rows, rows)).start()

        @pl.when(peer >= 3 * per)
        def _():
            spread.along(s, eighth_of(so_ref, (peer - 3 * per) * rows, rows)).start()

    def start_cross(s):
        @pl.when(peer < PEERS // 2)
        def _():
            cross.along(s, eighth_of(cq_ref, peer * few, few)).start()

        @pl.when(peer >= PEERS // 2)
        def _():
            cross.along(s, eighth_of(co_ref, (peer - PEERS // 2) * few, few)).start()

    self_any, cross_any = so_ref.at[pl.ds(0, rows)], co_ref.at[pl.ds(0, few)]
    feed_mine = eighth(in_ref)(0, peer, None)
    here = pl.ds(pl.multiple_of(tensor * cols, 16), cols)
    own_copies = [
        pltpu.make_async_copy(source, goal, local.at[n])
        for n, (source, goal) in enumerate(
            [(qkv_ref.at[c], attn_ref.at[c, here]) for c in range(3)]
            + [
                (so_ref, attn_ref.at[3, here]),
                (cq_ref, cross_ref.at[tensor, pl.ds(0, cols)]),
                (co_ref, cross_ref.at[tensor, pl.ds(cols, cols)]),
                (in_ref.at[0], win_ref.at[tensor]),
            ]
        )
    ]

    @pl.when(step == 0)
    def _():
        greet(spread.targets())
        for s in steps:
            start_self(s)
        for made in own_copies:
            made.start()

    @pl.when(step == 0)
    def _():
        low = 128
        w_ref[:cols] = wkv_ref[0]
        w_ref[cols : 2 * cols - low] = wkv_ref[1, low:]
        w_ref[2 * cols - low :] = wkv_ref[1, :low]

    def project(x, first, count):
        y = mm_nt(x, w_ref[...])
        for tile in range(y_ref.shape[0]):
            y_ref[tile, : count * items] = y[:, tile * 128 : (tile + 1) * 128]
        for item in range(items):
            k_low, high, v_low = [
                y_ref[tile, pl.ds(item, count, stride=items)].astype(NARROW) for tile in range(3)
            ]
            k_ref[item, first, :128] = k_low
            k_ref[item, first, 128:] = high[:, : cols - 128]
            v_ref[item, first, :128] = v_low
            v_ref[item, first, 128:] = high[:, cols - 128 :]

    project(
        x_ref[...].reshape(block * items, depth),
        pl.ds(pl.multiple_of(step * block, block), block),
        block,
    )

    @pl.when(step == last)
    def _():
        count = tail_ref.shape[0]
        project(
            tail_ref[...].reshape(count * items, depth),
            pl.ds(k_ref.shape[1] - count, count),
            count,
        )
        for s in steps:
            spread.along(s, self_any).wait_recv()
            spread.start_across(s)
        for s in steps:
            start_cross(s)
            feed.along(s, feed_mine).start()
        for s in steps:
            spread.start_onward(s)
        for s in steps:
            spread.start_last(s)
        for s in steps:
            spread.finish(s)
            spread.along(s, self_any).wait_send()
            cross.along(s, cross_any).wait()
            feed.along(s, feed_mine).wait()
        for made in own_copies:
            made.wait()


def start_layer(visual, wkv, qkv, so, cq, co, ffn_in, shards):
    span, items, depth = visual.shape
    cols, width = so.shape
    steps = 4
    tail = span % (16 * steps)
    block = (span - tail) // steps
    out = pl.BlockSpec((items, span, cols), lambda i: (0, 0, 0))
    shape = jax.ShapeDtypeStruct((items, span, cols), NARROW)
    copies = 3 * Spread.COPIES * (shards - 1)
    dma = pltpu.SemaphoreType.DMA
    hbm = pl.BlockSpec(memory_space=pl.ANY)

    def whole(array):
        return pl.BlockSpec(array.shape, lambda i: (0,) * array.ndim)

    return pl.pallas_call(
        start_kernel,
        grid=(steps,),
        in_specs=[
            pl.BlockSpec((block, items, depth), lambda i: (i, 0, 0)),
            pl.BlockSpec((tail, items, depth), lambda i: (span // tail - 1, 0, 0)),
            pl.BlockSpec(wkv.shape, lambda i: (0, 0, 0)),
            whole(qkv), whole(so), whole(cq), whole(co),
            pl.BlockSpec((1,) + ffn_in.shape[1:], lambda i: (0, 0, 0)),
        ],
        out_specs=[out, out, hbm, hbm, hbm],
        out_shape=[
            shape, shape,
            jax.ShapeDtypeStruct((4, shards * cols, width), NARROW),
            jax.ShapeDtypeStruct((shards,) + ffn_in.shape[1:], NARROW),
            jax.ShapeDtypeStruct((shards, 2 * cols, width), NARROW),
        ],
        scratch_shapes=[
            pltpu.VMEM((2 * cols, depth), NARROW),
            pltpu.VMEM((2 * cols // 128, block * items, 128), WIDE),
            dma((copies,)), dma((copies,)), dma((7,)),
        ],
        compiler_params=pltpu.CompilerParams(
            collective_id=0, has_side_effects=True, vmem_limit_bytes=VMEM_BYTES
        ),
        name="start_layer",
    )(visual, visual, wkv, qkv, so, cq, co, ffn_in)


def feed_copies(shards):
    return 5 * Spread.COPIES * (shards - 1)


def labels_of(position, ends):
    place = position - NQ
    label = jnp.zeros_like(position)
    for end in ends:
        label = label + jnp.where(place >= end, 1, 0)
    return jnp.where(position < NQ, -1, label)


def allowed_pairs(lens_ref, item, span, lanes):
    ends = []
    total = jnp.int32(0)
    for c in range(lens_ref.shape[1]):
        total = total + lens_ref[item, c]
        ends.append(total)
    key_label = labels_of(lax.broadcasted_iota(jnp.int32, (span, lanes), 0), ends)
    query_label = labels_of(lax.broadcasted_iota(jnp.int32, (span, lanes), 1) % span, ends)
    return (key_label == query_label) | (key_label == -1)


def self_forward_kernel(
    lens_ref, x_ref, w_ref, gain_ref, shift_ref, out_ref, in_ref, cross_in, ffn_in, ffn_out,
    q_ref, k_ref, v_ref, p_ref, ctx_ref, res_ref, fq_ref, ft_ref, win_ref, wout_ref, cross_ref, tin_ref, tout_ref,
    send, recv, local,
):
    del in_ref, cross_in
    step = pl.program_id(0)
    tensor = lax.axis_index("tensor")
    shards = lax.axis_size("tensor")
    base = Spread.COPIES * (shards - 1)
    first_in = Spread(eighth(win_ref), send, recv, 0)
    first_out = Spread(eighth(wout_ref), send, recv, base)
    cross = Spread(eighth(cross_ref), send, recv, 2 * base)
    mine = eighth(out_ref)(0, first_out.peer, None)
    text = [
        Spread(one_shard(ref), send, recv, n * base).along(FAR, eighth(own)(1, first_out.peer, None))
        for n, ref, own in ((3, tin_ref, ffn_in), (4, tout_ref, ffn_out))
    ]
    own = pltpu.make_async_copy(out_ref.at[0], wout_ref.at[tensor], local.at[0])
    hops = range(1, shards)

    @pl.when(step == 0)
    def _():
        greet(first_out.targets())
        for s in hops:
            first_out.along(s, mine).start()
            cross.start_across(s)
        for s in hops:
            first_in.start_across(s)
        for made in text:
            made.start()
        own.start()

    span = NQ + TXT
    items = x_ref.shape[0] // span
    lanes = QUAD * HEAD
    x = x_ref[...]
    q_ref[...] = (mm_nt(x, w_ref[0]) .astype(NARROW).astype(WIDE) * SCALE).astype(NARROW)
    k_ref[...] = mm_nt(x, w_ref[1]).astype(NARROW)
    v_ref[...] = mm_nt(x, w_ref[2]).astype(NARROW)

    units = []
    for item in range(items):
        rows = slice(item * span, (item + 1) * span)
        allowed = allowed_pairs(lens_ref, pl.program_id(0) * items + item, span, lanes)
        for quad in range(x_ref.shape[1] // lanes):
            units.append((rows, slice(quad * lanes, (quad + 1) * lanes), allowed))
    scores = [mm_nt(k_ref[r, c], spread_heads(q_ref[r, c], QUAD)) for r, c, _ in units]
    lows = []
    for value, (r, c, allowed) in zip(scores, units):
        value = jnp.where(allowed, value, MASKED_SCORE)
        lifted = jnp.exp(value - jnp.max(value, axis=0, keepdims=True))
        lows.append((lifted * (1.0 / jnp.sum(lifted, axis=0, keepdims=True))).astype(NARROW))
        p_ref[r, c] = lows[-1]
    parts = [mm_tn(low, v_ref[r, c]) for low, (r, c, _) in zip(lows, units)]
    for part, (r, c, _) in zip(parts, units):
        ctx_ref[r, c] = gather_heads(part, QUAD).astype(NARROW)

    residue = x.astype(WIDE) + mm(ctx_ref[...], w_ref[3])
    res_ref[...] = residue
    unit, _ = norm_parts(residue)
    first = unit * gain_ref[0:1] + shift_ref[0:1]
    for item in range(items):
        fq_ref[item * NQ : (item + 1) * NQ] = first[item * span : item * span + NQ]
        ft_ref[item * TXT : (item + 1) * TXT] = first[item * span + NQ : (item + 1) * span]

    @pl.when(step == pl.num_programs(0) - 1)
    def _():
        for s in hops:
            cross.wait_across(s)
            first_in.wait_across(s)
            first_out.along(s, mine).wait()
        for made in text:
            made.wait()
        own.wait()


def self_forward(hidden, lens, weights, gain, shift, ffn_in, ffn_out, win, cross, shards):
    rows, width = hidden.shape
    block = min(rows, 256)
    half = block // 2
    full = pl.BlockSpec((block, width), lambda i: (i, 0))
    halves = pl.BlockSpec((half, width), lambda i: (i, 0))
    low = jax.ShapeDtypeStruct((rows, width), NARROW)
    hbm = pl.BlockSpec(memory_space=pl.ANY)
    dma = pltpu.SemaphoreType.DMA
    return pl.pallas_call(
        self_forward_kernel,
        grid=(rows // block,),
        in_specs=[
            pl.BlockSpec(memory_space=pltpu.SMEM),
            full,
            pl.BlockSpec(weights.shape, lambda i: (0, 0, 0)),
            pl.BlockSpec(gain.shape, lambda i: (0, 0)),
            pl.BlockSpec(shift.shape, lambda i: (0, 0)),
            pl.BlockSpec((1,) + ffn_out.shape[1:], lambda i: (0, 0, 0)), hbm, hbm, hbm, hbm,
        ],
        out_specs=[full, full, full, full, full, full, halves, halves, hbm, hbm, hbm, hbm, hbm],
        out_shape=[
            low, low, low, low, low,
            jax.ShapeDtypeStruct((rows, width), WIDE),
            jax.ShapeDtypeStruct((rows // 2, width), WIDE),
            jax.ShapeDtypeStruct((rows // 2, width), WIDE),
            jax.ShapeDtypeStruct(win.shape, NARROW),
            jax.ShapeDtypeStruct((shards,) + ffn_out.shape[1:], NARROW),
            jax.ShapeDtypeStruct(cross.shape, NARROW),
            jax.ShapeDtypeStruct(ffn_in.shape[1:], NARROW),
            jax.ShapeDtypeStruct(ffn_out.shape[1:], NARROW),
        ],
        input_output_aliases={6: 8, 7: 10},
        scratch_shapes=[
            dma((feed_copies(shards),)), dma((feed_copies(shards),)), dma((1,)),
        ],
        compiler_params=pltpu.CompilerParams(
            collective_id=3, has_side_effects=True, vmem_limit_bytes=VMEM_BYTES
        ),
        name="self_forward",
    )(lens, hidden, weights, gain, shift, ffn_out, win, cross, ffn_in, ffn_out)


def self_backward_kernel(
    x_ref, w_ref, gain_ref, res_ref, gq_ref, gt_ref, q_ref, k_ref, v_ref, p_ref, ctx_ref,
    kv_ref, cross_ref, piece0_ref, piece1_ref,
    grad_ref, grads_ref, gain_out, shift_out, kv_low, kv_high, cross_piece, feed_total,
    down, dctx, dq, dk, dv, acc, *rest,
):
    parts = cross_parts(kv_ref.shape, cross_ref.shape)
    total, land, higher = rest[:2], rest[2:5], rest[5:8]
    send, recv, feed_send, feed_recv, local = rest[8:]
    later = PeerSum(feed_parts(x_ref.shape[1]), (), (feed_total,), (), (), feed_send, feed_recv)
    peers = PeerSum(parts, (kv_ref, cross_ref), total, land, higher, send, recv)
    span = NQ + TXT
    block = res_ref.shape[0]
    items = block // span
    lanes = QUAD * HEAD
    placed = [
        pltpu.make_async_copy(ref, later.rows((feed_total,), part, later.final_piece(part), 1), local.at[n])
        for n, (ref, part) in enumerate(zip((piece0_ref, piece1_ref), later.parts))
    ]
    step = pl.program_id(0)

    @pl.when(step == 0)
    def _():
        for made in placed:
            made.start()
        greet(peers.targets())
        peers.start_halving(0)
        for made in placed:
            made.wait()
        later.start_gathering(0)

    @pl.when(step == 1)
    def _():
        later.end_gathering(0)
        later.start_gathering(1)
        peers.end_halving(0)
        peers.start_halving(1)

    @pl.when(step == 3)
    def _():
        peers.end_halving(1)
        peers.start_halving(2)

    unit, inverse = norm_parts(res_ref[...])
    pieces = []
    for item in range(items):
        pieces.append(gq_ref[item * NQ : (item + 1) * NQ])
        pieces.append(gt_ref[item * TXT : (item + 1) * TXT])
    cotangent = jnp.concatenate(pieces, axis=0)
    grad_res = norm_back(unit, inverse, gain_ref[0:1], cotangent)
    gain_sum, shift_sum = column_sums(unit, cotangent)

    @pl.when(step == 0)
    def _():
        gain_out[...] = gain_sum
        shift_out[...] = shift_sum

    @pl.when(step > 0)
    def _():
        gain_out[...] += gain_sum
        shift_out[...] += shift_sum

    grad_ref[...] = grad_res
    low = grad_res.astype(NARROW)
    down[...] = low
    dctx[...] = mm_nt(low, w_ref[3]).astype(NARROW)

    units = [
        (slice(item * span, (item + 1) * span), slice(quad * lanes, (quad + 1) * lanes))
        for item in range(items)
        for quad in range(w_ref.shape[2] // lanes)
    ]
    for at in range(0, len(units), UNITS):
        some = units[at : at + UNITS]
        spread = [spread_heads(dctx[u], QUAD) for u in some]
        grad_chances = [mm_nt(v_ref[u], one) for u, one in zip(some, spread)]
        scores = []
        for u, value in zip(some, grad_chances):
            weighted = p_ref[u].astype(WIDE)
            inner = jnp.sum(value * weighted, axis=0, keepdims=True)
            scores.append((weighted * (value - inner)).astype(NARROW))
        for u, one in zip(some, spread):
            dv[u] = mm(p_ref[u], one).astype(NARROW)
        for u, one in zip(some, scores):
            dk[u] = mm(one, spread_heads(q_ref[u], QUAD)).astype(NARROW)
        values = [mm_tn(one, k_ref[u]) for u, one in zip(some, scores)]
        for u, value in zip(some, values):
            dq[u] = (gather_heads(value, QUAD) * SCALE).astype(NARROW)

    grad_ref[...] += mm(dq[...], w_ref[0]) + mm(dk[...], w_ref[1]) + mm(dv[...], w_ref[2])

    own = lax.axis_index("tensor")
    cols = grads_ref.shape[0] // 4
    window = acc.shape[1]
    start = pl.multiple_of((own * cols) // 128 * 128, 128)
    here = pl.ds(start, window)
    x = x_ref[...]
    products = (
        mm_tn(dq[:, here], x), mm_tn(dk[:, here], x), mm_tn(dv[:, here], x),
        mm_tn(ctx_ref[:, here], down[...]),
    )

    @pl.when(step == 0)
    def _():
        for c, product in enumerate(products):
            acc[c] = product

    @pl.when(step > 0)
    def _():
        for c, product in enumerate(products):
            acc[c] += product

    @pl.when(step == pl.num_programs(0) - 1)
    def _():
        offset = pl.multiple_of(own * cols - start, 64)
        for c in range(4):
            grads_ref[c * cols : (c + 1) * cols] = acc[c, pl.ds(offset, cols), :].astype(NARROW)
        peers.end_halving(2)
        peers.far()
        for out, part in zip((kv_low, kv_high, cross_piece), parts):
            out[...] = peers.rows(total, part, peers.final_piece(part), 1)[...]
        later.end_gathering(1)


def self_backward(
    hidden, weights, gain, residue, grad_q, grad_t, q, k, v, p, ctx, kv, cross, piece0, piece1,
    cols, ident, peers
):
    rows, width = hidden.shape
    block = min(rows, 256)
    half = block // 2
    full = pl.BlockSpec((block, width), lambda i: (i, 0))
    halves = pl.BlockSpec((half, width), lambda i: (i, 0))
    row = pl.BlockSpec((1, width), lambda i: (0, 0))
    parts = cross_parts(kv.shape, cross.shape)
    far = (peers // PEERS - 1).bit_length()
    pieces = [(p_[2], p_[4]) for p_ in parts]
    hbm = pl.BlockSpec(memory_space=pl.ANY)
    dma = pltpu.SemaphoreType.DMA
    count = PeerSum.copies(feed_parts(width), far)

    def whole(shape):
        return pl.BlockSpec(shape, lambda i: (0,) * len(shape))

    return pl.pallas_call(
        self_backward_kernel,
        grid=(rows // block,),
        in_specs=[
            full,
            pl.BlockSpec(weights.shape, lambda i: (0, 0, 0)),
            pl.BlockSpec(gain.shape, lambda i: (0, 0)),
            full, halves, halves, full, full, full, full, full,
            whole(kv.shape), whole(cross.shape), whole(piece0.shape), whole(piece1.shape),
        ],
        out_specs=[full, whole((4 * cols, width)), row, row] + [whole(p_) for p_ in pieces] + [hbm],
        out_shape=[
            jax.ShapeDtypeStruct((rows, width), WIDE),
            jax.ShapeDtypeStruct((4 * cols, width), NARROW),
            jax.ShapeDtypeStruct((1, width), WIDE),
            jax.ShapeDtypeStruct((1, width), WIDE),
        ]
        + [jax.ShapeDtypeStruct(p_, NARROW) for p_ in pieces]
        + [jax.ShapeDtypeStruct((4 * width, width), NARROW)],
        scratch_shapes=[pltpu.VMEM((block, width), NARROW)] * 5
        + [pltpu.VMEM((4, (cols + 64 + 127) // 128 * 128, width), WIDE)]
        + peer_scratch(parts, [kv.shape, cross.shape], far)
        + [dma((count,)), dma((count,)), dma((2,))],
        compiler_params=pltpu.CompilerParams(
            collective_id=ident, has_side_effects=True, vmem_limit_bytes=VMEM_BYTES
        ),
        name="self_backward",
    )(hidden, weights, gain, residue, grad_q, grad_t, q, k, v, p, ctx, kv, cross, piece0, piece1)


def feed_parts(width):
    rows = 4 * width
    return ((0, 0, rows // 2 // PIECES, 0, width, 0), (0, rows // 2, rows // 2 // PIECES, 0, width, 1))


LOADS = (
    "fq", "wq_own", "k", "v", "ft", "tin", "tout", "cotq", "tcot", "wo_own", "w_all", "tin2", "tout2",
)
STORES = ("outq", "outt", "gq", "gt", "grads", "kv", "piece0", "piece1")


def middle_kernel(names, *refs):
    r = types.SimpleNamespace(**dict(zip(names, refs)))
    cols = r.wq_own.shape[0]
    heads = cols // HEAD
    items, span = r.k.shape[:2]
    width = r.fq.shape[1]
    depth = r.visual.shape[2]
    chunks = r.win.shape[0]
    tensor = lax.axis_index("tensor")
    sources = dict(
        tin=r.ffn_in.at[1], tout=r.ffn_out.at[1],
        w_all=r.cross_o.at[:, pl.ds(cols, cols)], tin2=r.tin2_o, tout2=r.tout2_o,
    )
    rows = [slice(item * NQ, (item + 1) * NQ) for item in range(items)]
    tall = r.fq.shape

    def load(name, goal=None):
        return pltpu.make_async_copy(
            sources.get(name, getattr(r, name, None)),
            getattr(r, name + "_v") if goal is None else goal,
            r.load_sem.at[LOADS.index(name)],
        )

    def store(name, source):
        return pltpu.make_async_copy(source, getattr(r, name + "_o"), r.store_sem.at[STORES.index(name)])

    pair = (lax.axis_index("dp"), tensor + 1 - 2 * (tensor % 2))
    swaps = [remote(r.tpart.at[n], r.tland.at[n], r.swap_send.at[n], r.swap_recv.at[n], pair) for n in range(2)]
    forth = HeadGather(r.heads1, r.head_send1, r.head_recv1)
    gather = HeadGather(r.heads2, r.head_send2, r.head_recv2)
    base = Spread.COPIES * (chunks - 1)
    hops = range(1, chunks)
    first_in = Spread(eighth(r.win_o), r.spread_send, r.spread_recv, 0)
    first_out = Spread(eighth(r.wout_o), r.spread_send, r.spread_recv, base)
    cross = Spread(eighth(r.cross_o), r.spread_send, r.spread_recv, 2 * base)
    text = [
        Spread(one_shard(ref), r.spread_send, r.spread_recv, n * base) for n, ref in ((3, r.tin2_o), (4, r.tout2_o))
    ]
    parts = feed_parts(width)
    feed = [None]
    peers = PeerSum(
        parts, feed, (), r.land, r.higher, r.peer_send, r.peer_recv, pieces=(r.piece0, r.piece1)
    )
    early = ("tin_v", "tout_v", "tin2_v", "tout2_v", "tslope", "tslope2", "cotq_v", "tcot_v")

    def to_feed_forward(*buffers):
        for name, buffer in zip(early, buffers):
            setattr(r, name, buffer)
        for name in LOADS[:10]:
            load(name).start()
        greet(first_in.along_targets() + peers.targets())
        for s in hops:
            cross.start_onward(s, True)
        for s in hops:
            first_in.start_onward(s, True)
            first_out.start_across(s)
        for one in text:
            one.start_across(FAR)
        for name in ("fq", "wq_own", "k", "v"):
            load(name).wait()
        r.q[...] = (
            mm_nt(r.fq_v[...].astype(NARROW), r.wq_own_v[...]).astype(NARROW).astype(WIDE) * SCALE
        ).astype(NARROW)
        for half in range(2):
            some = range(half * items // 2, (half + 1) * items // 2)
            scores = [mm_nt(r.k_v[item], spread_heads(r.q[rows[item]], heads)) for item in some]
            lows = []
            for item, value in zip(some, scores):
                lifted = jnp.exp(value - jnp.max(value, axis=0, keepdims=True))
                lows.append((lifted * (1.0 / jnp.sum(lifted, axis=0, keepdims=True))).astype(NARROW))
                r.p[item] = lows[-1]
            values = [mm_tn(low, r.v_v[item]) for item, low in zip(some, lows)]
            for item, value in zip(some, values):
                r.ctx[rows[item]] = gather_heads(value, heads).astype(NARROW)
            count = items // 2 * NQ
            here = slice(half * count, (half + 1) * count)
            r.heads1[tensor, here] = r.ctx[here]
            forth.start(half)
        for s in hops:
            cross.start_last(s)

        def text_part(win, wout, slope_v, act_v):
            act, slope = gelu_parts(mm(r.ft_v[...].astype(NARROW), win[...]))
            slope_v[...] = slope.astype(NARROW)
            act = act.astype(NARROW)
            if act_v is not None:
                act_v[...] = act
            return mm(act, wout[...])

        for name in ("ft", "tin", "tout"):
            load(name).wait()
        r.gt_v[...] = text_part(r.tin_v, r.tout_v, r.tslope, r.tact)
        for s in hops:
            cross.finish(s, True)
        load("w_all").start()
        for one in text:
            one.start_onward(FAR)
        for s in hops:
            first_out.start_onward(s)
        for s in hops:
            first_in.start_last(s)
        for one in text:
            one.start_last(FAR)
        for one in text:
            one.finish(FAR)
        load("tin2").start()
        load("tout2").start()
        forth.wait(0)
        forth.wait(1)
        load("w_all").wait()
        r.gq_v[...] = forth.product(r.w_all_v)
        sources["w_all"] = r.cross_o.at[:, pl.ds(0, cols)]
        load("w_all").start()
        load("tin2").wait()
        load("tout2").wait()
        r.tpart[0] = (r.gt_v[...] + text_part(r.tin2_v, r.tout2_v, r.tslope2, None)).astype(NARROW)
        swaps[0].start()
        for s in hops:
            first_out.start_last(s)
        for s in hops:
            first_in.finish(s, True)

        def text_rows():
            load("tcot").wait()
            unit, inverse = norm_parts(r.ft_v[...] + r.tpart[0].astype(WIDE) + r.tland[0].astype(WIDE))
            r.outt[...] = (unit * r.gain[3:4] + r.shift[3:4]).astype(NARROW)
            store("outt", r.outt).start()
            cotangent = r.tcot_v[...].astype(WIDE)
            gain_sum, shift_sum = column_sums(unit, cotangent)
            r.gains[2:3] = gain_sum
            r.shifts[2:3] = shift_sum
            grad = norm_back(unit, inverse, r.gain[3:4], cotangent)
            r.gt_v[...] = grad
            r.ttop[...] = grad.astype(NARROW)
            r.tdpre[...] = (mm_nt(r.ttop[...], r.tout_v[...]) * r.tslope[...].astype(WIDE)).astype(NARROW)
            far = (mm_nt(r.ttop[...], r.tout2_v[...]) * r.tslope2[...].astype(WIDE)).astype(NARROW)
            r.tpart[1] = (mm_nt(r.tdpre[...], r.tin_v[...]) + mm_nt(far, r.tin2_v[...])).astype(NARROW)
            swaps[1].start()

        def query_rows(slopes, total, weights, outq):
            def fetch(j):
                slot, chunk = j % 2, j % chunks
                return [
                    pltpu.make_async_copy(ref.at[chunk], weights.at[slot, n], r.weight_sem.at[slot, n])
                    for n, ref in enumerate((r.win_o, r.wout_o))
                ]

            unit, _ = norm_parts(r.fq_v[...] + r.gq_v[...])
            value = unit * r.gain[1:2] + r.shift[1:2]
            r.low[...] = value.astype(NARROW)
            total[...] = value
            for s in hops:
                first_out.finish(s)
            for made in fetch(0):
                made.start()

            def next_weights(j):
                for made in fetch(j):
                    made.wait()

                @pl.when(j + 1 < 2 * chunks)
                def _():
                    for made in fetch(j + 1):
                        made.start()

                return weights.at[j % 2, 0], weights.at[j % 2, 1]

            @pl.loop(0, chunks)
            def _(j):
                win, wout = next_weights(j)
                act, slope = gelu_parts(mm(r.low[...], win[...]))
                slopes[j] = slope.astype(NARROW)
                act = act.astype(NARROW)
                total[...] += mm(act, wout[...])

                @pl.when(j == tensor)
                def _():
                    r.act[...] = act


            unit, inverse = norm_parts(total[...])
            outq[...] = (unit * r.gain[2:3] + r.shift[2:3]).astype(NARROW)
            store("outq", outq).start()
            load("cotq").wait()
            cotangent = r.cotq_v[...].astype(WIDE)
            gain_sum, shift_sum = column_sums(unit, cotangent)
            r.gains[1:2] = gain_sum
            r.shifts[1:2] = shift_sum
            grad = norm_back(unit, inverse, r.gain[2:3], cotangent)
            total[...] = grad
            r.top[...] = grad.astype(NARROW)

            @pl.loop(chunks, 2 * chunks)
            def _(j):
                win, wout = next_weights(j)
                chunk = j - chunks
                dpre = (mm_nt(r.top[...], wout[...]) * slopes[chunk].astype(WIDE)).astype(NARROW)
                total[...] += mm_nt(dpre, win[...])

                @pl.when(chunk == tensor)
                def _():
                    r.dpre[...] = dpre

                @pl.when(chunk == 2)
                def _():
                    swaps[0].wait()
                    text_rows()


            grad_second = total[...]
            unit, inverse = norm_parts(r.fq_v[...] + r.gq_v[...])
            gain_sum, shift_sum = column_sums(unit, grad_second)
            r.gains[0:1] = gain_sum
            r.shifts[0:1] = shift_sum
            grad = norm_back(unit, inverse, r.gain[1:2], grad_second)
            r.gq_v[...] = grad
            r.down[...] = grad.astype(NARROW)
            store("outq", outq).wait()

        pl.run_scoped(
            query_rows,
            pltpu.VMEM((chunks, tall[0], r.win.shape[2]), NARROW),
            pltpu.VMEM(tall, WIDE),
            pltpu.VMEM((2, 2) + r.win.shape[1:], NARROW),
            pltpu.VMEM(tall, NARROW),
        )

    inner, outer = r.ffn_in.shape[1:], r.ffn_out.shape[1:]
    pl.run_scoped(
        to_feed_forward,
        *[pltpu.VMEM(shape, NARROW) for shape in (inner, outer, inner, outer, (tall[0], inner[1]), (tall[0], inner[1]), tall, tall)],
    )

    def feed_gradients(goal):
        feed[0] = goal
        goal[:width] = mm_tn(r.low[...], r.dpre[...]).astype(NARROW)
        goal[width : 2 * width] = mm_tn(r.ft_v[...].astype(NARROW), r.tdpre[...]).astype(NARROW)
        goal[2 * width : 3 * width] = mm_tn(r.act[...], r.top[...]).astype(NARROW)
        goal[3 * width :] = mm_tn(r.tact[...], r.ttop[...]).astype(NARROW)
        peers.start_halving(0)

    def cross_rows(dctx, dq, score, dkv, acc, x, x_tail, kv, feed_v):
        group = items // 4
        steps = VISUAL_STEPS
        tail = span % steps
        block = (span - tail) // steps

        def fetch(j):
            return pltpu.make_async_copy(r.visual.at[pl.ds(j * block, block)], x.at[j % 2], r.x_sem.at[j % 2])

        rest = pltpu.make_async_copy(r.visual.at[pl.ds(span - tail, tail)], x_tail, r.x_sem.at[2])
        fetch(0).start()
        rest.start()
        load("wo_own").wait()
        dctx[...] = mm_nt(r.down[...], r.wo_own_v[...]).astype(NARROW)
        for g in range(4):
            some = range(g * group, (g + 1) * group)
            spread = [spread_heads(dctx[rows[item]], heads) for item in some]
            grad_chances = [mm_nt(r.v_v[item], one) for item, one in zip(some, spread)]
            scores = []
            for item, value in zip(some, grad_chances):
                weighted = r.p[item].astype(WIDE)
                inner = jnp.sum(value * weighted, axis=0, keepdims=True)
                scores.append((weighted * (value - inner)).astype(NARROW))
                score[item] = scores[-1]
            values = [mm_tn(one, r.k_v[item]) for item, one in zip(some, scores)]
            for item, value in zip(some, values):
                dq[rows[item]] = (gather_heads(value, heads) * SCALE).astype(NARROW)
            if g % 2:
                count = 2 * group * NQ
                here = slice(g // 2 * count, (g // 2 + 1) * count)
                r.heads2[tensor, here] = dq[here]
                gather.start(g // 2)
        feed_gradients(feed_v)
        none = jnp.zeros((QUAD * NQ, cols), NARROW)
        for g in range(4):
            some = range(g * group, (g + 1) * group)
            both = []
            for item in some:
                one = spread_heads(dctx[rows[item]], heads)
                both.append(
                    mm(
                        jnp.concatenate([score[item], r.p[item]], axis=1),
                        jnp.concatenate(
                            [
                                jnp.concatenate([spread_heads(r.q[rows[item]], heads), none], axis=1),
                                jnp.concatenate([none, one[:, 128:], one[:, :128]], axis=1),
                            ],
                            axis=0,
                        ),
                    )
                )
            for item, value in zip(some, both):
                for tile in range(dkv.shape[0]):
                    dkv[tile, pl.ds(item, span, stride=items)] = value[:, tile * 128 : (tile + 1) * 128]
            if g == 2:
                peers.end_halving(0)
                peers.start_halving(1)
        r.grads[:cols] = mm_tn(dq[...], r.fq_v[...].astype(NARROW)).astype(NARROW)
        r.grads[cols:] = mm_tn(r.ctx[...], r.down[...]).astype(NARROW)
        store("grads", r.grads).start()

        def product(first, count, value):
            grads = [dkv[tile, pl.ds(first, count)].astype(NARROW) for tile in range(dkv.shape[0])]
            return mm_tn(jnp.concatenate(grads, axis=1), value.reshape(count, depth))

        rest.wait()
        acc[...] = product((span - tail) * items, tail * items, x_tail[...])

        @pl.loop(0, steps)
        def _(j):
            fetch(j).wait()

            @pl.when(j + 1 < steps)
            def _():
                fetch(j + 1).start()

            acc[...] += product(pl.multiple_of(j * block * items, 16), block * items, x[j % 2])

            @pl.when(j == 11)
            def _():
                peers.end_halving(1)
                peers.start_halving(2)

        kv[...] = acc[...].astype(kv.dtype)
        store("kv", kv).start()
        gather.wait(0)
        gather.wait(1)
        load("w_all").wait()
        r.gq_v[...] += gather.product(r.w_all_v)
        store("gq", r.gq_v).start()
        swaps[1].wait()
        r.gt_v[...] += r.tpart[1].astype(WIDE) + r.tland[1].astype(WIDE)
        store("gt", r.gt_v).start()
        peers.end_halving(2)
        peers.far()
        store("piece0", r.piece0).start()
        store("piece1", r.piece1).start()
        store("kv", kv).wait()

    pl.run_scoped(
        cross_rows,
        pltpu.VMEM((tall[0], cols), NARROW),
        pltpu.VMEM((tall[0], cols), NARROW),
        pltpu.VMEM((items, span, QUAD * NQ), NARROW),
        pltpu.VMEM((2 * cols // 128, items * span, 128), WIDE),
        pltpu.VMEM((2 * cols, depth), WIDE),
        pltpu.VMEM((2, span // VISUAL_STEPS, items, depth), NARROW),
        pltpu.VMEM((span % VISUAL_STEPS, items, depth), NARROW),
        pltpu.VMEM((2 * cols, depth), NARROW),
        pltpu.VMEM((4 * width, width), NARROW),
    )
    for name, source in (
        ("outt", r.outt), ("gq", r.gq_v), ("gt", r.gt_v), ("grads", r.grads), ("piece0", r.piece0), ("piece1", r.piece1),
    ):
        store(name, source).wait()


def middle(arrays, ident, peers):
    rows, width = arrays["fq"].shape
    cols = arrays["wq_own"].shape[0]
    items, span = arrays["k"].shape[:2]
    hidden = arrays["ffn_in"].shape[2]
    depth = arrays["visual"].shape[2]
    shards = arrays["win"].shape[0]
    far = (peers // PEERS - 1).bit_length()
    parts = feed_parts(width)
    piece = (parts[0][2], width)
    dma = pltpu.SemaphoreType.DMA
    hbm, vmem = pl.BlockSpec(memory_space=pl.ANY), pl.BlockSpec(memory_space=pltpu.VMEM)

    def low(*dims):
        return pltpu.VMEM(dims, NARROW)

    def wide(*dims):
        return pltpu.VMEM(dims, WIDE)

    out = jax.ShapeDtypeStruct
    outs = dict(
        outq_o=out((rows, width), NARROW), outt_o=out((rows, width), NARROW),
        gq_o=out((rows, width), WIDE), gt_o=out((rows, width), WIDE),
        grads_o=out((2 * cols, width), NARROW), kv_o=out((2 * cols, depth), NARROW),
        piece0_o=out(piece, NARROW), piece1_o=out(piece, NARROW),
        gains=out((3, width), WIDE), shifts=out((3, width), WIDE),
        win_o=out(arrays["win"].shape, NARROW), wout_o=out(arrays["wout"].shape, NARROW),
        cross_o=out(arrays["cross_w"].shape, NARROW),
        tin2_o=out(arrays["tin2"].shape, NARROW), tout2_o=out(arrays["tout2"].shape, NARROW),
    )
    copies = feed_copies(shards)
    total = peer_scratch(parts, [], far)
    scratch = dict(
        fq_v=wide(rows, width), wq_own_v=low(cols, width), wo_own_v=low(cols, width),
        k_v=low(*arrays["k"].shape), v_v=low(*arrays["v"].shape), ft_v=wide(rows, width),
        w_all_v=low(shards, cols, width),
        q=low(rows, cols), ctx=low(rows, cols), p=low(items, span, QUAD * NQ),
        tact=low(rows, hidden),
        low=low(rows, width), top=low(rows, width), down=low(rows, width),
        act=low(rows, hidden), dpre=low(rows, hidden),
        ttop=low(rows, width), tdpre=low(rows, hidden), outt=low(rows, width),
        gq_v=wide(rows, width), gt_v=wide(rows, width), grads=low(2 * cols, width),
        tpart=low(2, rows, width), tland=low(2, rows, width), swap_send=dma((2,)), swap_recv=dma((2,)),
        heads1=low(shards, rows, cols), head_send1=dma((2, shards)), head_recv1=dma((2, shards)),
        heads2=low(shards, rows, cols), head_send2=dma((2, shards)), head_recv2=dma((2, shards)),
        spread_send=dma((copies,)), spread_recv=dma((copies,)),
        piece0=low(*piece), piece1=low(*piece),
        land=total[:2], higher=total[2:4], peer_send=total[4], peer_recv=total[5],
        load_sem=dma((len(LOADS),)), store_sem=dma((len(STORES),)), weight_sem=dma((2, 2)), x_sem=dma((3,)),
    )
    names = tuple(arrays) + tuple(outs) + tuple(scratch)
    return dict(
        zip(
            outs,
            pl.pallas_call(
                functools.partial(middle_kernel, names),
                in_specs=[vmem if name in ("gain", "shift") else hbm for name in arrays],
                out_specs=[vmem if name in ("gains", "shifts") else hbm for name in outs],
                out_shape=list(outs.values()),
                input_output_aliases={
                    list(arrays).index(a): list(outs).index(b)
                    for a, b in (
                        ("win", "win_o"), ("wout", "wout_o"), ("cross_w", "cross_o"), ("tin2", "tin2_o"), ("tout2", "tout2_o"),
                    )
                },
                scratch_shapes=list(scratch.values()),
                compiler_params=pltpu.CompilerParams(
                    collective_id=ident, has_side_effects=True, vmem_limit_bytes=62 * 2**20
                ),
                name="middle",
            )(*arrays.values()),
        )
    )


def on_device(
    hidden_in,
    visual_feats,
    caption_lengths,
    self_qkv,
    self_out,
    cross_query,
    cross_kv,
    cross_out,
    ffn_in,
    ffn_out,
    norm_gain,
    norm_shift,
    out_grad,
):
    items = visual_feats.shape[0]
    rows, width = hidden_in.shape
    span = rows // items
    cols = self_qkv.shape[2]
    shards = lax.axis_size("tensor")

    visual = jnp.swapaxes(visual_feats, 0, 1)
    cross_wq = jnp.swapaxes(cross_query, 0, 1)
    cross_k, cross_v, attn, win_q, cross_w = start_layer(
        visual, jnp.swapaxes(cross_kv, 1, 2), jnp.swapaxes(self_qkv, 1, 2), self_out, cross_wq, cross_out, ffn_in, shards
    )
    q, k, v, p, ctx, residue, first_q, first_t, win_q, wout_q, cross_w, tin_far, tout_far = self_forward(
        hidden_in, caption_lengths, attn, norm_gain, norm_shift, ffn_in, ffn_out, win_q, cross_w, shards
    )
    cot = out_grad.reshape(items, span, width)
    cot_q = cot[:, :NQ].reshape(items * NQ, width)
    cot_t = cot[:, NQ:].reshape(items * TXT, width)
    peers = lax.axis_size("dp")
    mid = middle(
        dict(
            fq=first_q, wq_own=cross_wq, k=cross_k, v=cross_v, ft=first_t, cotq=cot_q, tcot=cot_t, wo_own=cross_out,
            ffn_in=ffn_in, ffn_out=ffn_out, win=win_q, wout=wout_q, cross_w=cross_w, tin2=tin_far, tout2=tout_far, visual=visual,
            gain=norm_gain, shift=norm_shift,
        ),
        2, peers,
    )
    out_q, out_t, g_cross, g_kv = mid["outq_o"], mid["outt_o"], mid["grads_o"], mid["kv_o"]
    grad_hidden, g_self, gain_first, shift_first, *pieces, g_feed = self_backward(
        hidden_in, attn, norm_gain, residue, mid["gq_o"], mid["gt_o"], q, k, v, p, ctx, g_kv, g_cross,
        mid["piece0_o"], mid["piece1_o"], cols, 6, peers,
    )
    norms = (gain_first, shift_first, mid["gains"], mid["shifts"])
    kv_shape, cross_shape = g_kv.shape, g_cross.shape
    g_kv, g_cq, g_co, g_qkv, g_so, gains, g_feed = last_sums(
        g_self, pieces, norms, g_feed, kv_shape, cross_shape, 4, peers
    )
    g_feed = g_feed.reshape(2, 2, width, width).astype(WIDE)
    g_in, g_out = g_feed[0], g_feed[1]
    out = jnp.concatenate(
        [out_q.reshape(items, NQ, width), out_t.reshape(items, TXT, width)], axis=1
    ).reshape(rows, width)
    return (
        out,
        grad_hidden,
        jnp.swapaxes(g_qkv, 1, 2),
        g_so,
        jnp.swapaxes(g_cq, 0, 1),
        jnp.swapaxes(g_kv, 1, 2),
        g_co,
        g_in,
        g_out,
        gains[:4],
        gains[4:],
    )


def solution(mesh):
    placed = (
        P("dp", None),
        P("dp", None, None),
        P("dp", None),
        P(None, None, "tensor"),
        P("tensor", None),
        P(None, "tensor"),
        P(None, None, "tensor"),
        P("tensor", None),
        P(None, None, "tensor"),
        P(None, "tensor", None),
        P(),
        P(),
        P("dp", None),
    )
    return jax.shard_map(
        on_device,
        mesh=mesh,
        in_specs=placed,
        out_specs=(
            P("dp", None),
            P("dp", None),
            P(None, None, "tensor"),
            P("tensor", None),
            P(None, "tensor"),
            P(None, None, "tensor"),
            P("tensor", None),
            P(None, None, "tensor"),
            P(None, "tensor", None),
            P(),
            P(),
        ),
        check_vma=False,
    )
```

```python
import functools
import math
import types

import jax
import jax.numpy as jnp
from jax import lax
from jax.experimental import pallas as pl
from jax.experimental.pallas import tpu as pltpu
from jax.sharding import PartitionSpec as P

HEAD = 64
NQ = 32
TXT = 32
QUAD = 4
UNITS = 12
VISUAL_STEPS = 16
EPSILON = 1e-06
MASKED_SCORE = -1e30
SCALE = 1.0 / math.sqrt(HEAD)
WIDE = jnp.float32
NARROW = jnp.bfloat16
VMEM_BYTES = 60 * 2**20


def mm(a, b):
    return lax.dot_general(a, b, (((1,), (0,)), ((), ())), preferred_element_type=WIDE)


def mm_nt(a, b):
    return lax.dot_general(a, b, (((1,), (1,)), ((), ())), preferred_element_type=WIDE)


def mm_tn(a, b):
    return lax.dot_general(a, b, (((0,), (0,)), ((), ())), preferred_element_type=WIDE)


def lane_group(rows, lanes, size):
    return lax.broadcasted_iota(jnp.int32, (rows, lanes), 1) // size


def spread_heads(block, count):
    group = lane_group(1, block.shape[1], HEAD)
    return jnp.concatenate(
        [block * jnp.where(group == h, 1.0, 0.0).astype(NARROW) for h in range(QUAD)], axis=0
    )


def gather_heads(block, count):
    rows, lanes = block.shape[0] // QUAD, block.shape[1]
    group = lane_group(rows, lanes, HEAD)
    out = block[:rows]
    for h in range(1, count):
        out = jnp.where(group == h, block[h * rows : (h + 1) * rows], out)
    return out


def norm_parts(residue):
    mean = jnp.mean(residue, axis=-1, keepdims=True)
    centered = residue - mean
    variance = jnp.mean(centered * centered, axis=-1, keepdims=True)
    inverse = lax.rsqrt(variance + EPSILON)
    return centered * inverse, inverse


def norm_back(unit, inverse, gain_row, cotangent):
    scaled = gain_row * cotangent
    first = jnp.mean(scaled, axis=-1, keepdims=True)
    second = jnp.mean(scaled * unit, axis=-1, keepdims=True)
    return inverse * (scaled - first - unit * second)


def column_sums(unit, cotangent):
    return (
        jnp.sum(cotangent * unit, axis=0, keepdims=True),
        jnp.sum(cotangent, axis=0, keepdims=True),
    )


def gelu_parts(pre):
    bell = jnp.exp(-0.5 * pre * pre)
    half = 0.5 * lax.erf(pre * math.sqrt(0.5)) + 0.5
    return pre * half, half + pre * bell * (1.0 / math.sqrt(2.0 * math.pi))


MESH = pl.DeviceIdType.MESH
PEERS = 8


def flip(index, bit):
    return index + bit - 2 * bit * ((index // bit) % 2)


def greet(targets):
    barrier = pltpu.get_barrier_semaphore()
    for target in targets:
        pl.semaphore_signal(barrier, inc=1, device_id=target, device_id_type=MESH)
    pl.semaphore_wait(barrier, len(targets))


def remote(src, dst, send, recv, target):
    return pltpu.make_async_remote_copy(
        src_ref=src, dst_ref=dst, send_sem=send, recv_sem=recv, device_id=target, device_id_type=MESH
    )


class Spread:
    COPIES = 9

    def __init__(self, at, send, recv, base):
        self.at, self.send, self.recv, self.base = at, send, recv, base
        self.dp, self.tensor = lax.axis_index("dp"), lax.axis_index("tensor")
        self.shards = lax.axis_size("tensor")
        self.peer = self.dp % PEERS

    def hop(self, slot, s, src, dst, target):
        index = self.base + (s - 1) * self.COPIES + slot
        return remote(src, dst, self.send.at[index], self.recv.at[index], target)

    def came(self, s):
        return (self.tensor + self.shards - s) % self.shards

    def along(self, s, own):
        return self.hop(0, s, own, self.at(self.tensor, self.peer, None), (self.dp, (self.tensor + s) % self.shards))

    def hand(self, slot, s, bit, peer, half):
        place = self.at(self.came(s), peer, half)
        return self.hop(slot, s, place, place, (flip(self.dp, bit), self.tensor))

    def across(self, s):
        return [self.hand(1, s, 2, self.peer, None), self.hand(2, s, 4, self.peer, None), self.hand(3, s, 1, self.peer, None)]

    def onward(self, s):
        x, y = flip(self.peer, 2), flip(self.peer, 4)
        return (
            [self.hand(4, s, 4, x, 0), self.hand(5, s, 1, x, None)],
            [self.hand(6, s, 2, y, 1), self.hand(7, s, 1, y, None)],
        )

    def last(self, s):
        return self.hand(8, s, 1, flip(flip(self.peer, 2), 4), None)

    def start_across(self, s):
        for made in self.across(s):
            made.start()

    def wait_across(self, s):
        for made in self.across(s):
            made.wait()

    def start_onward(self, s, arrived=False):
        over_x, over_y, _ = self.across(s)
        by_x, by_y = self.onward(s)
        if not arrived:
            over_x.wait_recv()
        for made in by_x:
            made.start()
        if not arrived:
            over_y.wait_recv()
        for made in by_y:
            made.start()

    def start_last(self, s):
        by_x, by_y = self.onward(s)
        by_x[0].wait_recv()
        by_y[0].wait_recv()
        self.last(s).start()

    def finish(self, s, arrived=False):
        over = self.across(s)
        by_x, by_y = self.onward(s)
        final = self.last(s)
        for made in ([] if arrived else [over[2]]) + [by_x[1], by_y[1], final]:
            made.wait_recv()
        for made in ([] if arrived else over) + by_x + by_y + [final]:
            made.wait_send()

    def targets(self):
        return self.along_targets() + self.peer_targets()

    def along_targets(self):
        return [(self.dp, (self.tensor + s) % self.shards) for s in range(1, self.shards)]

    def peer_targets(self):
        return [(flip(self.dp, bit), self.tensor) for bit in (2, 4, 1)]


FAR = 2


def one_shard(ref):
    rows = ref.shape[0] // PEERS

    def at(shard, peer, half):
        return ref.at[half_rows(peer * rows, rows, half)]

    return at


def half_rows(first, rows, half):
    split = (rows // 2 + 15) // 16 * 16
    start, count = {None: (0, rows), 0: (0, split), 1: (split, rows - split)}[half]
    return pl.ds(pl.multiple_of(first + start, 16), count)


def eighth(ref):
    rows = ref.shape[1] // PEERS

    def at(shard, peer, half):
        return ref.at[shard, half_rows(peer * rows, rows, half)]

    return at


class HeadGather:
    def __init__(self, buffer, send, recv):
        self.buffer, self.send, self.recv = buffer, send, recv
        self.dp, self.tensor = lax.axis_index("dp"), lax.axis_index("tensor")
        self.shards = lax.axis_size("tensor")

    def copies(self, half):
        count = self.buffer.shape[1] // 2
        place = self.buffer.at[self.tensor, pl.ds(half * count, count)]
        return [
            remote(place, place, self.send.at[half, s], self.recv.at[half, s], (self.dp, (self.tensor + s) % self.shards))
            for s in range(1, self.shards)
        ]

    def start(self, half):
        for made in self.copies(half):
            made.start()

    def wait(self, half):
        for made in self.copies(half):
            made.wait()

    def product(self, weights):
        total = mm(self.buffer[0], weights[0])
        for shard in range(1, self.shards):
            total += mm(self.buffer[shard], weights[shard])
        return total


PIECES = 8


class PeerSum:
    def __init__(self, parts, source, total, land, higher, send, recv, base=0, pieces=None):
        self.parts, self.source, self.total, self.land, self.higher = parts, source, total, land, higher
        self.pieces = pieces
        self.send, self.recv, self.base = send, recv, base
        self.dp, self.tensor = lax.axis_index("dp"), lax.axis_index("tensor")
        self.bits = [(self.dp // b) % 2 for b in (1, 2, 4)]

    @staticmethod
    def far_bits():
        return [PEERS << k for k in range((lax.axis_size("dp") // PEERS - 1).bit_length())]

    @staticmethod
    def copies(parts, far):
        return len(parts) * (6 + far)

    def way(self, part):
        order = ((2, self.bits[1]), (4, self.bits[2]))
        return order if part[5] == 0 else order[::-1]

    def rows(self, refs, part, piece, count):
        array, first, size, column, columns, _ = part
        start = pl.multiple_of(first + piece * size, 16)
        return refs[array].at[pl.ds(start, count * size), pl.ds(column, columns)]

    def hop(self, n, stage, src, dst, bit):
        index = self.base + n * (6 + len(self.far_bits())) + stage
        return remote(src, dst, self.send.at[index], self.recv.at[index], (flip(self.dp, bit), self.tensor))

    def landed(self, n, piece, count):
        size = self.parts[n][2]
        return self.land[n].at[pl.ds(pl.multiple_of(piece * size, 16), count * size)]

    def halving(self, n, stage):
        part = self.parts[n]
        core = self.bits[0]
        (bit_1, own_1), (bit_2, own_2) = self.way(part)
        if stage == 0:
            bit, place = 1, self.landed(n, 0, 4)
            out = self.rows(self.source, part, (1 - core) * 4, 4)
            kept = self.rows(self.source, part, core * 4, 4)
        elif stage == 1:
            bit, place = bit_1, self.landed(n, 4, 2)
            out, kept = self.landed(n, (1 - own_1) * 2, 2), self.landed(n, own_1 * 2, 2)
        else:
            bit, place = bit_2, self.landed(n, 6, 1)
            out, kept = self.landed(n, 4 + 1 - own_2, 1), self.landed(n, 4 + own_2, 1)
        goal = self.final_place(n) if stage == 2 else place
        return self.hop(n, stage, out, place, bit), kept, place, goal

    def final_place(self, n):
        if self.pieces is not None:
            return self.pieces[n]
        return self.rows(self.total, self.parts[n], self.final_piece(self.parts[n]), 1)

    def final_piece(self, part):
        (_, own_1), (_, own_2) = self.way(part)
        return self.bits[0] * 4 + own_1 * 2 + own_2

    def gathering(self, n, stage):
        part = self.parts[n]
        core = self.bits[0]
        (bit_1, own_1), (bit_2, _) = self.way(part)
        piece, count, bit = (
            (self.final_piece(part), 1, bit_2), (core * 4 + own_1 * 2, 2, bit_1), (core * 4, 4, 1),
        )[stage]
        place = self.rows(self.total, part, piece, count)
        return self.hop(n, 3 + stage, place, place, bit)

    def targets(self):
        return [(flip(self.dp, bit), self.tensor) for bit in [1, 2, 4] + self.far_bits()]

    def start_halving(self, stage):
        for n in range(len(self.parts)):
            self.halving(n, stage)[0].start()

    def end_halving(self, stage):
        for n in range(len(self.parts)):
            made, kept, place, goal = self.halving(n, stage)
            made.wait_recv()
            goal[...] = (kept[...].astype(WIDE) + place[...].astype(WIDE)).astype(goal.dtype)
        for n in range(len(self.parts)):
            self.halving(n, stage)[0].wait_send()

    def far(self):
        for k, bit in enumerate(self.far_bits()):
            for n in range(len(self.parts)):
                place = self.final_place(n)
                made = self.hop(n, 6 + k, place, self.higher[n].at[k], bit)
                made.start()
                made.wait()
                place[...] = (place[...].astype(WIDE) + self.higher[n][k].astype(WIDE)).astype(place.dtype)

    def start_gathering(self, stage):
        for n in range(len(self.parts)):
            self.gathering(n, stage).start()

    def end_gathering(self, stage):
        for n in range(len(self.parts)):
            self.gathering(n, stage).wait()


def peer_scratch(parts, shapes, far):
    dma = pltpu.SemaphoreType.DMA
    count = PeerSum.copies(parts, far)
    land = [pltpu.VMEM((7 * p[2], p[4]), NARROW) for p in parts]
    higher = [pltpu.VMEM((far, p[2], p[4]) if far else (1, 16, 128), NARROW) for p in parts]
    return [pltpu.VMEM(shape, NARROW) for shape in shapes] + land + higher + [dma((count,)), dma((count,))]


def sum_rows(values, out, land, send, recv):
    dp, tensor = lax.axis_index("dp"), lax.axis_index("tensor")
    bits = [1, 2, 4] + PeerSum.far_bits()

    def hop(k):
        source = values if k == 0 else out.at[k - 1]
        return remote(source, land.at[k], send.at[k], recv.at[k], (flip(dp, bits[k]), tensor))

    def run(k):
        if k > 0:
            hop(k - 1).wait()
            out[k - 1] = (values if k == 1 else out.at[k - 2])[...] + land[k - 1]
        if k < len(bits):
            hop(k).start()

    return [functools.partial(run, k) for k in range(len(bits) + 1)]


def cross_parts(kv, cross):
    width = cross[1]
    return (
        (0, 0, kv[0] // PIECES, 0, width, 0),
        (0, 0, kv[0] // PIECES, width, kv[1] - width, 1),
        (1, 0, cross[0] // PIECES, 0, width, 0),
    )


def self_parts(own):
    third, width = own[0] // 3, own[1]
    return ((0, 0, third // PIECES, 0, width, 0), (0, third, 2 * third // PIECES, 0, width, 1))


def feed_copies(shards):
    return 5 * Spread.COPIES * (shards - 1)


def labels_of(position, ends):
    place = position - NQ
    label = jnp.zeros_like(position)
    for end in ends:
        label = label + jnp.where(place >= end, 1, 0)
    return jnp.where(position < NQ, -1, label)


def allowed_pairs(lens_ref, item, span, lanes):
    ends = []
    total = jnp.int32(0)
    for c in range(lens_ref.shape[0]):
        total = total + lens_ref[c, item]
        ends.append(total)
    key_label = labels_of(lax.broadcasted_iota(jnp.int32, (span, lanes), 0), ends)
    query_label = labels_of(lax.broadcasted_iota(jnp.int32, (span, lanes), 1) % span, ends)
    return (key_label == query_label) | (key_label == -1)


VISUAL_BLOCKS = 4


def first_kernel(names, *refs):
    r = types.SimpleNamespace(**dict(zip(names, refs)))
    step = pl.program_id(0)
    last = pl.num_programs(0) - 1
    block, items, depth = r.visual.shape
    cols = r.so.shape[0]
    per = PEERS // 4
    rows = cols // per
    base = Spread.COPIES * (lax.axis_size("tensor") - 1)

    def at(shard, peer, half):
        return r.attn_v.at[peer // per, half_rows(shard * cols + (peer % per) * rows, rows, half)]

    def spread_to(where, n):
        return Spread(where, r.send, r.recv, n * base)

    attn = spread_to(at, 0)
    first_in, first_out, cross = (spread_to(eighth(ref), n + 1) for n, ref in enumerate((r.win, r.wout, r.cross)))
    text = [spread_to(one_shard(ref), n + 4) for n, ref in enumerate((r.tin, r.tout))]
    peer, tensor = attn.peer, attn.tensor
    hops = range(1, attn.shards)
    few = 2 * cols // PEERS

    def eighth_of(ref, first, count):
        return ref.at[pl.ds(pl.multiple_of(first, 16), count)]

    def start_attn(s):
        @pl.when(peer < 3 * per)
        def _():
            attn.along(s, eighth_of(r.qkv.at[peer // per], (peer % per) * rows, rows)).start()

        @pl.when(peer >= 3 * per)
        def _():
            attn.along(s, eighth_of(r.so, (peer - 3 * per) * rows, rows)).start()

    def start_cross(s):
        @pl.when(peer < PEERS // 2)
        def _():
            cross.along(s, eighth_of(r.cq, peer * few, few)).start()

        @pl.when(peer >= PEERS // 2)
        def _():
            cross.along(s, eighth_of(r.co, (peer - PEERS // 2) * few, few)).start()

    attn_any, cross_any = r.so.at[pl.ds(0, rows)], r.co.at[pl.ds(0, few)]
    in_mine, out_mine = (eighth(ref)(0, peer, None) for ref in (r.ffn_in_first, r.ffn_out_first))
    text_mine = [eighth(ref)(1, peer, None) for ref in (r.ffn_in, r.ffn_out)]
    here = pl.ds(pl.multiple_of(tensor * cols, 16), cols)
    own_copies = [
        pltpu.make_async_copy(source, goal, r.local.at[n])
        for n, (source, goal) in enumerate(
            [(r.qkv.at[c], r.attn_v.at[c, here]) for c in range(3)]
            + [
                (r.so, r.attn_v.at[3, here]),
                (r.cq, r.cross.at[tensor, pl.ds(0, cols)]),
                (r.co, r.cross.at[tensor, pl.ds(cols, cols)]),
                (r.ffn_in_first.at[0], r.win.at[tensor]),
                (r.ffn_out_first.at[0], r.wout.at[tensor]),
            ]
        )
    ]
    keep = pltpu.make_async_copy(r.attn_v, r.attn, r.local.at[len(own_copies)])

    @pl.when(step == 0)
    def _():
        greet(attn.targets())
        for s in hops:
            start_attn(s)
        for made in own_copies:
            made.start()
        low = 128
        r.w[:cols] = r.wkv[0]
        r.w[cols : 2 * cols - low] = r.wkv[1, low:]
        r.w[2 * cols - low :] = r.wkv[1, :low]

    def project(x, first, count):
        y = mm_nt(x, r.w[...])
        for tile in range(r.y.shape[0]):
            r.y[tile, : count * items] = y[:, tile * 128 : (tile + 1) * 128]
        for item in range(items):
            k_low, high, v_low = [
                r.y[tile, pl.ds(item, count, stride=items)].astype(NARROW) for tile in range(3)
            ]
            r.cross_k[item, first, :128] = k_low
            r.cross_k[item, first, 128:] = high[:, : cols - 128]
            r.cross_v[item, first, :128] = v_low
            r.cross_v[item, first, 128:] = high[:, cols - 128 :]

    @pl.when(step < VISUAL_BLOCKS)
    def _():
        project(
            r.visual[...].reshape(block * items, depth),
            pl.ds(pl.multiple_of(step * block, block), block),
            block,
        )

    @pl.when(step == VISUAL_BLOCKS - 1)
    def _():
        count = r.visual_tail.shape[0]
        project(
            r.visual_tail[...].reshape(count * items, depth),
            pl.ds(r.cross_k.shape[1] - count, count),
            count,
        )
        for s in hops:
            attn.along(s, attn_any).wait_recv()
            attn.start_across(s)
        for s in hops:
            start_cross(s)
        for s in hops:
            first_in.along(s, in_mine).start()
        for one, mine in zip(text, text_mine):
            one.along(FAR, mine).start()
        for s in hops:
            first_out.along(s, out_mine).start()
        for s in hops:
            attn.start_onward(s)
        for s in hops:
            attn.start_last(s)
        for s in hops:
            attn.finish(s)
            attn.along(s, attn_any).wait_send()
        for made in own_copies:
            made.wait()
        keep.start()

    @pl.when(step == VISUAL_BLOCKS + 1)
    def _():
        for s in hops:
            cross.along(s, cross_any).wait()
            cross.start_across(s)

    @pl.when(step == VISUAL_BLOCKS + 2)
    def _():
        for s in hops:
            first_in.along(s, in_mine).wait()
            first_in.start_across(s)

    @pl.when(step >= VISUAL_BLOCKS)
    def _():
        self_rows(r, step - VISUAL_BLOCKS)

    @pl.when(step == last)
    def _():
        for s in hops:
            cross.wait_across(s)
            first_in.wait_across(s)
            first_out.along(s, out_mine).wait()
        for one, mine in zip(text, text_mine):
            one.along(FAR, mine).wait()
        keep.wait()


def self_rows(r, at):
    span = NQ + TXT
    items = r.hidden.shape[0] // span
    lanes = QUAD * HEAD
    x = r.hidden[...]
    r.q[...] = (mm_nt(x, r.attn_v[0]).astype(NARROW).astype(WIDE) * SCALE).astype(NARROW)
    r.k[...] = mm_nt(x, r.attn_v[1]).astype(NARROW)
    r.v[...] = mm_nt(x, r.attn_v[2]).astype(NARROW)

    units = []
    for item in range(items):
        rows = slice(item * span, (item + 1) * span)
        allowed = allowed_pairs(r.lens, at * items + item, span, lanes)
        for quad in range(r.hidden.shape[1] // lanes):
            units.append((rows, slice(quad * lanes, (quad + 1) * lanes), allowed))
    scores = [mm_nt(r.k[u, c], spread_heads(r.q[u, c], QUAD)) for u, c, _ in units]
    lows = []
    for value, (u, c, allowed) in zip(scores, units):
        value = jnp.where(allowed, value, MASKED_SCORE)
        lifted = jnp.exp(value - jnp.max(value, axis=0, keepdims=True))
        lows.append((lifted * (1.0 / jnp.sum(lifted, axis=0, keepdims=True))).astype(NARROW))
        r.p[u, c] = lows[-1]
    parts = [mm_tn(low, r.v[u, c]) for low, (u, c, _) in zip(lows, units)]
    for part, (u, c, _) in zip(parts, units):
        r.ctx[u, c] = gather_heads(part, QUAD).astype(NARROW)

    residue = x.astype(WIDE) + mm(r.ctx[...], r.attn_v[3])
    r.res[...] = residue
    unit, _ = norm_parts(residue)
    first = unit * r.gain[0:1] + r.shift[0:1]
    for item in range(items):
        r.fq[item * NQ : (item + 1) * NQ] = first[item * span : item * span + NQ]
        r.ft[item * TXT : (item + 1) * TXT] = first[item * span + NQ : (item + 1) * span]


def first_layer(hidden, lens, visual, wkv, qkv, so, cq, co, gain, shift, ffn_in, ffn_out, shards):
    rows, width = hidden.shape
    span, items, depth = visual.shape
    cols = so.shape[0]
    tail = span % (16 * VISUAL_BLOCKS)
    visual_block = (span - tail) // VISUAL_BLOCKS
    block = min(rows, 256)
    copies = 6 * Spread.COPIES * (shards - 1)
    dma = pltpu.SemaphoreType.DMA
    hbm = pl.BlockSpec(memory_space=pl.ANY)

    def later(i):
        return jnp.maximum(i - VISUAL_BLOCKS, 0)

    def whole(shape):
        return pl.BlockSpec(shape, lambda i: (0,) * len(shape), pipeline_mode=pl.Buffered(1))

    def by_rows(count, dtype=NARROW):
        return pl.BlockSpec((count, width), lambda i: (later(i), 0))

    def low(*shape):
        return jax.ShapeDtypeStruct(shape, NARROW)

    def wide(*shape):
        return jax.ShapeDtypeStruct(shape, WIDE)

    ins = dict(
        lens=(lens, pl.BlockSpec(memory_space=pltpu.SMEM)),
        hidden=(hidden, by_rows(block)),
        visual=(
            visual,
            pl.BlockSpec((visual_block, items, depth), lambda i: (jnp.minimum(i, VISUAL_BLOCKS - 1), 0, 0)),
        ),
        visual_tail=(visual, pl.BlockSpec((tail, items, depth), lambda i: (span // tail - 1, 0, 0))),
        wkv=(wkv, whole(wkv.shape)), qkv=(qkv, whole(qkv.shape)), so=(so, whole(so.shape)),
        cq=(cq, whole(cq.shape)), co=(co, whole(co.shape)), gain=(gain, whole(gain.shape)), shift=(shift, whole(shift.shape)),
        ffn_in_first=(ffn_in, whole((1,) + ffn_in.shape[1:])), ffn_out_first=(ffn_out, whole((1,) + ffn_out.shape[1:])),
        ffn_in=(ffn_in, hbm), ffn_out=(ffn_out, hbm),
    )
    kv = (items, span, cols)
    outs = dict(
        cross_k=(low(*kv), whole(kv)), cross_v=(low(*kv), whole(kv)),
        q=(low(rows, width), by_rows(block)), k=(low(rows, width), by_rows(block)), v=(low(rows, width), by_rows(block)),
        p=(low(rows, width), by_rows(block)), ctx=(low(rows, width), by_rows(block)),
        res=(wide(rows, width), by_rows(block)),
        fq=(wide(rows // 2, width), by_rows(block // 2)), ft=(wide(rows // 2, width), by_rows(block // 2)),
        attn=(low(4, shards * cols, width), hbm),
        win=(low(shards, *ffn_in.shape[1:]), hbm), wout=(low(shards, *ffn_out.shape[1:]), hbm),
        cross=(low(shards, 2 * cols, width), hbm),
        tin=(low(*ffn_in.shape[1:]), hbm), tout=(low(*ffn_out.shape[1:]), hbm),
    )
    scratch = dict(
        attn_v=pltpu.VMEM((4, shards * cols, width), NARROW),
        w=pltpu.VMEM((2 * cols, depth), NARROW),
        y=pltpu.VMEM((2 * cols // 128, visual_block * items, 128), WIDE),
        send=dma((copies,)), recv=dma((copies,)), local=dma((9,)),
    )
    names = tuple(ins) + tuple(outs) + tuple(scratch)
    values = pl.pallas_call(
        functools.partial(first_kernel, names),
        grid=(VISUAL_BLOCKS + rows // block,),
        in_specs=[spec for _, spec in ins.values()],
        out_specs=[spec for _, spec in outs.values()],
        out_shape=[shape for shape, _ in outs.values()],
        scratch_shapes=list(scratch.values()),
        compiler_params=pltpu.CompilerParams(
            collective_id=0, has_side_effects=True, vmem_limit_bytes=VMEM_BYTES
        ),
        name="first_layer",
    )(*[value for value, _ in ins.values()])
    return types.SimpleNamespace(**dict(zip(outs, values)))


def self_backward_kernel(
    x_ref, w_ref, gain_ref, res_ref, gq_ref, gt_ref, q_ref, k_ref, v_ref, p_ref, ctx_ref,
    kv_ref, cross_ref, piece0_ref, piece1_ref, other_gain, other_shift,
    grad_ref, kv_out, cq_out, co_out, qkv_out, so_out, rows_out, feed_total,
    down, dctx, dq, dk, dv, acc, gain_sums, shift_sums, grads_ref, *rest,
):
    parts = cross_parts(kv_ref.shape, cross_ref.shape)
    (kv_total, cross_total), land, higher = rest[:2], rest[2:5], rest[5:8]
    send, recv, feed_send, feed_recv, local = rest[8:13]
    own_total, own_land, own_higher, (own_send, own_recv) = rest[13], rest[14:16], rest[16:18], rest[18:20]
    few, few_land, few_send, few_recv, few_in = rest[20:]
    later = PeerSum(feed_parts(x_ref.shape[1]), (), (feed_total,), (), (), feed_send, feed_recv)
    peers = PeerSum(parts, (kv_ref, cross_ref), (kv_total, cross_total), land, higher, send, recv)
    last = PeerSum(
        self_parts(grads_ref.shape), (grads_ref,), (own_total,), own_land, own_higher, own_send, own_recv
    )
    span = NQ + TXT
    block = res_ref.shape[0]
    items = block // span
    lanes = QUAD * HEAD
    placed = [
        pltpu.make_async_copy(ref, later.rows((feed_total,), part, later.final_piece(part), 1), local.at[n])
        for n, (ref, part) in enumerate(zip((piece0_ref, piece1_ref), later.parts))
    ]
    step = pl.program_id(0)

    @pl.when(step == 0)
    def _():
        for made in placed:
            made.start()
        greet(peers.targets())
        peers.start_halving(0)
        for made in placed:
            made.wait()
        later.start_gathering(0)

    @pl.when(step == 1)
    def _():
        peers.end_halving(0)
        peers.start_halving(1)
        later.end_gathering(0)
        later.start_gathering(1)

    @pl.when(step == 2)
    def _():
        peers.end_halving(1)
        peers.start_halving(2)

    @pl.when(step == 3)
    def _():
        peers.end_halving(2)
        peers.far()
        peers.start_gathering(0)

    unit, inverse = norm_parts(res_ref[...])
    pieces = []
    for item in range(items):
        pieces.append(gq_ref[item * NQ : (item + 1) * NQ])
        pieces.append(gt_ref[item * TXT : (item + 1) * TXT])
    cotangent = jnp.concatenate(pieces, axis=0)
    grad_res = norm_back(unit, inverse, gain_ref[0:1], cotangent)
    gain_sum, shift_sum = column_sums(unit, cotangent)

    @pl.when(step == 0)
    def _():
        gain_sums[...] = gain_sum
        shift_sums[...] = shift_sum

    @pl.when(step > 0)
    def _():
        gain_sums[...] += gain_sum
        shift_sums[...] += shift_sum

    grad_ref[...] = grad_res
    low = grad_res.astype(NARROW)
    down[...] = low
    dctx[...] = mm_nt(low, w_ref[3]).astype(NARROW)

    units = [
        (slice(item * span, (item + 1) * span), slice(quad * lanes, (quad + 1) * lanes))
        for item in range(items)
        for quad in range(w_ref.shape[2] // lanes)
    ]
    for at in range(0, len(units), UNITS):
        some = units[at : at + UNITS]
        spread = [spread_heads(dctx[u], QUAD) for u in some]
        grad_chances = [mm_nt(v_ref[u], one) for u, one in zip(some, spread)]
        scores = []
        for u, value in zip(some, grad_chances):
            weighted = p_ref[u].astype(WIDE)
            inner = jnp.sum(value * weighted, axis=0, keepdims=True)
            scores.append((weighted * (value - inner)).astype(NARROW))
        for u, one in zip(some, spread):
            dv[u] = mm(p_ref[u], one).astype(NARROW)
        for u, one in zip(some, scores):
            dk[u] = mm(one, spread_heads(q_ref[u], QUAD)).astype(NARROW)
        values = [mm_tn(one, k_ref[u]) for u, one in zip(some, scores)]
        for u, value in zip(some, values):
            dq[u] = (gather_heads(value, QUAD) * SCALE).astype(NARROW)

    grad_ref[...] += mm(dq[...], w_ref[0]) + mm(dk[...], w_ref[1]) + mm(dv[...], w_ref[2])

    own = lax.axis_index("tensor")
    cols = grads_ref.shape[0] // 4
    window = acc.shape[1]
    start = pl.multiple_of((own * cols) // 128 * 128, 128)
    here = pl.ds(start, window)
    x = x_ref[...]
    products = (
        mm_tn(dq[:, here], x), mm_tn(dk[:, here], x), mm_tn(dv[:, here], x),
        mm_tn(ctx_ref[:, here], down[...]),
    )

    @pl.when(step == 0)
    def _():
        for c, product in enumerate(products):
            acc[c] = product

    @pl.when(step > 0)
    def _():
        for c, product in enumerate(products):
            acc[c] += product

    @pl.when(step == pl.num_programs(0) - 1)
    def _():
        offset = pl.multiple_of(own * cols - start, 64)
        for c in range(4):
            grads_ref[c * cols : (c + 1) * cols] = acc[c, pl.ds(offset, cols), :].astype(NARROW)
        last.start_halving(0)
        few_in[0:1] = gain_sums[...]
        few_in[1:4] = other_gain[...]
        few_in[4:5] = shift_sums[...]
        few_in[5:8] = other_shift[...]
        few_steps = sum_rows(few_in, few, few_land, few_send, few_recv)
        few_steps[0]()
        peers.end_gathering(0)
        last.end_halving(0)
        last.start_halving(1)
        peers.start_gathering(1)
        few_steps[1]()
        later.end_gathering(1)
        later.start_gathering(2)
        last.end_halving(1)
        last.start_halving(2)
        for run in few_steps[2:]:
            run()
        rows_out[...] = few[few.shape[0] - 1]
        peers.end_gathering(1)
        peers.start_gathering(2)
        last.end_halving(2)
        last.far()
        last.start_gathering(0)
        peers.end_gathering(2)
        kv_out[0] = kv_total[:cols].astype(WIDE)
        kv_out[1, 128:] = kv_total[cols : 2 * cols - 128].astype(WIDE)
        kv_out[1, :128] = kv_total[2 * cols - 128 :].astype(WIDE)
        last.end_gathering(0)
        last.start_gathering(1)
        cq_out[...] = cross_total[:cols].astype(WIDE)
        co_out[...] = cross_total[cols:].astype(WIDE)
        last.end_gathering(1)
        last.start_gathering(2)
        later.end_gathering(2)
        last.end_gathering(2)
        for c in range(3):
            qkv_out[c] = own_total[c * cols : (c + 1) * cols].astype(WIDE)
        so_out[...] = own_total[3 * cols :].astype(WIDE)


def self_backward(
    hidden, weights, gain, residue, grad_q, grad_t, q, k, v, p, ctx, kv, cross, piece0, piece1, gains, shifts,
    cols, ident, peers
):
    rows, width = hidden.shape
    block = min(rows, 256)
    half = block // 2
    full = pl.BlockSpec((block, width), lambda i: (i, 0))
    halves = pl.BlockSpec((half, width), lambda i: (i, 0))
    parts = cross_parts(kv.shape, cross.shape)
    far = (peers // PEERS - 1).bit_length()
    depth = kv.shape[1]
    own = (4 * cols, width)
    steps = 3 + far
    hbm = pl.BlockSpec(memory_space=pl.ANY)
    dma = pltpu.SemaphoreType.DMA
    count = PeerSum.copies(feed_parts(width), far)

    def whole(shape):
        return pl.BlockSpec(shape, lambda i: (0,) * len(shape), pipeline_mode=pl.Buffered(1))

    def wide(*shape):
        return jax.ShapeDtypeStruct(shape, WIDE)

    totals = [
        wide(2, cols, depth), wide(cols, width), wide(cols, width), wide(3, cols, width), wide(cols, width), wide(8, width),
    ]
    return pl.pallas_call(
        self_backward_kernel,
        grid=(rows // block,),
        in_specs=[
            full,
            whole(weights.shape),
            pl.BlockSpec(gain.shape, lambda i: (0, 0)),
            full, halves, halves, full, full, full, full, full,
        ]
        + [whole(a.shape) for a in (kv, cross, piece0, piece1, gains, shifts)],
        out_specs=[full] + [whole(t.shape) for t in totals] + [hbm],
        out_shape=[wide(rows, width)] + totals + [jax.ShapeDtypeStruct((4 * width, width), NARROW)],
        scratch_shapes=[pltpu.VMEM((block, width), NARROW)] * 5
        + [pltpu.VMEM((4, (cols + 64 + 127) // 128 * 128, width), WIDE)]
        + [pltpu.VMEM((1, width), WIDE)] * 2
        + [pltpu.VMEM(own, NARROW)]
        + peer_scratch(parts, [kv.shape, cross.shape], far)
        + [dma((count,)), dma((count,)), dma((2,))]
        + peer_scratch(self_parts(own), [own], far)
        + [pltpu.VMEM((steps, 8, width), WIDE)] * 2
        + [dma((steps,)), dma((steps,)), pltpu.VMEM((8, width), WIDE)],
        compiler_params=pltpu.CompilerParams(
            collective_id=ident, has_side_effects=True, vmem_limit_bytes=VMEM_BYTES
        ),
        name="self_backward",
    )(hidden, weights, gain, residue, grad_q, grad_t, q, k, v, p, ctx, kv, cross, piece0, piece1, gains, shifts)


def feed_parts(width):
    rows = 4 * width
    return ((0, 0, rows // 2 // PIECES, 0, width, 0), (0, rows // 2, rows // 2 // PIECES, 0, width, 1))


LOADS = (
    "fq", "wq_own", "k", "v", "ft", "tin", "tout", "cotq", "tcot", "wo_own", "w_all", "tin2", "tout2",
)
STORES = ("outq", "outt", "gq", "gt", "grads", "kv", "piece0", "piece1")


def middle_kernel(names, *refs):
    r = types.SimpleNamespace(**dict(zip(names, refs)))
    cols = r.wq_own.shape[0]
    heads = cols // HEAD
    items, span = r.k.shape[:2]
    width = r.fq.shape[1]
    depth = r.visual.shape[2]
    chunks = r.win.shape[0]
    tensor = lax.axis_index("tensor")
    sources = dict(
        tin=r.ffn_in.at[1], tout=r.ffn_out.at[1],
        w_all=r.cross_o.at[:, pl.ds(cols, cols)], tin2=r.tin2_o, tout2=r.tout2_o,
        cotq=r.cot.at[:, pl.ds(0, NQ)], tcot=r.cot.at[:, pl.ds(NQ, TXT)],
    )
    rows = [slice(item * NQ, (item + 1) * NQ) for item in range(items)]
    tall = r.fq.shape

    def load(name, goal=None):
        return pltpu.make_async_copy(
            sources.get(name, getattr(r, name, None)),
            getattr(r, name + "_v") if goal is None else goal,
            r.load_sem.at[LOADS.index(name)],
        )

    def store(name, source):
        return pltpu.make_async_copy(source, getattr(r, name + "_o"), r.store_sem.at[STORES.index(name)])

    pair = (lax.axis_index("dp"), tensor + 1 - 2 * (tensor % 2))
    swaps = [remote(r.tpart.at[n], r.tland.at[n], r.swap_send.at[n], r.swap_recv.at[n], pair) for n in range(2)]
    forth = HeadGather(r.heads1, r.head_send1, r.head_recv1)
    gather = HeadGather(r.heads2, r.head_send2, r.head_recv2)
    base = Spread.COPIES * (chunks - 1)
    hops = range(1, chunks)
    first_in = Spread(eighth(r.win_o), r.spread_send, r.spread_recv, 0)
    first_out = Spread(eighth(r.wout_o), r.spread_send, r.spread_recv, base)
    cross = Spread(eighth(r.cross_o), r.spread_send, r.spread_recv, 2 * base)
    text = [
        Spread(one_shard(ref), r.spread_send, r.spread_recv, n * base) for n, ref in ((3, r.tin2_o), (4, r.tout2_o))
    ]
    parts = feed_parts(width)
    feed = [None]
    peers = PeerSum(
        parts, feed, (), r.land, r.higher, r.peer_send, r.peer_recv, pieces=(r.piece0, r.piece1)
    )
    early = ("tin_v", "tout_v", "tin2_v", "tout2_v", "tslope", "tslope2", "cotq_v", "tcot_v")

    def to_feed_forward(*buffers):
        for name, buffer in zip(early, buffers):
            setattr(r, name, buffer)
        for name in LOADS[:10]:
            load(name).start()
        greet(first_in.along_targets() + peers.targets())
        for s in hops:
            cross.start_onward(s, True)
        for s in hops:
            first_in.start_onward(s, True)
            first_out.start_across(s)
        for one in text:
            one.start_across(FAR)
        for name in ("fq", "wq_own", "k", "v"):
            load(name).wait()
        r.q[...] = (
            mm_nt(r.fq_v[...].astype(NARROW), r.wq_own_v[...]).astype(NARROW).astype(WIDE) * SCALE
        ).astype(NARROW)
        for half in range(2):
            some = range(half * items // 2, (half + 1) * items // 2)
            scores = [mm_nt(r.k_v[item], spread_heads(r.q[rows[item]], heads)) for item in some]
            lows = []
            for item, value in zip(some, scores):
                lifted = jnp.exp(value - jnp.max(value, axis=0, keepdims=True))
                lows.append((lifted * (1.0 / jnp.sum(lifted, axis=0, keepdims=True))).astype(NARROW))
                r.p[item] = lows[-1]
            values = [mm_tn(low, r.v_v[item]) for item, low in zip(some, lows)]
            for item, value in zip(some, values):
                r.ctx[rows[item]] = gather_heads(value, heads).astype(NARROW)
            count = items // 2 * NQ
            here = slice(half * count, (half + 1) * count)
            r.heads1[tensor, here] = r.ctx[here]
            forth.start(half)
        for s in hops:
            cross.start_last(s)

        def text_part(win, wout, slope_v, act_v):
            act, slope = gelu_parts(mm(r.ft_v[...].astype(NARROW), win[...]))
            slope_v[...] = slope.astype(NARROW)
            act = act.astype(NARROW)
            if act_v is not None:
                act_v[...] = act
            return mm(act, wout[...])

        for name in ("ft", "tin", "tout"):
            load(name).wait()
        r.gt_v[...] = text_part(r.tin_v, r.tout_v, r.tslope, r.tact)
        for s in hops:
            cross.finish(s, True)
        load("w_all").start()
        for one in text:
            one.start_onward(FAR)
        for s in hops:
            first_out.start_onward(s)
        for s in hops:
            first_in.start_last(s)
        for one in text:
            one.start_last(FAR)
        for one in text:
            one.finish(FAR)
        load("tin2").start()
        load("tout2").start()
        forth.wait(0)
        forth.wait(1)
        load("w_all").wait()
        r.gq_v[...] = forth.product(r.w_all_v)
        sources["w_all"] = r.cross_o.at[:, pl.ds(0, cols)]
        load("w_all").start()
        load("tin2").wait()
        load("tout2").wait()
        r.tpart[0] = (r.gt_v[...] + text_part(r.tin2_v, r.tout2_v, r.tslope2, None)).astype(NARROW)
        swaps[0].start()
        for s in hops:
            first_out.start_last(s)
        for s in hops:
            first_in.finish(s, True)

        def text_rows():
            load("tcot").wait()
            unit, inverse = norm_parts(r.ft_v[...] + r.tpart[0].astype(WIDE) + r.tland[0].astype(WIDE))
            r.outt[...] = (unit * r.gain[3:4] + r.shift[3:4]).astype(NARROW)
            store("outt", r.outt).start()
            cotangent = r.tcot_v[...].astype(WIDE).reshape(tall)
            gain_sum, shift_sum = column_sums(unit, cotangent)
            r.gains[2:3] = gain_sum
            r.shifts[2:3] = shift_sum
            grad = norm_back(unit, inverse, r.gain[3:4], cotangent)
            r.gt_v[...] = grad
            r.ttop[...] = grad.astype(NARROW)
            r.tdpre[...] = (mm_nt(r.ttop[...], r.tout_v[...]) * r.tslope[...].astype(WIDE)).astype(NARROW)
            far = (mm_nt(r.ttop[...], r.tout2_v[...]) * r.tslope2[...].astype(WIDE)).astype(NARROW)
            r.tpart[1] = (mm_nt(r.tdpre[...], r.tin_v[...]) + mm_nt(far, r.tin2_v[...])).astype(NARROW)
            swaps[1].start()

        def query_rows(slopes, total, weights, outq):
            def fetch(j):
                slot, chunk = j % 2, j % chunks
                return [
                    pltpu.make_async_copy(ref.at[chunk], weights.at[slot, n], r.weight_sem.at[slot, n])
                    for n, ref in enumerate((r.win_o, r.wout_o))
                ]

            unit, _ = norm_parts(r.fq_v[...] + r.gq_v[...])
            value = unit * r.gain[1:2] + r.shift[1:2]
            r.low[...] = value.astype(NARROW)
            total[...] = value
            for s in hops:
                first_out.finish(s)
            for made in fetch(0):
                made.start()

            def next_weights(j):
                for made in fetch(j):
                    made.wait()

                @pl.when(j + 1 < 2 * chunks)
                def _():
                    for made in fetch(j + 1):
                        made.start()

                return weights.at[j % 2, 0], weights.at[j % 2, 1]

            @pl.loop(0, chunks)
            def _(j):
                win, wout = next_weights(j)
                act, slope = gelu_parts(mm(r.low[...], win[...]))
                slopes[j] = slope.astype(NARROW)
                act = act.astype(NARROW)
                total[...] += mm(act, wout[...])

                @pl.when(j == tensor)
                def _():
                    r.act[...] = act


            unit, inverse = norm_parts(total[...])
            outq[...] = (unit * r.gain[2:3] + r.shift[2:3]).astype(NARROW)
            store("outq", outq).start()
            load("cotq").wait()
            cotangent = r.cotq_v[...].astype(WIDE).reshape(tall)
            gain_sum, shift_sum = column_sums(unit, cotangent)
            r.gains[1:2] = gain_sum
            r.shifts[1:2] = shift_sum
            grad = norm_back(unit, inverse, r.gain[2:3], cotangent)
            total[...] = grad
            r.top[...] = grad.astype(NARROW)

            @pl.loop(chunks, 2 * chunks)
            def _(j):
                win, wout = next_weights(j)
                chunk = j - chunks
                dpre = (mm_nt(r.top[...], wout[...]) * slopes[chunk].astype(WIDE)).astype(NARROW)
                total[...] += mm_nt(dpre, win[...])

                @pl.when(chunk == tensor)
                def _():
                    r.dpre[...] = dpre

                @pl.when(chunk == 2)
                def _():
                    swaps[0].wait()
                    text_rows()


            grad_second = total[...]
            unit, inverse = norm_parts(r.fq_v[...] + r.gq_v[...])
            gain_sum, shift_sum = column_sums(unit, grad_second)
            r.gains[0:1] = gain_sum
            r.shifts[0:1] = shift_sum
            grad = norm_back(unit, inverse, r.gain[1:2], grad_second)
            r.gq_v[...] = grad
            r.down[...] = grad.astype(NARROW)
            store("outq", outq).wait()

        pl.run_scoped(
            query_rows,
            pltpu.VMEM((chunks, tall[0], r.win.shape[2]), NARROW),
            pltpu.VMEM(tall, WIDE),
            pltpu.VMEM((2, 2) + r.win.shape[1:], NARROW),
            pltpu.VMEM(tall, NARROW),
        )

    inner, outer = r.ffn_in.shape[1:], r.ffn_out.shape[1:]
    pl.run_scoped(
        to_feed_forward,
        *[pltpu.VMEM(shape, NARROW) for shape in (inner, outer, inner, outer, (tall[0], inner[1]), (tall[0], inner[1]), (items, NQ, width), (items, TXT, width))],
    )

    def feed_gradients(goal):
        feed[0] = goal
        goal[:width] = mm_tn(r.low[...], r.dpre[...]).astype(NARROW)
        goal[width : 2 * width] = mm_tn(r.ft_v[...].astype(NARROW), r.tdpre[...]).astype(NARROW)
        goal[2 * width : 3 * width] = mm_tn(r.act[...], r.top[...]).astype(NARROW)
        goal[3 * width :] = mm_tn(r.tact[...], r.ttop[...]).astype(NARROW)
        peers.start_halving(0)

    def cross_rows(dctx, dq, score, dkv, acc, x, x_tail, kv, feed_v):
        group = items // 4
        steps = VISUAL_STEPS
        tail = span % steps
        block = (span - tail) // steps

        def fetch(j):
            return pltpu.make_async_copy(r.visual.at[pl.ds(j * block, block)], x.at[j % 2], r.x_sem.at[j % 2])

        rest = pltpu.make_async_copy(r.visual.at[pl.ds(span - tail, tail)], x_tail, r.x_sem.at[2])
        fetch(0).start()
        rest.start()
        load("wo_own").wait()
        dctx[...] = mm_nt(r.down[...], r.wo_own_v[...]).astype(NARROW)
        for g in range(4):
            some = range(g * group, (g + 1) * group)
            spread = [spread_heads(dctx[rows[item]], heads) for item in some]
            grad_chances = [mm_nt(r.v_v[item], one) for item, one in zip(some, spread)]
            scores = []
            for item, value in zip(some, grad_chances):
                weighted = r.p[item].astype(WIDE)
                inner = jnp.sum(value * weighted, axis=0, keepdims=True)
                scores.append((weighted * (value - inner)).astype(NARROW))
                score[item] = scores[-1]
            values = [mm_tn(one, r.k_v[item]) for item, one in zip(some, scores)]
            for item, value in zip(some, values):
                dq[rows[item]] = (gather_heads(value, heads) * SCALE).astype(NARROW)
            if g % 2:
                count = 2 * group * NQ
                here = slice(g // 2 * count, (g // 2 + 1) * count)
                r.heads2[tensor, here] = dq[here]
                gather.start(g // 2)
        feed_gradients(feed_v)
        none = jnp.zeros((QUAD * NQ, cols), NARROW)
        for g in range(4):
            some = range(g * group, (g + 1) * group)
            both = []
            for item in some:
                one = spread_heads(dctx[rows[item]], heads)
                both.append(
                    mm(
                        jnp.concatenate([score[item], r.p[item]], axis=1),
                        jnp.concatenate(
                            [
                                jnp.concatenate([spread_heads(r.q[rows[item]], heads), none], axis=1),
                                jnp.concatenate([none, one[:, 128:], one[:, :128]], axis=1),
                            ],
                            axis=0,
                        ),
                    )
                )
            for item, value in zip(some, both):
                for tile in range(dkv.shape[0]):
                    dkv[tile, pl.ds(item, span, stride=items)] = value[:, tile * 128 : (tile + 1) * 128]
            if g == 2:
                peers.end_halving(0)
                peers.start_halving(1)
        r.grads[:cols] = mm_tn(dq[...], r.fq_v[...].astype(NARROW)).astype(NARROW)
        r.grads[cols:] = mm_tn(r.ctx[...], r.down[...]).astype(NARROW)
        store("grads", r.grads).start()

        def product(first, count, value):
            grads = [dkv[tile, pl.ds(first, count)].astype(NARROW) for tile in range(dkv.shape[0])]
            return mm_tn(jnp.concatenate(grads, axis=1), value.reshape(count, depth))

        rest.wait()
        acc[...] = product((span - tail) * items, tail * items, x_tail[...])

        @pl.loop(0, steps)
        def _(j):
            fetch(j).wait()

            @pl.when(j + 1 < steps)
            def _():
                fetch(j + 1).start()

            acc[...] += product(pl.multiple_of(j * block * items, 16), block * items, x[j % 2])

            @pl.when(j == 11)
            def _():
                peers.end_halving(1)
                peers.start_halving(2)

        kv[...] = acc[...].astype(kv.dtype)
        store("kv", kv).start()
        gather.wait(0)
        gather.wait(1)
        load("w_all").wait()
        r.gq_v[...] += gather.product(r.w_all_v)
        store("gq", r.gq_v).start()
        swaps[1].wait()
        r.gt_v[...] += r.tpart[1].astype(WIDE) + r.tland[1].astype(WIDE)
        store("gt", r.gt_v).start()
        peers.end_halving(2)
        peers.far()
        store("piece0", r.piece0).start()
        store("piece1", r.piece1).start()
        store("kv", kv).wait()

    pl.run_scoped(
        cross_rows,
        pltpu.VMEM((tall[0], cols), NARROW),
        pltpu.VMEM((tall[0], cols), NARROW),
        pltpu.VMEM((items, span, QUAD * NQ), NARROW),
        pltpu.VMEM((2 * cols // 128, items * span, 128), WIDE),
        pltpu.VMEM((2 * cols, depth), WIDE),
        pltpu.VMEM((2, span // VISUAL_STEPS, items, depth), NARROW),
        pltpu.VMEM((span % VISUAL_STEPS, items, depth), NARROW),
        pltpu.VMEM((2 * cols, depth), NARROW),
        pltpu.VMEM((4 * width, width), NARROW),
    )
    for name, source in (
        ("outt", r.outt), ("gq", r.gq_v), ("gt", r.gt_v), ("grads", r.grads), ("piece0", r.piece0), ("piece1", r.piece1),
    ):
        store(name, source).wait()


def middle(arrays, ident, peers):
    rows, width = arrays["fq"].shape
    cols = arrays["wq_own"].shape[0]
    items, span = arrays["k"].shape[:2]
    hidden = arrays["ffn_in"].shape[2]
    depth = arrays["visual"].shape[2]
    shards = arrays["win"].shape[0]
    far = (peers // PEERS - 1).bit_length()
    parts = feed_parts(width)
    piece = (parts[0][2], width)
    dma = pltpu.SemaphoreType.DMA
    hbm, vmem = pl.BlockSpec(memory_space=pl.ANY), pl.BlockSpec(memory_space=pltpu.VMEM)

    def low(*dims):
        return pltpu.VMEM(dims, NARROW)

    def wide(*dims):
        return pltpu.VMEM(dims, WIDE)

    out = jax.ShapeDtypeStruct
    outs = dict(
        outq_o=out((rows, width), NARROW), outt_o=out((rows, width), NARROW),
        gq_o=out((rows, width), WIDE), gt_o=out((rows, width), WIDE),
        grads_o=out((2 * cols, width), NARROW), kv_o=out((2 * cols, depth), NARROW),
        piece0_o=out(piece, NARROW), piece1_o=out(piece, NARROW),
        gains=out((3, width), WIDE), shifts=out((3, width), WIDE),
        win_o=out(arrays["win"].shape, NARROW), wout_o=out(arrays["wout"].shape, NARROW),
        cross_o=out(arrays["cross_w"].shape, NARROW),
        tin2_o=out(arrays["tin2"].shape, NARROW), tout2_o=out(arrays["tout2"].shape, NARROW),
    )
    copies = feed_copies(shards)
    total = peer_scratch(parts, [], far)
    scratch = dict(
        fq_v=wide(rows, width), wq_own_v=low(cols, width), wo_own_v=low(cols, width),
        k_v=low(*arrays["k"].shape), v_v=low(*arrays["v"].shape), ft_v=wide(rows, width),
        w_all_v=low(shards, cols, width),
        q=low(rows, cols), ctx=low(rows, cols), p=low(items, span, QUAD * NQ),
        tact=low(rows, hidden),
        low=low(rows, width), top=low(rows, width), down=low(rows, width),
        act=low(rows, hidden), dpre=low(rows, hidden),
        ttop=low(rows, width), tdpre=low(rows, hidden), outt=low(rows, width),
        gq_v=wide(rows, width), gt_v=wide(rows, width), grads=low(2 * cols, width),
        tpart=low(2, rows, width), tland=low(2, rows, width), swap_send=dma((2,)), swap_recv=dma((2,)),
        heads1=low(shards, rows, cols), head_send1=dma((2, shards)), head_recv1=dma((2, shards)),
        heads2=low(shards, rows, cols), head_send2=dma((2, shards)), head_recv2=dma((2, shards)),
        spread_send=dma((copies,)), spread_recv=dma((copies,)),
        piece0=low(*piece), piece1=low(*piece),
        land=total[:2], higher=total[2:4], peer_send=total[4], peer_recv=total[5],
        load_sem=dma((len(LOADS),)), store_sem=dma((len(STORES),)), weight_sem=dma((2, 2)), x_sem=dma((3,)),
    )
    names = tuple(arrays) + tuple(outs) + tuple(scratch)
    return dict(
        zip(
            outs,
            pl.pallas_call(
                functools.partial(middle_kernel, names),
                in_specs=[vmem if name in ("gain", "shift") else hbm for name in arrays],
                out_specs=[vmem if name in ("gains", "shifts") else hbm for name in outs],
                out_shape=list(outs.values()),
                input_output_aliases={
                    list(arrays).index(a): list(outs).index(b)
                    for a, b in (
                        ("win", "win_o"), ("wout", "wout_o"), ("cross_w", "cross_o"), ("tin2", "tin2_o"), ("tout2", "tout2_o"),
                    )
                },
                scratch_shapes=list(scratch.values()),
                compiler_params=pltpu.CompilerParams(
                    collective_id=ident, has_side_effects=True, vmem_limit_bytes=62 * 2**20
                ),
                name="middle",
            )(*arrays.values()),
        )
    )


def on_device(
    hidden_in,
    visual_feats,
    caption_lengths,
    self_qkv,
    self_out,
    cross_query,
    cross_kv,
    cross_out,
    ffn_in,
    ffn_out,
    norm_gain,
    norm_shift,
    out_grad,
):
    items = visual_feats.shape[0]
    rows, width = hidden_in.shape
    span = rows // items
    cols = self_qkv.shape[2]
    shards = lax.axis_size("tensor")

    visual = jnp.swapaxes(visual_feats, 0, 1)
    cross_wq = jnp.swapaxes(cross_query, 0, 1)
    first = first_layer(
        hidden_in, jnp.swapaxes(caption_lengths, 0, 1), visual, jnp.swapaxes(cross_kv, 1, 2), jnp.swapaxes(self_qkv, 1, 2),
        self_out, cross_wq, cross_out, norm_gain, norm_shift, ffn_in, ffn_out, shards,
    )
    peers = lax.axis_size("dp")
    mid = middle(
        dict(
            fq=first.fq, wq_own=cross_wq, k=first.cross_k, v=first.cross_v, ft=first.ft,
            cot=out_grad.reshape(items, span, width), wo_own=cross_out, ffn_in=ffn_in, ffn_out=ffn_out, win=first.win,
            wout=first.wout, cross_w=first.cross, tin2=first.tin, tout2=first.tout, visual=visual,
            gain=norm_gain, shift=norm_shift,
        ),
        2, peers,
    )
    out_q, out_t, g_cross, g_kv = mid["outq_o"], mid["outt_o"], mid["grads_o"], mid["kv_o"]
    grad_hidden, g_kv, g_cq, g_co, g_qkv, g_so, gains, g_feed = self_backward(
        hidden_in, first.attn, norm_gain, first.res, mid["gq_o"], mid["gt_o"], first.q, first.k, first.v, first.p, first.ctx,
        g_kv, g_cross,
        mid["piece0_o"], mid["piece1_o"], mid["gains"], mid["shifts"], cols, 6, peers,
    )
    g_feed = g_feed.reshape(2, 2, width, width).astype(WIDE)
    g_in, g_out = g_feed[0], g_feed[1]
    out = jnp.concatenate(
        [out_q.reshape(items, NQ, width), out_t.reshape(items, TXT, width)], axis=1
    ).reshape(rows, width)
    return (
        out,
        grad_hidden,
        jnp.swapaxes(g_qkv, 1, 2),
        g_so,
        jnp.swapaxes(g_cq, 0, 1),
        jnp.swapaxes(g_kv, 1, 2),
        g_co,
        g_in,
        g_out,
        gains[:4],
        gains[4:],
    )


def solution(mesh):
    placed = (
        P("dp", None),
        P("dp", None, None),
        P("dp", None),
        P(None, None, "tensor"),
        P("tensor", None),
        P(None, "tensor"),
        P(None, None, "tensor"),
        P("tensor", None),
        P(None, None, "tensor"),
        P(None, "tensor", None),
        P(),
        P(),
        P("dp", None),
    )
    return jax.shard_map(
        on_device,
        mesh=mesh,
        in_specs=placed,
        out_specs=(
            P("dp", None),
            P("dp", None),
            P(None, None, "tensor"),
            P("tensor", None),
            P(None, "tensor"),
            P(None, None, "tensor"),
            P("tensor", None),
            P(None, None, "tensor"),
            P(None, "tensor", None),
            P(),
            P(),
        ),
        check_vma=False,
    )
```

```python
import functools
import math
import types

import jax
import jax.numpy as jnp
from jax import lax
from jax.experimental import pallas as pl
from jax.experimental.pallas import tpu as pltpu
from jax.sharding import PartitionSpec as P

HEAD = 64
NQ = 32
TXT = 32
QUAD = 4
UNITS = 12
VISUAL_STEPS = 16
EPSILON = 1e-06
MASKED_SCORE = -1e30
SCALE = 1.0 / math.sqrt(HEAD)
WIDE = jnp.float32
NARROW = jnp.bfloat16
VMEM_BYTES = 60 * 2**20


def mm(a, b):
    return lax.dot_general(a, b, (((1,), (0,)), ((), ())), preferred_element_type=WIDE)


def mm_nt(a, b):
    return lax.dot_general(a, b, (((1,), (1,)), ((), ())), preferred_element_type=WIDE)


def mm_tn(a, b):
    return lax.dot_general(a, b, (((0,), (0,)), ((), ())), preferred_element_type=WIDE)


def lane_group(rows, lanes, size):
    return lax.broadcasted_iota(jnp.int32, (rows, lanes), 1) // size


def spread_heads(block, count):
    group = lane_group(1, block.shape[1], HEAD)
    return jnp.concatenate(
        [block * jnp.where(group == h, 1.0, 0.0).astype(NARROW) for h in range(QUAD)], axis=0
    )


def gather_heads(block, count):
    rows, lanes = block.shape[0] // QUAD, block.shape[1]
    group = lane_group(rows, lanes, HEAD)
    out = block[:rows]
    for h in range(1, count):
        out = jnp.where(group == h, block[h * rows : (h + 1) * rows], out)
    return out


def norm_parts(residue):
    mean = jnp.mean(residue, axis=-1, keepdims=True)
    centered = residue - mean
    variance = jnp.mean(centered * centered, axis=-1, keepdims=True)
    inverse = lax.rsqrt(variance + EPSILON)
    return centered * inverse, inverse


def norm_back(unit, inverse, gain_row, cotangent):
    scaled = gain_row * cotangent
    first = jnp.mean(scaled, axis=-1, keepdims=True)
    second = jnp.mean(scaled * unit, axis=-1, keepdims=True)
    return inverse * (scaled - first - unit * second)


def column_sums(unit, cotangent):
    return (
        jnp.sum(cotangent * unit, axis=0, keepdims=True),
        jnp.sum(cotangent, axis=0, keepdims=True),
    )


def gelu_parts(pre):
    bell = jnp.exp(-0.5 * pre * pre)
    half = 0.5 * lax.erf(pre * math.sqrt(0.5)) + 0.5
    return pre * half, half + pre * bell * (1.0 / math.sqrt(2.0 * math.pi))


MESH = pl.DeviceIdType.MESH
PEERS = 8


def flip(index, bit):
    return index + bit - 2 * bit * ((index // bit) % 2)


def greet(targets):
    barrier = pltpu.get_barrier_semaphore()
    for target in targets:
        pl.semaphore_signal(barrier, inc=1, device_id=target, device_id_type=MESH)
    pl.semaphore_wait(barrier, len(targets))


def remote(src, dst, send, recv, target):
    return pltpu.make_async_remote_copy(
        src_ref=src, dst_ref=dst, send_sem=send, recv_sem=recv, device_id=target, device_id_type=MESH
    )


class Spread:
    COPIES = 9

    def __init__(self, at, send, recv, base):
        self.at, self.send, self.recv, self.base = at, send, recv, base
        self.dp, self.tensor = lax.axis_index("dp"), lax.axis_index("tensor")
        self.shards = lax.axis_size("tensor")
        self.peer = self.dp % PEERS

    def hop(self, slot, s, src, dst, target):
        index = self.base + (s - 1) * self.COPIES + slot
        return remote(src, dst, self.send.at[index], self.recv.at[index], target)

    def came(self, s):
        return (self.tensor + self.shards - s) % self.shards

    def along(self, s, own):
        return self.hop(0, s, own, self.at(self.tensor, self.peer, None), (self.dp, (self.tensor + s) % self.shards))

    def hand(self, slot, s, bit, peer, half):
        place = self.at(self.came(s), peer, half)
        return self.hop(slot, s, place, place, (flip(self.dp, bit), self.tensor))

    def across(self, s):
        return [self.hand(1, s, 2, self.peer, None), self.hand(2, s, 4, self.peer, None), self.hand(3, s, 1, self.peer, None)]

    def onward(self, s):
        x, y = flip(self.peer, 2), flip(self.peer, 4)
        return (
            [self.hand(4, s, 4, x, 0), self.hand(5, s, 1, x, None)],
            [self.hand(6, s, 2, y, 1), self.hand(7, s, 1, y, None)],
        )

    def last(self, s):
        return self.hand(8, s, 1, flip(flip(self.peer, 2), 4), None)

    def start_across(self, s):
        for made in self.across(s):
            made.start()

    def wait_across(self, s):
        for made in self.across(s):
            made.wait()

    def start_onward(self, s, arrived=False):
        over_x, over_y, _ = self.across(s)
        by_x, by_y = self.onward(s)
        if not arrived:
            over_x.wait_recv()
        for made in by_x:
            made.start()
        if not arrived:
            over_y.wait_recv()
        for made in by_y:
            made.start()

    def start_last(self, s):
        by_x, by_y = self.onward(s)
        by_x[0].wait_recv()
        by_y[0].wait_recv()
        self.last(s).start()

    def finish(self, s, arrived=False):
        over = self.across(s)
        by_x, by_y = self.onward(s)
        final = self.last(s)
        for made in ([] if arrived else [over[2]]) + [by_x[1], by_y[1], final]:
            made.wait_recv()
        for made in ([] if arrived else over) + by_x + by_y + [final]:
            made.wait_send()

    def targets(self):
        return self.along_targets() + self.peer_targets()

    def along_targets(self):
        return [(self.dp, (self.tensor + s) % self.shards) for s in range(1, self.shards)]

    def peer_targets(self):
        return [(flip(self.dp, bit), self.tensor) for bit in (2, 4, 1)]


FAR = 2


def one_shard(ref):
    rows = ref.shape[0] // PEERS

    def at(shard, peer, half):
        return ref.at[half_rows(peer * rows, rows, half)]

    return at


def half_rows(first, rows, half):
    split = (rows // 2 + 15) // 16 * 16
    start, count = {None: (0, rows), 0: (0, split), 1: (split, rows - split)}[half]
    return pl.ds(pl.multiple_of(first + start, 16), count)


def eighth(ref):
    rows = ref.shape[1] // PEERS

    def at(shard, peer, half):
        return ref.at[shard, half_rows(peer * rows, rows, half)]

    return at


class HeadGather:
    def __init__(self, buffer, send, recv):
        self.buffer, self.send, self.recv = buffer, send, recv
        self.dp, self.tensor = lax.axis_index("dp"), lax.axis_index("tensor")
        self.shards = lax.axis_size("tensor")

    def copies(self, half):
        count = self.buffer.shape[1] // 2
        place = self.buffer.at[self.tensor, pl.ds(half * count, count)]
        return [
            remote(place, place, self.send.at[half, s], self.recv.at[half, s], (self.dp, (self.tensor + s) % self.shards))
            for s in range(1, self.shards)
        ]

    def start(self, half):
        for made in self.copies(half):
            made.start()

    def wait(self, half):
        for made in self.copies(half):
            made.wait()

    def product(self, weights):
        total = mm(self.buffer[0], weights[0])
        for shard in range(1, self.shards):
            total += mm(self.buffer[shard], weights[shard])
        return total


PIECES = 8


class PeerSum:
    def __init__(self, parts, source, total, land, higher, send, recv, base=0, pieces=None):
        self.parts, self.source, self.total, self.land, self.higher = parts, source, total, land, higher
        self.pieces = pieces
        self.send, self.recv, self.base = send, recv, base
        self.dp, self.tensor = lax.axis_index("dp"), lax.axis_index("tensor")
        self.bits = [(self.dp // b) % 2 for b in (1, 2, 4)]

    @staticmethod
    def far_bits():
        return [PEERS << k for k in range((lax.axis_size("dp") // PEERS - 1).bit_length())]

    @staticmethod
    def copies(parts, far):
        return len(parts) * (6 + far)

    def way(self, part):
        order = ((2, self.bits[1]), (4, self.bits[2]))
        return order if part[5] == 0 else order[::-1]

    def rows(self, refs, part, piece, count):
        array, first, size, column, columns, _ = part
        start = pl.multiple_of(first + piece * size, 16)
        return refs[array].at[pl.ds(start, count * size), pl.ds(column, columns)]

    def hop(self, n, stage, src, dst, bit):
        index = self.base + n * (6 + len(self.far_bits())) + stage
        return remote(src, dst, self.send.at[index], self.recv.at[index], (flip(self.dp, bit), self.tensor))

    def landed(self, n, piece, count):
        size = self.parts[n][2]
        return self.land[n].at[pl.ds(pl.multiple_of(piece * size, 16), count * size)]

    def halving(self, n, stage):
        part = self.parts[n]
        core = self.bits[0]
        (bit_1, own_1), (bit_2, own_2) = self.way(part)
        if stage == 0:
            bit, place = 1, self.landed(n, 0, 4)
            out = self.rows(self.source, part, (1 - core) * 4, 4)
            kept = self.rows(self.source, part, core * 4, 4)
        elif stage == 1:
            bit, place = bit_1, self.landed(n, 4, 2)
            out, kept = self.landed(n, (1 - own_1) * 2, 2), self.landed(n, own_1 * 2, 2)
        else:
            bit, place = bit_2, self.landed(n, 6, 1)
            out, kept = self.landed(n, 4 + 1 - own_2, 1), self.landed(n, 4 + own_2, 1)
        goal = self.final_place(n) if stage == 2 else place
        return self.hop(n, stage, out, place, bit), kept, place, goal

    def final_place(self, n):
        if self.pieces is not None:
            return self.pieces[n]
        return self.rows(self.total, self.parts[n], self.final_piece(self.parts[n]), 1)

    def final_piece(self, part):
        (_, own_1), (_, own_2) = self.way(part)
        return self.bits[0] * 4 + own_1 * 2 + own_2

    def gathering(self, n, stage):
        part = self.parts[n]
        core = self.bits[0]
        (bit_1, own_1), (bit_2, _) = self.way(part)
        piece, count, bit = (
            (self.final_piece(part), 1, bit_2), (core * 4 + own_1 * 2, 2, bit_1), (core * 4, 4, 1),
        )[stage]
        place = self.rows(self.total, part, piece, count)
        return self.hop(n, 3 + stage, place, place, bit)

    def targets(self):
        return [(flip(self.dp, bit), self.tensor) for bit in [1, 2, 4] + self.far_bits()]

    def start_halving(self, stage):
        for n in range(len(self.parts)):
            self.halving(n, stage)[0].start()

    def end_halving(self, stage):
        for n in range(len(self.parts)):
            made, kept, place, goal = self.halving(n, stage)
            made.wait_recv()
            goal[...] = (kept[...].astype(WIDE) + place[...].astype(WIDE)).astype(goal.dtype)
        for n in range(len(self.parts)):
            self.halving(n, stage)[0].wait_send()

    def far(self):
        for k, bit in enumerate(self.far_bits()):
            for n in range(len(self.parts)):
                place = self.final_place(n)
                made = self.hop(n, 6 + k, place, self.higher[n].at[k], bit)
                made.start()
                made.wait()
                place[...] = (place[...].astype(WIDE) + self.higher[n][k].astype(WIDE)).astype(place.dtype)

    def start_gathering(self, stage):
        for n in range(len(self.parts)):
            self.gathering(n, stage).start()

    def end_gathering(self, stage):
        for n in range(len(self.parts)):
            self.gathering(n, stage).wait()


def peer_scratch(parts, shapes, far):
    dma = pltpu.SemaphoreType.DMA
    count = PeerSum.copies(parts, far)
    land = [pltpu.VMEM((7 * p[2], p[4]), NARROW) for p in parts]
    higher = [pltpu.VMEM((far, p[2], p[4]) if far else (1, 16, 128), NARROW) for p in parts]
    return [pltpu.VMEM(shape, NARROW) for shape in shapes] + land + higher + [dma((count,)), dma((count,))]


def sum_rows(values, out, land, send, recv):
    dp, tensor = lax.axis_index("dp"), lax.axis_index("tensor")
    bits = [1, 2, 4] + PeerSum.far_bits()

    def hop(k):
        source = values if k == 0 else out.at[k - 1]
        return remote(source, land.at[k], send.at[k], recv.at[k], (flip(dp, bits[k]), tensor))

    def run(k):
        if k > 0:
            hop(k - 1).wait()
            out[k - 1] = (values if k == 1 else out.at[k - 2])[...] + land[k - 1]
        if k < len(bits):
            hop(k).start()

    return [functools.partial(run, k) for k in range(len(bits) + 1)]


def cross_parts(kv, cross):
    width = cross[1]
    return (
        (0, 0, kv[0] // PIECES, 0, width, 0),
        (0, 0, kv[0] // PIECES, width, kv[1] - width, 1),
        (1, 0, cross[0] // PIECES, 0, width, 0),
    )


def self_parts(own):
    third, width = own[0] // 3, own[1]
    return ((0, 0, third // PIECES, 0, width, 0), (0, third, 2 * third // PIECES, 0, width, 1))


def feed_copies(shards):
    return 5 * Spread.COPIES * (shards - 1)


def labels_of(position, ends):
    place = position - NQ
    label = jnp.zeros_like(position)
    for end in ends:
        label = label + jnp.where(place >= end, 1, 0)
    return jnp.where(position < NQ, -1, label)


def allowed_pairs(lens_ref, item, span, lanes):
    ends = []
    total = jnp.int32(0)
    for c in range(lens_ref.shape[0]):
        total = total + lens_ref[c, item]
        ends.append(total)
    key_label = labels_of(lax.broadcasted_iota(jnp.int32, (span, lanes), 0), ends)
    query_label = labels_of(lax.broadcasted_iota(jnp.int32, (span, lanes), 1) % span, ends)
    return (key_label == query_label) | (key_label == -1)


VISUAL_BLOCKS = 4


def first_kernel(names, *refs):
    r = types.SimpleNamespace(**dict(zip(names, refs)))
    step = pl.program_id(0)
    last = pl.num_programs(0) - 1
    block, items, depth = r.visual.shape
    cols = r.so.shape[0]
    per = PEERS // 4
    rows = cols // per
    base = Spread.COPIES * (lax.axis_size("tensor") - 1)

    def at(shard, peer, half):
        return r.attn_v.at[peer // per, half_rows(shard * cols + (peer % per) * rows, rows, half)]

    def spread_to(where, n):
        return Spread(where, r.send, r.recv, n * base)

    attn = spread_to(at, 0)
    first_in, first_out, cross = (spread_to(eighth(ref), n + 1) for n, ref in enumerate((r.win, r.wout, r.cross)))
    text = [spread_to(one_shard(ref), n + 4) for n, ref in enumerate((r.tin, r.tout))]
    peer, tensor = attn.peer, attn.tensor
    hops = range(1, attn.shards)
    few = 2 * cols // PEERS

    def eighth_of(ref, first, count):
        return ref.at[pl.ds(pl.multiple_of(first, 16), count)]

    def start_attn(s):
        @pl.when(peer < 3 * per)
        def _():
            attn.along(s, eighth_of(r.qkv.at[peer // per], (peer % per) * rows, rows)).start()

        @pl.when(peer >= 3 * per)
        def _():
            attn.along(s, eighth_of(r.so, (peer - 3 * per) * rows, rows)).start()

    def start_cross(s):
        @pl.when(peer < PEERS // 2)
        def _():
            cross.along(s, eighth_of(r.cq, peer * few, few)).start()

        @pl.when(peer >= PEERS // 2)
        def _():
            cross.along(s, eighth_of(r.co, (peer - PEERS // 2) * few, few)).start()

    attn_any, cross_any = r.so.at[pl.ds(0, rows)], r.co.at[pl.ds(0, few)]
    in_mine, out_mine = (eighth(ref)(0, peer, None) for ref in (r.ffn_in_first, r.ffn_out_first))
    text_mine = [eighth(ref)(1, peer, None) for ref in (r.ffn_in, r.ffn_out)]
    here = pl.ds(pl.multiple_of(tensor * cols, 16), cols)
    own_copies = [
        pltpu.make_async_copy(source, goal, r.local.at[n])
        for n, (source, goal) in enumerate(
            [(r.qkv.at[c], r.attn_v.at[c, here]) for c in range(3)]
            + [
                (r.so, r.attn_v.at[3, here]),
                (r.cq, r.cross.at[tensor, pl.ds(0, cols)]),
                (r.co, r.cross.at[tensor, pl.ds(cols, cols)]),
                (r.ffn_in_first.at[0], r.win.at[tensor]),
                (r.ffn_out_first.at[0], r.wout.at[tensor]),
            ]
        )
    ]
    keep = pltpu.make_async_copy(r.attn_v, r.attn, r.local.at[len(own_copies)])

    @pl.when(step == 0)
    def _():
        greet(attn.targets())
        for s in hops:
            start_attn(s)
        for made in own_copies:
            made.start()
        low = 128
        r.w[:cols] = r.wkv[0]
        r.w[cols : 2 * cols - low] = r.wkv[1, low:]
        r.w[2 * cols - low :] = r.wkv[1, :low]

    def project(x, first, count):
        y = mm_nt(x, r.w[...])
        for tile in range(r.y.shape[0]):
            r.y[tile, : count * items] = y[:, tile * 128 : (tile + 1) * 128]
        for item in range(items):
            k_low, high, v_low = [
                r.y[tile, pl.ds(item, count, stride=items)].astype(NARROW) for tile in range(3)
            ]
            r.cross_k[item, first, :128] = k_low
            r.cross_k[item, first, 128:] = high[:, : cols - 128]
            r.cross_v[item, first, :128] = v_low
            r.cross_v[item, first, 128:] = high[:, cols - 128 :]

    @pl.when(step < VISUAL_BLOCKS)
    def _():
        project(
            r.visual[...].reshape(block * items, depth),
            pl.ds(pl.multiple_of(step * block, block), block),
            block,
        )

    @pl.when(step == VISUAL_BLOCKS - 1)
    def _():
        count = r.visual_tail.shape[0]
        project(
            r.visual_tail[...].reshape(count * items, depth),
            pl.ds(r.cross_k.shape[1] - count, count),
            count,
        )
        for s in hops:
            attn.along(s, attn_any).wait_recv()
            attn.start_across(s)
        for s in hops:
            start_cross(s)
        for s in hops:
            first_in.along(s, in_mine).start()
        for one, mine in zip(text, text_mine):
            one.along(FAR, mine).start()
        for s in hops:
            first_out.along(s, out_mine).start()
        for s in hops:
            attn.start_onward(s)
        for s in hops:
            attn.start_last(s)
        for s in hops:
            attn.finish(s)
            attn.along(s, attn_any).wait_send()
        for made in own_copies:
            made.wait()
        keep.start()

    @pl.when(step == VISUAL_BLOCKS + 1)
    def _():
        for s in hops:
            cross.along(s, cross_any).wait()
            cross.start_across(s)

    @pl.when(step == VISUAL_BLOCKS + 2)
    def _():
        for s in hops:
            first_in.along(s, in_mine).wait()
            first_in.start_across(s)

    @pl.when(step >= VISUAL_BLOCKS)
    def _():
        self_rows(r, step - VISUAL_BLOCKS)

    @pl.when(step == last)
    def _():
        for s in hops:
            cross.wait_across(s)
            cross.start_onward(s, True)
        for s in hops:
            first_in.wait_across(s)
            first_in.start_onward(s, True)
        for one, mine in zip(text, text_mine):
            one.along(FAR, mine).wait()
            one.start_across(FAR)
        for s in hops:
            cross.start_last(s)
        for s in hops:
            first_in.start_last(s)
        for s in hops:
            cross.finish(s, True)
            first_in.finish(s, True)
        for one in text:
            one.wait_across(FAR)
        for s in hops:
            first_out.along(s, out_mine).wait()
        keep.wait()


def self_rows(r, at):
    span = NQ + TXT
    items = r.hidden.shape[0] // span
    lanes = QUAD * HEAD
    x = r.hidden[...]
    r.q[...] = (mm_nt(x, r.attn_v[0]).astype(NARROW).astype(WIDE) * SCALE).astype(NARROW)
    r.k[...] = mm_nt(x, r.attn_v[1]).astype(NARROW)
    r.v[...] = mm_nt(x, r.attn_v[2]).astype(NARROW)

    units = []
    for item in range(items):
        rows = slice(item * span, (item + 1) * span)
        allowed = allowed_pairs(r.lens, at * items + item, span, lanes)
        for quad in range(r.hidden.shape[1] // lanes):
            units.append((rows, slice(quad * lanes, (quad + 1) * lanes), allowed))
    scores = [mm_nt(r.k[u, c], spread_heads(r.q[u, c], QUAD)) for u, c, _ in units]
    lows = []
    for value, (u, c, allowed) in zip(scores, units):
        value = jnp.where(allowed, value, MASKED_SCORE)
        lifted = jnp.exp(value - jnp.max(value, axis=0, keepdims=True))
        lows.append((lifted * (1.0 / jnp.sum(lifted, axis=0, keepdims=True))).astype(NARROW))
        r.p[u, c] = lows[-1]
    parts = [mm_tn(low, r.v[u, c]) for low, (u, c, _) in zip(lows, units)]
    for part, (u, c, _) in zip(parts, units):
        r.ctx[u, c] = gather_heads(part, QUAD).astype(NARROW)

    residue = x.astype(WIDE) + mm(r.ctx[...], r.attn_v[3])
    r.res[...] = residue
    unit, _ = norm_parts(residue)
    first = unit * r.gain[0:1] + r.shift[0:1]
    for item in range(items):
        r.fq[item * NQ : (item + 1) * NQ] = first[item * span : item * span + NQ]
        r.ft[item * TXT : (item + 1) * TXT] = first[item * span + NQ : (item + 1) * span]


def first_layer(hidden, lens, visual, wkv, qkv, so, cq, co, gain, shift, ffn_in, ffn_out, shards):
    rows, width = hidden.shape
    span, items, depth = visual.shape
    cols = so.shape[0]
    tail = span % (16 * VISUAL_BLOCKS)
    visual_block = (span - tail) // VISUAL_BLOCKS
    block = min(rows, 256)
    copies = 6 * Spread.COPIES * (shards - 1)
    dma = pltpu.SemaphoreType.DMA
    hbm = pl.BlockSpec(memory_space=pl.ANY)

    def later(i):
        return jnp.maximum(i - VISUAL_BLOCKS, 0)

    def whole(shape):
        return pl.BlockSpec(shape, lambda i: (0,) * len(shape), pipeline_mode=pl.Buffered(1))

    def by_rows(count, dtype=NARROW):
        return pl.BlockSpec((count, width), lambda i: (later(i), 0))

    def low(*shape):
        return jax.ShapeDtypeStruct(shape, NARROW)

    def wide(*shape):
        return jax.ShapeDtypeStruct(shape, WIDE)

    ins = dict(
        lens=(lens, pl.BlockSpec(memory_space=pltpu.SMEM)),
        hidden=(hidden, by_rows(block)),
        visual=(
            visual,
            pl.BlockSpec((visual_block, items, depth), lambda i: (jnp.minimum(i, VISUAL_BLOCKS - 1), 0, 0)),
        ),
        visual_tail=(visual, pl.BlockSpec((tail, items, depth), lambda i: (span // tail - 1, 0, 0))),
        wkv=(wkv, whole(wkv.shape)), qkv=(qkv, whole(qkv.shape)), so=(so, whole(so.shape)),
        cq=(cq, whole(cq.shape)), co=(co, whole(co.shape)), gain=(gain, whole(gain.shape)), shift=(shift, whole(shift.shape)),
        ffn_in_first=(ffn_in, whole((1,) + ffn_in.shape[1:])), ffn_out_first=(ffn_out, whole((1,) + ffn_out.shape[1:])),
        ffn_in=(ffn_in, hbm), ffn_out=(ffn_out, hbm),
    )
    kv = (items, span, cols)
    outs = dict(
        cross_k=(low(*kv), whole(kv)), cross_v=(low(*kv), whole(kv)),
        q=(low(rows, width), by_rows(block)), k=(low(rows, width), by_rows(block)), v=(low(rows, width), by_rows(block)),
        p=(low(rows, width), by_rows(block)), ctx=(low(rows, width), by_rows(block)),
        res=(wide(rows, width), by_rows(block)),
        fq=(wide(rows // 2, width), by_rows(block // 2)), ft=(wide(rows // 2, width), by_rows(block // 2)),
        attn=(low(4, shards * cols, width), hbm),
        win=(low(shards, *ffn_in.shape[1:]), hbm), wout=(low(shards, *ffn_out.shape[1:]), hbm),
        cross=(low(shards, 2 * cols, width), hbm),
        tin=(low(*ffn_in.shape[1:]), hbm), tout=(low(*ffn_out.shape[1:]), hbm),
    )
    scratch = dict(
        attn_v=pltpu.VMEM((4, shards * cols, width), NARROW),
        w=pltpu.VMEM((2 * cols, depth), NARROW),
        y=pltpu.VMEM((2 * cols // 128, visual_block * items, 128), WIDE),
        send=dma((copies,)), recv=dma((copies,)), local=dma((9,)),
    )
    names = tuple(ins) + tuple(outs) + tuple(scratch)
    values = pl.pallas_call(
        functools.partial(first_kernel, names),
        grid=(VISUAL_BLOCKS + rows // block,),
        in_specs=[spec for _, spec in ins.values()],
        out_specs=[spec for _, spec in outs.values()],
        out_shape=[shape for shape, _ in outs.values()],
        scratch_shapes=list(scratch.values()),
        compiler_params=pltpu.CompilerParams(
            collective_id=0, has_side_effects=True, vmem_limit_bytes=VMEM_BYTES
        ),
        name="first_layer",
    )(*[value for value, _ in ins.values()])
    return types.SimpleNamespace(**dict(zip(outs, values)))


def self_backward_kernel(
    x_ref, w_ref, gain_ref, res_ref, gq_ref, gt_ref, q_ref, k_ref, v_ref, p_ref, ctx_ref,
    kv_ref, cross_ref, piece0_ref, piece1_ref, piece2_ref, piece3_ref, other_gain, other_shift,
    grad_ref, kv_out, cq_out, co_out, qkv_out, so_out, rows_out, feed_total,
    down, dctx, dq, dk, dv, acc, gain_sums, shift_sums, grads_ref, *rest,
):
    parts = cross_parts(kv_ref.shape, cross_ref.shape)
    (kv_total, cross_total), land, higher = rest[:2], rest[2:5], rest[5:8]
    send, recv, feed_send, feed_recv, local = rest[8:13]
    own_total, own_land, own_higher, (own_send, own_recv) = rest[13], rest[14:16], rest[16:18], rest[18:20]
    few, few_land, few_send, few_recv, few_in = rest[20:]
    later = PeerSum(feed_parts(x_ref.shape[1]), (), (feed_total,), (), (), feed_send, feed_recv)
    peers = PeerSum(parts, (kv_ref, cross_ref), (kv_total, cross_total), land, higher, send, recv)
    last = PeerSum(
        self_parts(grads_ref.shape), (grads_ref,), (own_total,), own_land, own_higher, own_send, own_recv
    )
    span = NQ + TXT
    block = res_ref.shape[0]
    items = block // span
    lanes = QUAD * HEAD
    placed = [
        pltpu.make_async_copy(ref, later.rows((feed_total,), part, later.final_piece(part), 1), local.at[n])
        for n, (ref, part) in enumerate(zip((piece0_ref, piece1_ref, piece2_ref, piece3_ref), later.parts))
    ]
    step = pl.program_id(0)

    @pl.when(step == 0)
    def _():
        for made in placed:
            made.start()
        greet(peers.targets())
        peers.start_halving(0)
        for made in placed:
            made.wait()
        later.start_gathering(0)

    @pl.when(step == 1)
    def _():
        peers.end_halving(0)
        peers.start_halving(1)
        later.end_gathering(0)
        later.start_gathering(1)

    @pl.when(step == 2)
    def _():
        peers.end_halving(1)
        peers.start_halving(2)

    @pl.when(step == 3)
    def _():
        peers.end_halving(2)
        peers.far()
        peers.start_gathering(0)

    unit, inverse = norm_parts(res_ref[...])
    pieces = []
    for item in range(items):
        pieces.append(gq_ref[item * NQ : (item + 1) * NQ])
        pieces.append(gt_ref[item * TXT : (item + 1) * TXT])
    cotangent = jnp.concatenate(pieces, axis=0)
    grad_res = norm_back(unit, inverse, gain_ref[0:1], cotangent)
    gain_sum, shift_sum = column_sums(unit, cotangent)

    @pl.when(step == 0)
    def _():
        gain_sums[...] = gain_sum
        shift_sums[...] = shift_sum

    @pl.when(step > 0)
    def _():
        gain_sums[...] += gain_sum
        shift_sums[...] += shift_sum

    grad_ref[...] = grad_res
    low = grad_res.astype(NARROW)
    down[...] = low
    dctx[...] = mm_nt(low, w_ref[3]).astype(NARROW)

    units = [
        (slice(item * span, (item + 1) * span), slice(quad * lanes, (quad + 1) * lanes))
        for item in range(items)
        for quad in range(w_ref.shape[2] // lanes)
    ]
    for at in range(0, len(units), UNITS):
        some = units[at : at + UNITS]
        spread = [spread_heads(dctx[u], QUAD) for u in some]
        grad_chances = [mm_nt(v_ref[u], one) for u, one in zip(some, spread)]
        scores = []
        for u, value in zip(some, grad_chances):
            weighted = p_ref[u].astype(WIDE)
            inner = jnp.sum(value * weighted, axis=0, keepdims=True)
            scores.append((weighted * (value - inner)).astype(NARROW))
        for u, one in zip(some, spread):
            dv[u] = mm(p_ref[u], one).astype(NARROW)
        for u, one in zip(some, scores):
            dk[u] = mm(one, spread_heads(q_ref[u], QUAD)).astype(NARROW)
        values = [mm_tn(one, k_ref[u]) for u, one in zip(some, scores)]
        for u, value in zip(some, values):
            dq[u] = (gather_heads(value, QUAD) * SCALE).astype(NARROW)

    grad_ref[...] += mm(dq[...], w_ref[0]) + mm(dk[...], w_ref[1]) + mm(dv[...], w_ref[2])

    own = lax.axis_index("tensor")
    cols = grads_ref.shape[0] // 4
    window = acc.shape[1]
    start = pl.multiple_of((own * cols) // 128 * 128, 128)
    here = pl.ds(start, window)
    x = x_ref[...]
    products = (
        mm_tn(dq[:, here], x), mm_tn(dk[:, here], x), mm_tn(dv[:, here], x),
        mm_tn(ctx_ref[:, here], down[...]),
    )

    @pl.when(step == 0)
    def _():
        for c, product in enumerate(products):
            acc[c] = product

    @pl.when(step > 0)
    def _():
        for c, product in enumerate(products):
            acc[c] += product

    @pl.when(step == pl.num_programs(0) - 1)
    def _():
        offset = pl.multiple_of(own * cols - start, 64)
        for c in range(4):
            grads_ref[c * cols : (c + 1) * cols] = acc[c, pl.ds(offset, cols), :].astype(NARROW)
        last.start_halving(0)
        few_in[0:1] = gain_sums[...]
        few_in[1:4] = other_gain[...]
        few_in[4:5] = shift_sums[...]
        few_in[5:8] = other_shift[...]
        few_steps = sum_rows(few_in, few, few_land, few_send, few_recv)
        few_steps[0]()
        peers.end_gathering(0)
        last.end_halving(0)
        last.start_halving(1)
        peers.start_gathering(1)
        few_steps[1]()
        later.end_gathering(1)
        later.start_gathering(2)
        last.end_halving(1)
        last.start_halving(2)
        for run in few_steps[2:]:
            run()
        rows_out[...] = few[few.shape[0] - 1]
        peers.end_gathering(1)
        peers.start_gathering(2)
        last.end_halving(2)
        last.far()
        last.start_gathering(0)
        peers.end_gathering(2)
        kv_out[0] = kv_total[:cols]
        kv_out[1, 128:] = kv_total[cols : 2 * cols - 128]
        kv_out[1, :128] = kv_total[2 * cols - 128 :]
        last.end_gathering(0)
        last.start_gathering(1)
        cq_out[...] = cross_total[:cols]
        co_out[...] = cross_total[cols:]
        last.end_gathering(1)
        last.start_gathering(2)
        later.end_gathering(2)
        last.end_gathering(2)
        for c in range(3):
            qkv_out[c] = own_total[c * cols : (c + 1) * cols]
        so_out[...] = own_total[3 * cols :]


def self_backward(
    hidden, weights, gain, residue, grad_q, grad_t, q, k, v, p, ctx, kv, cross, pieces, gains, shifts,
    cols, ident, peers
):
    rows, width = hidden.shape
    block = min(rows, 256)
    half = block // 2
    full = pl.BlockSpec((block, width), lambda i: (i, 0))
    halves = pl.BlockSpec((half, width), lambda i: (i, 0))
    parts = cross_parts(kv.shape, cross.shape)
    far = (peers // PEERS - 1).bit_length()
    depth = kv.shape[1]
    own = (4 * cols, width)
    steps = 3 + far
    hbm = pl.BlockSpec(memory_space=pl.ANY)
    dma = pltpu.SemaphoreType.DMA
    count = PeerSum.copies(feed_parts(width), far)

    def whole(shape):
        return pl.BlockSpec(shape, lambda i: (0,) * len(shape), pipeline_mode=pl.Buffered(1))

    def wide(*shape):
        return jax.ShapeDtypeStruct(shape, WIDE)

    totals = [
        jax.ShapeDtypeStruct(dims, NARROW)
        for dims in ((2, cols, depth), (cols, width), (cols, width), (3, cols, width), (cols, width))
    ] + [wide(8, width)]
    return pl.pallas_call(
        self_backward_kernel,
        grid=(rows // block,),
        in_specs=[
            full,
            whole(weights.shape),
            pl.BlockSpec(gain.shape, lambda i: (0, 0)),
            full, halves, halves, full, full, full, full, full,
        ]
        + [whole(a.shape) for a in (kv, cross, *pieces, gains, shifts)],
        out_specs=[full] + [whole(t.shape) for t in totals] + [hbm],
        out_shape=[wide(rows, width)] + totals + [jax.ShapeDtypeStruct((4 * width, width), NARROW)],
        scratch_shapes=[pltpu.VMEM((block, width), NARROW)] * 5
        + [pltpu.VMEM((4, (cols + 64 + 127) // 128 * 128, width), WIDE)]
        + [pltpu.VMEM((1, width), WIDE)] * 2
        + [pltpu.VMEM(own, NARROW)]
        + peer_scratch(parts, [kv.shape, cross.shape], far)
        + [dma((count,)), dma((count,)), dma((4,))]
        + peer_scratch(self_parts(own), [own], far)
        + [pltpu.VMEM((steps, 8, width), WIDE)] * 2
        + [dma((steps,)), dma((steps,)), pltpu.VMEM((8, width), WIDE)],
        compiler_params=pltpu.CompilerParams(
            collective_id=ident, has_side_effects=True, vmem_limit_bytes=VMEM_BYTES
        ),
        name="self_backward",
    )(hidden, weights, gain, residue, grad_q, grad_t, q, k, v, p, ctx, kv, cross, *pieces, gains, shifts)


def feed_parts(width):
    return tuple((0, n * width, width // PIECES, 0, width, n // 2) for n in range(4))


LOADS = (
    "fq", "wq_own", "k", "v", "ft", "tin", "tout", "cotq", "tcot", "wo_own", "w_all", "tin2", "tout2",
)
STORES = ("outq", "outt", "gq", "gt", "grads", "kv", "piece0", "piece1", "piece2", "piece3")


def middle_kernel(names, *refs):
    r = types.SimpleNamespace(**dict(zip(names, refs)))
    cols = r.wq_own.shape[0]
    heads = cols // HEAD
    items, span = r.k.shape[:2]
    width = r.fq.shape[1]
    depth = r.visual.shape[2]
    chunks = r.win.shape[0]
    tensor = lax.axis_index("tensor")
    sources = dict(
        tin=r.ffn_in.at[1], tout=r.ffn_out.at[1],
        w_all=r.cross_o.at[:, pl.ds(cols, cols)], tin2=r.tin2_o, tout2=r.tout2_o,
        cotq=r.cot.at[:, pl.ds(0, NQ)], tcot=r.cot.at[:, pl.ds(NQ, TXT)],
    )
    rows = [slice(item * NQ, (item + 1) * NQ) for item in range(items)]
    tall = r.fq.shape

    def load(name, goal=None):
        return pltpu.make_async_copy(
            sources.get(name, getattr(r, name, None)),
            getattr(r, name + "_v") if goal is None else goal,
            r.load_sem.at[LOADS.index(name)],
        )

    def store(name, source):
        return pltpu.make_async_copy(source, getattr(r, name + "_o"), r.store_sem.at[STORES.index(name)])

    pair = (lax.axis_index("dp"), tensor + 1 - 2 * (tensor % 2))
    swaps = [remote(r.tpart.at[n], r.tland.at[n], r.swap_send.at[n], r.swap_recv.at[n], pair) for n in range(2)]
    forth = HeadGather(r.heads1, r.head_send1, r.head_recv1)
    gather = HeadGather(r.heads2, r.head_send2, r.head_recv2)
    base = Spread.COPIES * (chunks - 1)
    hops = range(1, chunks)
    first_out = Spread(eighth(r.wout_o), r.spread_send, r.spread_recv, base)
    text = [
        Spread(one_shard(ref), r.spread_send, r.spread_recv, n * base) for n, ref in ((3, r.tin2_o), (4, r.tout2_o))
    ]
    parts = feed_parts(width)
    kind_parts = ((0, 0, width // PIECES, 0, width, 0), (0, width, width // PIECES, 0, width, 1))
    feed_q = [None]
    pieces = (r.piece0, r.piece1, r.piece2, r.piece3)
    peers_q, peers_t = (
        PeerSum(
            kind_parts, source, (), r.land[kind::2], r.higher[kind::2], r.peer_send, r.peer_recv,
            kind * PeerSum.copies(kind_parts, len(PeerSum.far_bits())), pieces[kind::2],
        )
        for kind, source in enumerate((feed_q, (r.feed_t,)))
    )

    early = ("tin_v", "tout_v", "tin2_v", "tout2_v", "tslope", "tslope2", "cotq_v", "tcot_v")

    def to_feed_forward(*buffers):
        for name, buffer in zip(early, buffers):
            setattr(r, name, buffer)
        for name in LOADS[:11]:
            load(name).start()
        greet(first_out.along_targets() + peers_q.targets())
        for s in hops:
            first_out.start_across(s)
        for one in text:
            one.start_onward(FAR, True)
        for name in ("fq", "wq_own", "k", "v"):
            load(name).wait()
        r.q[...] = (
            mm_nt(r.fq_v[...].astype(NARROW), r.wq_own_v[...]).astype(NARROW).astype(WIDE) * SCALE
        ).astype(NARROW)
        for half in range(2):
            some = range(half * items // 2, (half + 1) * items // 2)
            scores = [mm_nt(r.k_v[item], spread_heads(r.q[rows[item]], heads)) for item in some]
            lows = []
            for item, value in zip(some, scores):
                lifted = jnp.exp(value - jnp.max(value, axis=0, keepdims=True))
                lows.append((lifted * (1.0 / jnp.sum(lifted, axis=0, keepdims=True))).astype(NARROW))
                r.p[item] = lows[-1]
            values = [mm_tn(low, r.v_v[item]) for item, low in zip(some, lows)]
            for item, value in zip(some, values):
                r.ctx[rows[item]] = gather_heads(value, heads).astype(NARROW)
            count = items // 2 * NQ
            here = slice(half * count, (half + 1) * count)
            r.heads1[tensor, here] = r.ctx[here]
            forth.start(half)
        def text_part(win, wout, slope_v, act_v):
            act, slope = gelu_parts(mm(r.ft_v[...].astype(NARROW), win[...]))
            slope_v[...] = slope.astype(NARROW)
            act = act.astype(NARROW)
            if act_v is not None:
                act_v[...] = act
            return mm(act, wout[...])

        for name in ("ft", "tin", "tout"):
            load(name).wait()
        r.gt_v[...] = text_part(r.tin_v, r.tout_v, r.tslope, r.tact)
        for s in hops:
            first_out.start_onward(s)
        for one in text:
            one.start_last(FAR)
        for one in text:
            one.finish(FAR, True)
        load("tin2").start()
        load("tout2").start()
        forth.wait(0)
        for s in hops:
            first_out.start_last(s)
        forth.wait(1)
        load("w_all").wait()
        r.gq_v[...] = forth.product(r.w_all_v)
        sources["w_all"] = r.cross_o.at[:, pl.ds(0, cols)]
        load("w_all").start()
        load("tin2").wait()
        load("tout2").wait()
        r.tpart[0] = (r.gt_v[...] + text_part(r.tin2_v, r.tout2_v, r.tslope2, None)).astype(NARROW)
        swaps[0].start()

        def text_rows():
            load("tcot").wait()
            unit, inverse = norm_parts(r.ft_v[...] + r.tpart[0].astype(WIDE) + r.tland[0].astype(WIDE))
            r.outt[...] = (unit * r.gain[3:4] + r.shift[3:4]).astype(NARROW)
            store("outt", r.outt).start()
            cotangent = r.tcot_v[...].astype(WIDE).reshape(tall)
            gain_sum, shift_sum = column_sums(unit, cotangent)
            r.gains[2:3] = gain_sum
            r.shifts[2:3] = shift_sum
            grad = norm_back(unit, inverse, r.gain[3:4], cotangent)
            r.gt_v[...] = grad
            r.ttop[...] = grad.astype(NARROW)
            r.tdpre[...] = (mm_nt(r.ttop[...], r.tout_v[...]) * r.tslope[...].astype(WIDE)).astype(NARROW)
            far = (mm_nt(r.ttop[...], r.tout2_v[...]) * r.tslope2[...].astype(WIDE)).astype(NARROW)
            r.tpart[1] = (mm_nt(r.tdpre[...], r.tin_v[...]) + mm_nt(far, r.tin2_v[...])).astype(NARROW)
            swaps[1].start()
            r.feed_t[:width] = mm_tn(r.ft_v[...].astype(NARROW), r.tdpre[...]).astype(NARROW)
            r.feed_t[width:] = mm_tn(r.tact[...], r.ttop[...]).astype(NARROW)
            peers_t.start_halving(0)

        def query_rows(slopes, total, weights, outq):
            def fetch(j):
                slot, chunk = j % 2, j % chunks
                return [
                    pltpu.make_async_copy(ref.at[chunk], weights.at[slot, n], r.weight_sem.at[slot, n])
                    for n, ref in enumerate((r.win_o, r.wout_o))
                ]

            unit, _ = norm_parts(r.fq_v[...] + r.gq_v[...])
            value = unit * r.gain[1:2] + r.shift[1:2]
            r.low[...] = value.astype(NARROW)
            total[...] = value
            for s in hops:
                first_out.finish(s)
            for made in fetch(0):
                made.start()

            def next_weights(j):
                for made in fetch(j):
                    made.wait()

                @pl.when(j + 1 < 2 * chunks)
                def _():
                    for made in fetch(j + 1):
                        made.start()

                return weights.at[j % 2, 0], weights.at[j % 2, 1]

            @pl.loop(0, chunks)
            def _(j):
                win, wout = next_weights(j)
                act, slope = gelu_parts(mm(r.low[...], win[...]))
                slopes[j] = slope.astype(NARROW)
                act = act.astype(NARROW)
                total[...] += mm(act, wout[...])

                @pl.when(j == tensor)
                def _():
                    r.act[...] = act


            unit, inverse = norm_parts(total[...])
            outq[...] = (unit * r.gain[2:3] + r.shift[2:3]).astype(NARROW)
            store("outq", outq).start()
            load("cotq").wait()
            cotangent = r.cotq_v[...].astype(WIDE).reshape(tall)
            gain_sum, shift_sum = column_sums(unit, cotangent)
            r.gains[1:2] = gain_sum
            r.shifts[1:2] = shift_sum
            grad = norm_back(unit, inverse, r.gain[2:3], cotangent)
            total[...] = grad
            r.top[...] = grad.astype(NARROW)

            @pl.loop(chunks, 2 * chunks)
            def _(j):
                win, wout = next_weights(j)
                chunk = j - chunks
                dpre = (mm_nt(r.top[...], wout[...]) * slopes[chunk].astype(WIDE)).astype(NARROW)
                total[...] += mm_nt(dpre, win[...])

                @pl.when(chunk == tensor)
                def _():
                    r.dpre[...] = dpre

                @pl.when(chunk == 2)
                def _():
                    swaps[0].wait()
                    text_rows()


            grad_second = total[...]
            unit, inverse = norm_parts(r.fq_v[...] + r.gq_v[...])
            gain_sum, shift_sum = column_sums(unit, grad_second)
            r.gains[0:1] = gain_sum
            r.shifts[0:1] = shift_sum
            grad = norm_back(unit, inverse, r.gain[1:2], grad_second)
            r.gq_v[...] = grad
            r.down[...] = grad.astype(NARROW)
            store("outq", outq).wait()

        pl.run_scoped(
            query_rows,
            pltpu.VMEM((chunks, tall[0], r.win.shape[2]), NARROW),
            pltpu.VMEM(tall, WIDE),
            pltpu.VMEM((2, 2) + r.win.shape[1:], NARROW),
            pltpu.VMEM(tall, NARROW),
        )

    inner, outer = r.ffn_in.shape[1:], r.ffn_out.shape[1:]
    pl.run_scoped(
        to_feed_forward,
        *[pltpu.VMEM(shape, NARROW) for shape in (inner, outer, inner, outer, (tall[0], inner[1]), (tall[0], inner[1]), (items, NQ, width), (items, TXT, width))],
    )

    def query_gradients(goal):
        feed_q[0] = goal
        goal[:width] = mm_tn(r.low[...], r.dpre[...]).astype(NARROW)
        goal[width:] = mm_tn(r.act[...], r.top[...]).astype(NARROW)
        peers_q.start_halving(0)

    def cross_rows(dctx, dq, score, dkv, acc, x, x_tail, kv, feed_v):
        group = items // 4
        steps = VISUAL_STEPS
        tail = span % steps
        block = (span - tail) // steps

        def fetch(j):
            return pltpu.make_async_copy(r.visual.at[pl.ds(j * block, block)], x.at[j % 2], r.x_sem.at[j % 2])

        rest = pltpu.make_async_copy(r.visual.at[pl.ds(span - tail, tail)], x_tail, r.x_sem.at[2])
        fetch(0).start()
        rest.start()
        query_gradients(feed_v)
        peers_t.end_halving(0)
        peers_t.start_halving(1)
        load("wo_own").wait()
        dctx[...] = mm_nt(r.down[...], r.wo_own_v[...]).astype(NARROW)
        for g in range(4):
            some = range(g * group, (g + 1) * group)
            spread = [spread_heads(dctx[rows[item]], heads) for item in some]
            grad_chances = [mm_nt(r.v_v[item], one) for item, one in zip(some, spread)]
            scores = []
            for item, value in zip(some, grad_chances):
                weighted = r.p[item].astype(WIDE)
                inner = jnp.sum(value * weighted, axis=0, keepdims=True)
                scores.append((weighted * (value - inner)).astype(NARROW))
                score[item] = scores[-1]
            values = [mm_tn(one, r.k_v[item]) for item, one in zip(some, scores)]
            for item, value in zip(some, values):
                dq[rows[item]] = (gather_heads(value, heads) * SCALE).astype(NARROW)
            if g % 2:
                count = 2 * group * NQ
                here = slice(g // 2 * count, (g // 2 + 1) * count)
                r.heads2[tensor, here] = dq[here]
                gather.start(g // 2)
        peers_q.end_halving(0)
        peers_q.start_halving(1)
        none = jnp.zeros((QUAD * NQ, cols), NARROW)
        for g in range(4):
            some = range(g * group, (g + 1) * group)
            both = []
            for item in some:
                one = spread_heads(dctx[rows[item]], heads)
                both.append(
                    mm(
                        jnp.concatenate([score[item], r.p[item]], axis=1),
                        jnp.concatenate(
                            [
                                jnp.concatenate([spread_heads(r.q[rows[item]], heads), none], axis=1),
                                jnp.concatenate([none, one[:, 128:], one[:, :128]], axis=1),
                            ],
                            axis=0,
                        ),
                    )
                )
            for item, value in zip(some, both):
                for tile in range(dkv.shape[0]):
                    dkv[tile, pl.ds(item, span, stride=items)] = value[:, tile * 128 : (tile + 1) * 128]
        r.grads[:cols] = mm_tn(dq[...], r.fq_v[...].astype(NARROW)).astype(NARROW)
        r.grads[cols:] = mm_tn(r.ctx[...], r.down[...]).astype(NARROW)
        store("grads", r.grads).start()

        def product(first, count, value):
            grads = [dkv[tile, pl.ds(first, count)].astype(NARROW) for tile in range(dkv.shape[0])]
            return mm_tn(jnp.concatenate(grads, axis=1), value.reshape(count, depth))

        rest.wait()
        acc[...] = product((span - tail) * items, tail * items, x_tail[...])

        @pl.loop(0, steps)
        def _(j):
            fetch(j).wait()

            @pl.when(j + 1 < steps)
            def _():
                fetch(j + 1).start()

            acc[...] += product(pl.multiple_of(j * block * items, 16), block * items, x[j % 2])

            @pl.when(j == 1)
            def _():
                peers_t.end_halving(1)
                peers_t.start_halving(2)

            @pl.when(j == 5)
            def _():
                peers_q.end_halving(1)
                peers_q.start_halving(2)

        kv[...] = acc[...].astype(kv.dtype)
        store("kv", kv).start()
        gather.wait(0)
        gather.wait(1)
        load("w_all").wait()
        r.gq_v[...] += gather.product(r.w_all_v)
        store("gq", r.gq_v).start()
        swaps[1].wait()
        r.gt_v[...] += r.tpart[1].astype(WIDE) + r.tland[1].astype(WIDE)
        store("gt", r.gt_v).start()
        for one in (peers_t, peers_q):
            one.end_halving(2)
            one.far()
        for n, piece in enumerate(pieces):
            store("piece%d" % n, piece).start()
        store("kv", kv).wait()

    pl.run_scoped(
        cross_rows,
        pltpu.VMEM((tall[0], cols), NARROW),
        pltpu.VMEM((tall[0], cols), NARROW),
        pltpu.VMEM((items, span, QUAD * NQ), NARROW),
        pltpu.VMEM((2 * cols // 128, items * span, 128), WIDE),
        pltpu.VMEM((2 * cols, depth), WIDE),
        pltpu.VMEM((2, span // VISUAL_STEPS, items, depth), NARROW),
        pltpu.VMEM((span % VISUAL_STEPS, items, depth), NARROW),
        pltpu.VMEM((2 * cols, depth), NARROW),
        pltpu.VMEM((2 * width, width), NARROW),
    )
    for name, source in (
        ("outt", r.outt), ("gq", r.gq_v), ("gt", r.gt_v), ("grads", r.grads),
        ("piece0", r.piece0), ("piece1", r.piece1), ("piece2", r.piece2), ("piece3", r.piece3),
    ):
        store(name, source).wait()


def middle(arrays, ident, peers):
    rows, width = arrays["fq"].shape
    cols = arrays["wq_own"].shape[0]
    items, span = arrays["k"].shape[:2]
    hidden = arrays["ffn_in"].shape[2]
    depth = arrays["visual"].shape[2]
    shards = arrays["win"].shape[0]
    far = (peers // PEERS - 1).bit_length()
    parts = feed_parts(width)
    piece = (parts[0][2], width)
    dma = pltpu.SemaphoreType.DMA
    hbm, vmem = pl.BlockSpec(memory_space=pl.ANY), pl.BlockSpec(memory_space=pltpu.VMEM)

    def low(*dims):
        return pltpu.VMEM(dims, NARROW)

    def wide(*dims):
        return pltpu.VMEM(dims, WIDE)

    out = jax.ShapeDtypeStruct
    outs = dict(
        outq_o=out((rows, width), NARROW), outt_o=out((rows, width), NARROW),
        gq_o=out((rows, width), WIDE), gt_o=out((rows, width), WIDE),
        grads_o=out((2 * cols, width), NARROW), kv_o=out((2 * cols, depth), NARROW),
        piece0_o=out(piece, NARROW), piece1_o=out(piece, NARROW), piece2_o=out(piece, NARROW), piece3_o=out(piece, NARROW),
        gains=out((3, width), WIDE), shifts=out((3, width), WIDE),
        win_o=out(arrays["win"].shape, NARROW), wout_o=out(arrays["wout"].shape, NARROW),
        cross_o=out(arrays["cross_w"].shape, NARROW),
        tin2_o=out(arrays["tin2"].shape, NARROW), tout2_o=out(arrays["tout2"].shape, NARROW),
    )
    copies = feed_copies(shards)
    total = peer_scratch(parts, [], far)
    scratch = dict(
        fq_v=wide(rows, width), wq_own_v=low(cols, width), wo_own_v=low(cols, width),
        k_v=low(*arrays["k"].shape), v_v=low(*arrays["v"].shape), ft_v=wide(rows, width),
        w_all_v=low(shards, cols, width),
        q=low(rows, cols), ctx=low(rows, cols), p=low(items, span, QUAD * NQ),
        tact=low(rows, hidden),
        low=low(rows, width), top=low(rows, width), down=low(rows, width),
        act=low(rows, hidden), dpre=low(rows, hidden),
        ttop=low(rows, width), tdpre=low(rows, hidden), outt=low(rows, width),
        gq_v=wide(rows, width), gt_v=wide(rows, width), grads=low(2 * cols, width),
        tpart=low(2, rows, width), tland=low(2, rows, width), swap_send=dma((2,)), swap_recv=dma((2,)),
        heads1=low(shards, rows, cols), head_send1=dma((2, shards)), head_recv1=dma((2, shards)),
        heads2=low(shards, rows, cols), head_send2=dma((2, shards)), head_recv2=dma((2, shards)),
        spread_send=dma((copies,)), spread_recv=dma((copies,)),
        feed_t=low(2 * width, width), piece0=low(*piece), piece1=low(*piece), piece2=low(*piece), piece3=low(*piece),
        land=total[:4], higher=total[4:8], peer_send=total[8], peer_recv=total[9],
        load_sem=dma((len(LOADS),)), store_sem=dma((len(STORES),)), weight_sem=dma((2, 2)), x_sem=dma((3,)),
    )
    names = tuple(arrays) + tuple(outs) + tuple(scratch)
    return dict(
        zip(
            outs,
            pl.pallas_call(
                functools.partial(middle_kernel, names),
                in_specs=[vmem if name in ("gain", "shift") else hbm for name in arrays],
                out_specs=[vmem if name in ("gains", "shifts") else hbm for name in outs],
                out_shape=list(outs.values()),
                input_output_aliases={
                    list(arrays).index(a): list(outs).index(b)
                    for a, b in (
                        ("win", "win_o"), ("wout", "wout_o"), ("cross_w", "cross_o"), ("tin2", "tin2_o"), ("tout2", "tout2_o"),
                    )
                },
                scratch_shapes=list(scratch.values()),
                compiler_params=pltpu.CompilerParams(
                    collective_id=ident, has_side_effects=True, vmem_limit_bytes=62 * 2**20
                ),
                name="middle",
            )(*arrays.values()),
        )
    )


def on_device(
    hidden_in,
    visual_feats,
    caption_lengths,
    self_qkv,
    self_out,
    cross_query,
    cross_kv,
    cross_out,
    ffn_in,
    ffn_out,
    norm_gain,
    norm_shift,
    out_grad,
):
    items = visual_feats.shape[0]
    rows, width = hidden_in.shape
    span = rows // items
    cols = self_qkv.shape[2]
    shards = lax.axis_size("tensor")

    visual = jnp.swapaxes(visual_feats, 0, 1)
    cross_wq = jnp.swapaxes(cross_query, 0, 1)
    first = first_layer(
        hidden_in, jnp.swapaxes(caption_lengths, 0, 1), visual, jnp.swapaxes(cross_kv, 1, 2), jnp.swapaxes(self_qkv, 1, 2),
        self_out, cross_wq, cross_out, norm_gain, norm_shift, ffn_in, ffn_out, shards,
    )
    peers = lax.axis_size("dp")
    mid = middle(
        dict(
            fq=first.fq, wq_own=cross_wq, k=first.cross_k, v=first.cross_v, ft=first.ft,
            cot=out_grad.reshape(items, span, width), wo_own=cross_out, ffn_in=ffn_in, ffn_out=ffn_out, win=first.win,
            wout=first.wout, cross_w=first.cross, tin2=first.tin, tout2=first.tout, visual=visual,
            gain=norm_gain, shift=norm_shift,
        ),
        2, peers,
    )
    out_q, out_t, g_cross, g_kv = mid["outq_o"], mid["outt_o"], mid["grads_o"], mid["kv_o"]
    grad_hidden, g_kv, g_cq, g_co, g_qkv, g_so, gains, g_feed = self_backward(
        hidden_in, first.attn, norm_gain, first.res, mid["gq_o"], mid["gt_o"], first.q, first.k, first.v, first.p, first.ctx,
        g_kv, g_cross,
        [mid["piece%d_o" % n] for n in range(4)], mid["gains"], mid["shifts"], cols, 6, peers,
    )
    g_feed = g_feed.reshape(2, 2, width, width).astype(WIDE)
    g_in, g_out = g_feed[0], g_feed[1]
    g_kv, g_cq, g_co, g_qkv, g_so = [g.astype(WIDE) for g in (g_kv, g_cq, g_co, g_qkv, g_so)]
    out = jnp.concatenate(
        [out_q.reshape(items, NQ, width), out_t.reshape(items, TXT, width)], axis=1
    ).reshape(rows, width)
    return (
        out,
        grad_hidden,
        jnp.swapaxes(g_qkv, 1, 2),
        g_so,
        jnp.swapaxes(g_cq, 0, 1),
        jnp.swapaxes(g_kv, 1, 2),
        g_co,
        g_in,
        g_out,
        gains[:4],
        gains[4:],
    )


def solution(mesh):
    placed = (
        P("dp", None),
        P("dp", None, None),
        P("dp", None),
        P(None, None, "tensor"),
        P("tensor", None),
        P(None, "tensor"),
        P(None, None, "tensor"),
        P("tensor", None),
        P(None, None, "tensor"),
        P(None, "tensor", None),
        P(),
        P(),
        P("dp", None),
    )
    return jax.shard_map(
        on_device,
        mesh=mesh,
        in_specs=placed,
        out_specs=(
            P("dp", None),
            P("dp", None),
            P(None, None, "tensor"),
            P("tensor", None),
            P(None, "tensor"),
            P(None, None, "tensor"),
            P("tensor", None),
            P(None, None, "tensor"),
            P(None, "tensor", None),
            P(),
            P(),
        ),
        check_vma=False,
    )
```

```python
import functools
import math
import types

import jax
import jax.numpy as jnp
from jax import lax
from jax.experimental import pallas as pl
from jax.experimental.pallas import tpu as pltpu
from jax.sharding import PartitionSpec as P

HEAD = 64
NQ = 32
TXT = 32
QUAD = 4
UNITS = 12
VISUAL_STEPS = 8
EPSILON = 1e-06
MASKED_SCORE = -1e30
SCALE = 1.0 / math.sqrt(HEAD)
WIDE = jnp.float32
NARROW = jnp.bfloat16
VMEM_BYTES = 60 * 2**20


def mm(a, b):
    return lax.dot_general(a, b, (((1,), (0,)), ((), ())), preferred_element_type=WIDE)


def mm_nt(a, b):
    return lax.dot_general(a, b, (((1,), (1,)), ((), ())), preferred_element_type=WIDE)


def mm_tn(a, b):
    return lax.dot_general(a, b, (((0,), (0,)), ((), ())), preferred_element_type=WIDE)


def lane_group(rows, lanes, size):
    return lax.broadcasted_iota(jnp.int32, (rows, lanes), 1) // size


def spread_heads(block, count):
    group = lane_group(1, block.shape[1], HEAD)
    return jnp.concatenate(
        [block * jnp.where(group == h, 1.0, 0.0).astype(NARROW) for h in range(QUAD)], axis=0
    )


def gather_heads(block, count):
    rows, lanes = block.shape[0] // QUAD, block.shape[1]
    group = lane_group(rows, lanes, HEAD)
    out = block[:rows]
    for h in range(1, count):
        out = jnp.where(group == h, block[h * rows : (h + 1) * rows], out)
    return out


def norm_parts(residue):
    mean = jnp.mean(residue, axis=-1, keepdims=True)
    centered = residue - mean
    variance = jnp.mean(centered * centered, axis=-1, keepdims=True)
    inverse = lax.rsqrt(variance + EPSILON)
    return centered * inverse, inverse


def norm_back(unit, inverse, gain_row, cotangent):
    scaled = gain_row * cotangent
    first = jnp.mean(scaled, axis=-1, keepdims=True)
    second = jnp.mean(scaled * unit, axis=-1, keepdims=True)
    return inverse * (scaled - first - unit * second)


def column_sums(unit, cotangent):
    return (
        jnp.sum(cotangent * unit, axis=0, keepdims=True),
        jnp.sum(cotangent, axis=0, keepdims=True),
    )


def gelu_parts(pre):
    bell = jnp.exp(-0.5 * pre * pre)
    half = 0.5 * lax.erf(pre * math.sqrt(0.5)) + 0.5
    return pre * half, half + pre * bell * (1.0 / math.sqrt(2.0 * math.pi))


MESH = pl.DeviceIdType.MESH
PEERS = 8


def flip(index, bit):
    return index + bit - 2 * bit * ((index // bit) % 2)


def greet(targets):
    barrier = pltpu.get_barrier_semaphore()
    for target in targets:
        pl.semaphore_signal(barrier, inc=1, device_id=target, device_id_type=MESH)
    pl.semaphore_wait(barrier, len(targets))


def remote(src, dst, send, recv, target):
    return pltpu.make_async_remote_copy(
        src_ref=src, dst_ref=dst, send_sem=send, recv_sem=recv, device_id=target, device_id_type=MESH
    )


class Spread:
    COPIES = 9

    def __init__(self, at, send, recv, base):
        self.at, self.send, self.recv, self.base = at, send, recv, base
        self.dp, self.tensor = lax.axis_index("dp"), lax.axis_index("tensor")
        self.shards = lax.axis_size("tensor")
        self.peer = self.dp % PEERS

    def hop(self, slot, s, src, dst, target):
        index = self.base + (s - 1) * self.COPIES + slot
        return remote(src, dst, self.send.at[index], self.recv.at[index], target)

    def came(self, s):
        return (self.tensor + self.shards - s) % self.shards

    def along(self, s, own):
        return self.hop(0, s, own, self.at(self.tensor, self.peer, None), (self.dp, (self.tensor + s) % self.shards))

    def hand(self, slot, s, bit, peer, half):
        place = self.at(self.came(s), peer, half)
        return self.hop(slot, s, place, place, (flip(self.dp, bit), self.tensor))

    def across(self, s):
        return [self.hand(1, s, 2, self.peer, None), self.hand(2, s, 4, self.peer, None), self.hand(3, s, 1, self.peer, None)]

    def onward(self, s):
        x, y = flip(self.peer, 2), flip(self.peer, 4)
        return (
            [self.hand(4, s, 4, x, 0), self.hand(5, s, 1, x, None)],
            [self.hand(6, s, 2, y, 1), self.hand(7, s, 1, y, None)],
        )

    def last(self, s):
        return self.hand(8, s, 1, flip(flip(self.peer, 2), 4), None)

    def start_across(self, s):
        for made in self.across(s):
            made.start()

    def wait_across(self, s):
        for made in self.across(s):
            made.wait()

    def start_onward(self, s, arrived=False):
        over_x, over_y, _ = self.across(s)
        by_x, by_y = self.onward(s)
        if not arrived:
            over_x.wait_recv()
        for made in by_x:
            made.start()
        if not arrived:
            over_y.wait_recv()
        for made in by_y:
            made.start()

    def start_last(self, s):
        by_x, by_y = self.onward(s)
        by_x[0].wait_recv()
        by_y[0].wait_recv()
        self.last(s).start()

    def finish(self, s, arrived=False):
        over = self.across(s)
        by_x, by_y = self.onward(s)
        final = self.last(s)
        for made in ([] if arrived else [over[2]]) + [by_x[1], by_y[1], final]:
            made.wait_recv()
        for made in ([] if arrived else over) + by_x + by_y + [final]:
            made.wait_send()

    def targets(self):
        return self.along_targets() + self.peer_targets()

    def along_targets(self):
        return [(self.dp, (self.tensor + s) % self.shards) for s in range(1, self.shards)]

    def peer_targets(self):
        return [(flip(self.dp, bit), self.tensor) for bit in (2, 4, 1)]


FAR = 2


def one_shard(ref):
    rows = ref.shape[0] // PEERS

    def at(shard, peer, half):
        return ref.at[half_rows(peer * rows, rows, half)]

    return at


def half_rows(first, rows, half):
    split = (rows // 2 + 15) // 16 * 16
    start, count = {None: (0, rows), 0: (0, split), 1: (split, rows - split)}[half]
    return pl.ds(pl.multiple_of(first + start, 16), count)


def eighth(ref):
    rows = ref.shape[1] // PEERS

    def at(shard, peer, half):
        return ref.at[shard, half_rows(peer * rows, rows, half)]

    return at


class HeadGather:
    def __init__(self, buffer, send, recv):
        self.buffer, self.send, self.recv = buffer, send, recv
        self.dp, self.tensor = lax.axis_index("dp"), lax.axis_index("tensor")
        self.shards = lax.axis_size("tensor")

    def put(self, half, value):
        rows = value.shape[0]
        first = half * (rows + rows // 2)
        self.buffer[self.tensor, first : first + rows] = value[:, :128]
        self.buffer[self.tensor, first + rows : first + rows + rows // 2] = jnp.concatenate(
            [value[: rows // 2, 128:], value[rows // 2 :, 128:]], axis=1
        )

    def take(self, shard):
        count = self.buffer.shape[1] // 2
        rows = count * 2 // 3
        parts = []
        for half in range(2):
            low = self.buffer[shard, half * count : half * count + rows]
            rest = self.buffer[shard, half * count + rows : (half + 1) * count]
            high = jnp.concatenate([rest[:, :HEAD], rest[:, HEAD:]], axis=0)
            parts.append(jnp.concatenate([low, high], axis=1))
        return jnp.concatenate(parts, axis=0)

    def copies(self, half):
        count = self.buffer.shape[1] // 2
        place = self.buffer.at[self.tensor, pl.ds(half * count, count)]
        return [
            remote(place, place, self.send.at[half, s], self.recv.at[half, s], (self.dp, (self.tensor + s) % self.shards))
            for s in range(1, self.shards)
        ]

    def start(self, half):
        for made in self.copies(half):
            made.start()

    def wait(self, half):
        for made in self.copies(half):
            made.wait()

    def product(self, weights):
        total = mm(self.take(0), weights[0])
        for shard in range(1, self.shards):
            total += mm(self.take(shard), weights[shard])
        return total


PIECES = 8


class PeerSum:
    def __init__(self, parts, source, total, land, higher, send, recv, base=0, pieces=None):
        self.parts, self.source, self.total, self.land, self.higher = parts, source, total, land, higher
        self.pieces = pieces
        self.send, self.recv, self.base = send, recv, base
        self.dp, self.tensor = lax.axis_index("dp"), lax.axis_index("tensor")
        self.bits = [(self.dp // b) % 2 for b in (1, 2, 4)]

    @staticmethod
    def far_bits():
        return [PEERS << k for k in range((lax.axis_size("dp") // PEERS - 1).bit_length())]

    @staticmethod
    def copies(parts, far):
        return len(parts) * (6 + far)

    def way(self, part):
        order = ((2, self.bits[1]), (4, self.bits[2]))
        return order if part[5] == 0 else order[::-1]

    def rows(self, refs, part, piece, count):
        array, first, size, column, columns, _ = part
        start = pl.multiple_of(first + piece * size, 16)
        return refs[array].at[pl.ds(start, count * size), pl.ds(column, columns)]

    def hop(self, n, stage, src, dst, bit):
        index = self.base + n * (6 + len(self.far_bits())) + stage
        return remote(src, dst, self.send.at[index], self.recv.at[index], (flip(self.dp, bit), self.tensor))

    def landed(self, n, piece, count):
        size = self.parts[n][2]
        return self.land[n].at[pl.ds(pl.multiple_of(piece * size, 16), count * size)]

    def halving(self, n, stage):
        part = self.parts[n]
        core = self.bits[0]
        (bit_1, own_1), (bit_2, own_2) = self.way(part)
        if stage == 0:
            bit, place = 1, self.landed(n, 0, 4)
            out = self.rows(self.source, part, (1 - core) * 4, 4)
            kept = self.rows(self.source, part, core * 4, 4)
        elif stage == 1:
            bit, place = bit_1, self.landed(n, 4, 2)
            out, kept = self.landed(n, (1 - own_1) * 2, 2), self.landed(n, own_1 * 2, 2)
        else:
            bit, place = bit_2, self.landed(n, 6, 1)
            out, kept = self.landed(n, 4 + 1 - own_2, 1), self.landed(n, 4 + own_2, 1)
        goal = self.final_place(n) if stage == 2 else place
        return self.hop(n, stage, out, place, bit), kept, place, goal

    def final_place(self, n):
        if self.pieces is not None:
            return self.pieces[n]
        return self.rows(self.total, self.parts[n], self.final_piece(self.parts[n]), 1)

    def final_piece(self, part):
        (_, own_1), (_, own_2) = self.way(part)
        return self.bits[0] * 4 + own_1 * 2 + own_2

    def gathering(self, n, stage):
        part = self.parts[n]
        core = self.bits[0]
        (bit_1, own_1), (bit_2, _) = self.way(part)
        piece, count, bit = (
            (self.final_piece(part), 1, bit_2), (core * 4 + own_1 * 2, 2, bit_1), (core * 4, 4, 1),
        )[stage]
        place = self.rows(self.total, part, piece, count)
        return self.hop(n, 3 + stage, place, place, bit)

    def targets(self):
        return [(flip(self.dp, bit), self.tensor) for bit in [1, 2, 4] + self.far_bits()]

    def start_halving(self, stage):
        for n in range(len(self.parts)):
            self.halving(n, stage)[0].start()

    def end_halving(self, stage):
        for n in range(len(self.parts)):
            made, kept, place, goal = self.halving(n, stage)
            made.wait_recv()
            goal[...] = (kept[...].astype(WIDE) + place[...].astype(WIDE)).astype(goal.dtype)
        for n in range(len(self.parts)):
            self.halving(n, stage)[0].wait_send()

    def far(self):
        for k, bit in enumerate(self.far_bits()):
            for n in range(len(self.parts)):
                place = self.final_place(n)
                made = self.hop(n, 6 + k, place, self.higher[n].at[k], bit)
                made.start()
                made.wait()
                place[...] = (place[...].astype(WIDE) + self.higher[n][k].astype(WIDE)).astype(place.dtype)

    def start_gathering(self, stage):
        for n in range(len(self.parts)):
            self.gathering(n, stage).start()

    def end_gathering(self, stage):
        for n in range(len(self.parts)):
            self.gathering(n, stage).wait()


def peer_scratch(parts, shapes, far):
    dma = pltpu.SemaphoreType.DMA
    count = PeerSum.copies(parts, far)
    land = [pltpu.VMEM((7 * p[2], p[4]), NARROW) for p in parts]
    higher = [pltpu.VMEM((far, p[2], p[4]) if far else (1, 16, 128), NARROW) for p in parts]
    return [pltpu.VMEM(shape, NARROW) for shape in shapes] + land + higher + [dma((count,)), dma((count,))]


def sum_rows(values, out, land, send, recv):
    dp, tensor = lax.axis_index("dp"), lax.axis_index("tensor")
    bits = [1, 2, 4] + PeerSum.far_bits()

    def hop(k):
        source = values if k == 0 else out.at[k - 1]
        return remote(source, land.at[k], send.at[k], recv.at[k], (flip(dp, bits[k]), tensor))

    def run(k):
        if k > 0:
            hop(k - 1).wait()
            out[k - 1] = (values if k == 1 else out.at[k - 2])[...] + land[k - 1]
        if k < len(bits):
            hop(k).start()

    return [functools.partial(run, k) for k in range(len(bits) + 1)]


def cross_parts(kv, cross):
    width = cross[1]
    return (
        (0, 0, kv[0] // PIECES, 0, width, 0),
        (0, 0, kv[0] // PIECES, width, kv[1] - width, 1),
        (1, 0, cross[0] // PIECES, 0, width, 0),
    )


def self_parts(own):
    third, width = own[0] // 3, own[1]
    return ((0, 0, third // PIECES, 0, width, 0), (0, third, 2 * third // PIECES, 0, width, 1))


def feed_copies(shards):
    return 5 * Spread.COPIES * (shards - 1)


def labels_of(position, ends):
    place = position - NQ
    label = jnp.zeros_like(position)
    for end in ends:
        label = label + jnp.where(place >= end, 1, 0)
    return jnp.where(position < NQ, -1, label)


def allowed_pairs(lens_ref, item, span, lanes):
    ends = []
    total = jnp.int32(0)
    for c in range(lens_ref.shape[0]):
        total = total + lens_ref[c, item]
        ends.append(total)
    key_label = labels_of(lax.broadcasted_iota(jnp.int32, (span, lanes), 0), ends)
    query_label = labels_of(lax.broadcasted_iota(jnp.int32, (span, lanes), 1) % span, ends)
    return (key_label == query_label) | (key_label == -1)


VISUAL_BLOCKS = 4


def first_kernel(names, *refs):
    r = types.SimpleNamespace(**dict(zip(names, refs)))
    step = pl.program_id(0)
    last = pl.num_programs(0) - 1
    block, items, depth = r.visual.shape
    cols = r.so.shape[0]
    per = PEERS // 4
    rows = cols // per
    base = Spread.COPIES * (lax.axis_size("tensor") - 1)

    def at(shard, peer, half):
        return r.attn_v.at[peer // per, half_rows(shard * cols + (peer % per) * rows, rows, half)]

    def spread_to(where, n):
        return Spread(where, r.send, r.recv, n * base)

    attn = spread_to(at, 0)
    first_in, first_out, cross = (spread_to(eighth(ref), n + 1) for n, ref in enumerate((r.win, r.wout, r.cross)))
    text = [spread_to(one_shard(ref), n + 4) for n, ref in enumerate((r.tin, r.tout))]
    peer, tensor = attn.peer, attn.tensor
    hops = range(1, attn.shards)
    few = 2 * cols // PEERS

    def eighth_of(ref, first, count):
        return ref.at[pl.ds(pl.multiple_of(first, 16), count)]

    def start_attn(s):
        @pl.when(peer < 3 * per)
        def _():
            attn.along(s, eighth_of(r.qkv.at[peer // per], (peer % per) * rows, rows)).start()

        @pl.when(peer >= 3 * per)
        def _():
            attn.along(s, eighth_of(r.so, (peer - 3 * per) * rows, rows)).start()

    def start_cross(s):
        @pl.when(peer < PEERS // 2)
        def _():
            cross.along(s, eighth_of(r.cq, peer * few, few)).start()

        @pl.when(peer >= PEERS // 2)
        def _():
            cross.along(s, eighth_of(r.co, (peer - PEERS // 2) * few, few)).start()

    attn_any, cross_any = r.so.at[pl.ds(0, rows)], r.co.at[pl.ds(0, few)]
    in_mine, out_mine = (eighth(ref)(0, peer, None) for ref in (r.ffn_in_first, r.ffn_out_first))
    text_mine = [eighth(ref)(1, peer, None) for ref in (r.ffn_in, r.ffn_out)]
    here = pl.ds(pl.multiple_of(tensor * cols, 16), cols)
    own_copies = [
        pltpu.make_async_copy(source, goal, r.local.at[n])
        for n, (source, goal) in enumerate(
            [(r.qkv.at[c], r.attn_v.at[c, here]) for c in range(3)]
            + [
                (r.so, r.attn_v.at[3, here]),
                (r.cq, r.cross.at[tensor, pl.ds(0, cols)]),
                (r.co, r.cross.at[tensor, pl.ds(cols, cols)]),
                (r.ffn_in_first.at[0], r.win.at[tensor]),
                (r.ffn_out_first.at[0], r.wout.at[tensor]),
            ]
        )
    ]
    keep = pltpu.make_async_copy(r.attn_v, r.attn, r.local.at[len(own_copies)])

    @pl.when(step == 0)
    def _():
        greet(attn.targets())
        for s in hops:
            start_attn(s)
        for made in own_copies:
            made.start()
        low = 128
        r.w[:cols] = r.wkv[0]
        r.w[cols : 2 * cols - low] = r.wkv[1, low:]
        r.w[2 * cols - low :] = r.wkv[1, :low]

    def project(x, first, count):
        y = mm_nt(x, r.w[...])
        for tile in range(r.y.shape[0]):
            r.y[tile, : count * items] = y[:, tile * 128 : (tile + 1) * 128]
        for item in range(items):
            k_low, high, v_low = [
                r.y[tile, pl.ds(item, count, stride=items)].astype(NARROW) for tile in range(3)
            ]
            r.cross_k[item, first, :128] = k_low
            r.cross_k[item, first, 128:] = high[:, : cols - 128]
            r.cross_v[item, first, :128] = v_low
            r.cross_v[item, first, 128:] = high[:, cols - 128 :]

    @pl.when(step < VISUAL_BLOCKS)
    def _():
        project(
            r.visual[...].reshape(block * items, depth),
            pl.ds(pl.multiple_of(step * block, block), block),
            block,
        )

    @pl.when(step == VISUAL_BLOCKS - 1)
    def _():
        count = r.visual_tail.shape[0]
        project(
            r.visual_tail[...].reshape(count * items, depth),
            pl.ds(r.cross_k.shape[1] - count, count),
            count,
        )
        for s in hops:
            attn.along(s, attn_any).wait_recv()
            attn.start_across(s)
        for s in hops:
            start_cross(s)
        for s in hops:
            first_in.along(s, in_mine).start()
        for one, mine in zip(text, text_mine):
            one.along(FAR, mine).start()
        for s in hops:
            first_out.along(s, out_mine).start()
        for s in hops:
            attn.start_onward(s)
        for s in hops:
            attn.start_last(s)
        for s in hops:
            attn.finish(s)
            attn.along(s, attn_any).wait_send()
        for made in own_copies:
            made.wait()
        keep.start()

    @pl.when(step == VISUAL_BLOCKS + 1)
    def _():
        for s in hops:
            cross.along(s, cross_any).wait()
            cross.start_across(s)

    @pl.when(step == VISUAL_BLOCKS + 2)
    def _():
        for s in hops:
            first_in.along(s, in_mine).wait()
            first_in.start_across(s)

    @pl.when(step >= VISUAL_BLOCKS)
    def _():
        self_rows(r, step - VISUAL_BLOCKS)

    @pl.when(step == last)
    def _():
        for s in hops:
            cross.wait_across(s)
            cross.start_onward(s, True)
        for s in hops:
            first_in.wait_across(s)
            first_in.start_onward(s, True)
        for one, mine in zip(text, text_mine):
            one.along(FAR, mine).wait()
            one.start_across(FAR)
        for s in hops:
            cross.start_last(s)
        for s in hops:
            first_in.start_last(s)
        for s in hops:
            cross.finish(s, True)
            first_in.finish(s, True)
        for one in text:
            one.wait_across(FAR)
        for s in hops:
            first_out.along(s, out_mine).wait()
        keep.wait()


def self_rows(r, at):
    span = NQ + TXT
    items = r.hidden.shape[0] // span
    lanes = QUAD * HEAD
    x = r.hidden[...]
    r.q[...] = (mm_nt(x, r.attn_v[0]).astype(NARROW).astype(WIDE) * SCALE).astype(NARROW)
    r.k[...] = mm_nt(x, r.attn_v[1]).astype(NARROW)
    r.v[...] = mm_nt(x, r.attn_v[2]).astype(NARROW)

    units = []
    for item in range(items):
        rows = slice(item * span, (item + 1) * span)
        allowed = allowed_pairs(r.lens, at * items + item, span, lanes)
        for quad in range(r.hidden.shape[1] // lanes):
            units.append((rows, slice(quad * lanes, (quad + 1) * lanes), allowed))
    scores = [mm_nt(r.k[u, c], spread_heads(r.q[u, c], QUAD)) for u, c, _ in units]
    lows = []
    for value, (u, c, allowed) in zip(scores, units):
        value = jnp.where(allowed, value, MASKED_SCORE)
        lifted = jnp.exp(value - jnp.max(value, axis=0, keepdims=True))
        lows.append((lifted * (1.0 / jnp.sum(lifted, axis=0, keepdims=True))).astype(NARROW))
        r.p[u, c] = lows[-1]
    parts = [mm_tn(low, r.v[u, c]) for low, (u, c, _) in zip(lows, units)]
    for part, (u, c, _) in zip(parts, units):
        r.ctx[u, c] = gather_heads(part, QUAD).astype(NARROW)

    residue = x.astype(WIDE) + mm(r.ctx[...], r.attn_v[3])
    r.res[...] = residue
    unit, _ = norm_parts(residue)
    first = unit * r.gain[0:1] + r.shift[0:1]
    for item in range(items):
        r.fq[item * NQ : (item + 1) * NQ] = first[item * span : item * span + NQ]
        r.ft[item * TXT : (item + 1) * TXT] = first[item * span + NQ : (item + 1) * span]


def first_layer(hidden, lens, visual, wkv, qkv, so, cq, co, gain, shift, ffn_in, ffn_out, shards):
    rows, width = hidden.shape
    span, items, depth = visual.shape
    cols = so.shape[0]
    tail = span % (16 * VISUAL_BLOCKS)
    visual_block = (span - tail) // VISUAL_BLOCKS
    block = min(rows, 256)
    copies = 6 * Spread.COPIES * (shards - 1)
    dma = pltpu.SemaphoreType.DMA
    hbm = pl.BlockSpec(memory_space=pl.ANY)

    def later(i):
        return jnp.maximum(i - VISUAL_BLOCKS, 0)

    def whole(shape):
        return pl.BlockSpec(shape, lambda i: (0,) * len(shape), pipeline_mode=pl.Buffered(1))

    def by_rows(count, dtype=NARROW):
        return pl.BlockSpec((count, width), lambda i: (later(i), 0))

    def low(*shape):
        return jax.ShapeDtypeStruct(shape, NARROW)

    def wide(*shape):
        return jax.ShapeDtypeStruct(shape, WIDE)

    ins = dict(
        lens=(lens, pl.BlockSpec(memory_space=pltpu.SMEM)),
        hidden=(hidden, by_rows(block)),
        visual=(
            visual,
            pl.BlockSpec((visual_block, items, depth), lambda i: (jnp.minimum(i, VISUAL_BLOCKS - 1), 0, 0)),
        ),
        visual_tail=(visual, pl.BlockSpec((tail, items, depth), lambda i: (span // tail - 1, 0, 0))),
        wkv=(wkv, whole(wkv.shape)), qkv=(qkv, whole(qkv.shape)), so=(so, whole(so.shape)),
        cq=(cq, whole(cq.shape)), co=(co, whole(co.shape)), gain=(gain, whole(gain.shape)), shift=(shift, whole(shift.shape)),
        ffn_in_first=(ffn_in, whole((1,) + ffn_in.shape[1:])), ffn_out_first=(ffn_out, whole((1,) + ffn_out.shape[1:])),
        ffn_in=(ffn_in, hbm), ffn_out=(ffn_out, hbm),
    )
    kv = (items, span, cols)
    outs = dict(
        cross_k=(low(*kv), whole(kv)), cross_v=(low(*kv), whole(kv)),
        q=(low(rows, width), by_rows(block)), k=(low(rows, width), by_rows(block)), v=(low(rows, width), by_rows(block)),
        p=(low(rows, width), by_rows(block)), ctx=(low(rows, width), by_rows(block)),
        res=(wide(rows, width), by_rows(block)),
        fq=(wide(rows // 2, width), by_rows(block // 2)), ft=(wide(rows // 2, width), by_rows(block // 2)),
        attn=(low(4, shards * cols, width), hbm),
        win=(low(shards, *ffn_in.shape[1:]), hbm), wout=(low(shards, *ffn_out.shape[1:]), hbm),
        cross=(low(shards, 2 * cols, width), hbm),
        tin=(low(*ffn_in.shape[1:]), hbm), tout=(low(*ffn_out.shape[1:]), hbm),
    )
    scratch = dict(
        attn_v=pltpu.VMEM((4, shards * cols, width), NARROW),
        w=pltpu.VMEM((2 * cols, depth), NARROW),
        y=pltpu.VMEM((2 * cols // 128, visual_block * items, 128), WIDE),
        send=dma((copies,)), recv=dma((copies,)), local=dma((9,)),
    )
    names = tuple(ins) + tuple(outs) + tuple(scratch)
    values = pl.pallas_call(
        functools.partial(first_kernel, names),
        grid=(VISUAL_BLOCKS + rows // block,),
        in_specs=[spec for _, spec in ins.values()],
        out_specs=[spec for _, spec in outs.values()],
        out_shape=[shape for shape, _ in outs.values()],
        scratch_shapes=list(scratch.values()),
        compiler_params=pltpu.CompilerParams(
            collective_id=0, has_side_effects=True, vmem_limit_bytes=VMEM_BYTES
        ),
        name="first_layer",
    )(*[value for value, _ in ins.values()])
    return types.SimpleNamespace(**dict(zip(outs, values)))


def self_backward_kernel(
    x_ref, w_ref, gain_ref, res_ref, gq_ref, gt_ref, q_ref, k_ref, v_ref, p_ref, ctx_ref,
    kv_ref, cross_ref, piece0_ref, piece1_ref, piece2_ref, piece3_ref, other_gain, other_shift,
    grad_ref, kv_out, cq_out, co_out, qkv_out, so_out, rows_out, feed_total,
    down, dctx, dq, dk, dv, acc, gain_sums, shift_sums, grads_ref, *rest,
):
    parts = cross_parts(kv_ref.shape, cross_ref.shape)
    (kv_total, cross_total), land, higher = rest[:2], rest[2:5], rest[5:8]
    send, recv, feed_send, feed_recv, local = rest[8:13]
    own_total, own_land, own_higher, (own_send, own_recv) = rest[13], rest[14:16], rest[16:18], rest[18:20]
    few, few_land, few_send, few_recv, few_in = rest[20:]
    later = PeerSum(feed_parts(x_ref.shape[1]), (), (feed_total,), (), (), feed_send, feed_recv)
    peers = PeerSum(parts, (kv_ref, cross_ref), (kv_total, cross_total), land, higher, send, recv)
    last = PeerSum(
        self_parts(grads_ref.shape), (grads_ref,), (own_total,), own_land, own_higher, own_send, own_recv
    )
    span = NQ + TXT
    block = res_ref.shape[0]
    items = block // span
    lanes = QUAD * HEAD
    placed = [
        pltpu.make_async_copy(ref, later.rows((feed_total,), part, later.final_piece(part), 1), local.at[n])
        for n, (ref, part) in enumerate(zip((piece0_ref, piece1_ref, piece2_ref, piece3_ref), later.parts))
    ]
    step = pl.program_id(0)

    @pl.when(step == 0)
    def _():
        for made in placed:
            made.start()
        greet(peers.targets())
        peers.start_halving(0)
        for made in placed:
            made.wait()
        later.start_gathering(0)

    @pl.when(step == 1)
    def _():
        peers.end_halving(0)
        peers.start_halving(1)
        later.end_gathering(0)
        later.start_gathering(1)

    @pl.when(step == 2)
    def _():
        peers.end_halving(1)
        peers.start_halving(2)

    @pl.when(step == 3)
    def _():
        peers.end_halving(2)
        peers.far()
        peers.start_gathering(0)

    unit, inverse = norm_parts(res_ref[...])
    pieces = []
    for item in range(items):
        pieces.append(gq_ref[item * NQ : (item + 1) * NQ])
        pieces.append(gt_ref[item * TXT : (item + 1) * TXT])
    cotangent = jnp.concatenate(pieces, axis=0)
    grad_res = norm_back(unit, inverse, gain_ref[0:1], cotangent)
    gain_sum, shift_sum = column_sums(unit, cotangent)

    @pl.when(step == 0)
    def _():
        gain_sums[...] = gain_sum
        shift_sums[...] = shift_sum

    @pl.when(step > 0)
    def _():
        gain_sums[...] += gain_sum
        shift_sums[...] += shift_sum

    grad_ref[...] = grad_res
    low = grad_res.astype(NARROW)
    down[...] = low
    dctx[...] = mm_nt(low, w_ref[3]).astype(NARROW)

    units = [
        (slice(item * span, (item + 1) * span), slice(quad * lanes, (quad + 1) * lanes))
        for item in range(items)
        for quad in range(w_ref.shape[2] // lanes)
    ]
    for at in range(0, len(units), UNITS):
        some = units[at : at + UNITS]
        spread = [spread_heads(dctx[u], QUAD) for u in some]
        grad_chances = [mm_nt(v_ref[u], one) for u, one in zip(some, spread)]
        scores = []
        for u, value in zip(some, grad_chances):
            weighted = p_ref[u].astype(WIDE)
            inner = jnp.sum(value * weighted, axis=0, keepdims=True)
            scores.append((weighted * (value - inner)).astype(NARROW))
        for u, one in zip(some, spread):
            dv[u] = mm(p_ref[u], one).astype(NARROW)
        for u, one in zip(some, scores):
            dk[u] = mm(one, spread_heads(q_ref[u], QUAD)).astype(NARROW)
        values = [mm_tn(one, k_ref[u]) for u, one in zip(some, scores)]
        for u, value in zip(some, values):
            dq[u] = (gather_heads(value, QUAD) * SCALE).astype(NARROW)

    grad_ref[...] += mm(dq[...], w_ref[0]) + mm(dk[...], w_ref[1]) + mm(dv[...], w_ref[2])

    own = lax.axis_index("tensor")
    cols = grads_ref.shape[0] // 4
    window = acc.shape[1]
    start = pl.multiple_of((own * cols) // 128 * 128, 128)
    here = pl.ds(start, window)
    x = x_ref[...]
    products = (
        mm_tn(dq[:, here], x), mm_tn(dk[:, here], x), mm_tn(dv[:, here], x),
        mm_tn(ctx_ref[:, here], down[...]),
    )

    @pl.when(step == 0)
    def _():
        for c, product in enumerate(products):
            acc[c] = product

    @pl.when(step > 0)
    def _():
        for c, product in enumerate(products):
            acc[c] += product

    @pl.when(step == pl.num_programs(0) - 1)
    def _():
        offset = pl.multiple_of(own * cols - start, 64)
        for c in range(4):
            grads_ref[c * cols : (c + 1) * cols] = acc[c, pl.ds(offset, cols), :].astype(NARROW)
        last.start_halving(0)
        few_in[0:1] = gain_sums[...]
        few_in[1:4] = other_gain[...]
        few_in[4:5] = shift_sums[...]
        few_in[5:8] = other_shift[...]
        few_steps = sum_rows(few_in, few, few_land, few_send, few_recv)
        few_steps[0]()
        peers.end_gathering(0)
        last.end_halving(0)
        last.start_halving(1)
        peers.start_gathering(1)
        few_steps[1]()
        later.end_gathering(1)
        later.start_gathering(2)
        last.end_halving(1)
        last.start_halving(2)
        for run in few_steps[2:]:
            run()
        rows_out[...] = few[few.shape[0] - 1]
        peers.end_gathering(1)
        peers.start_gathering(2)
        last.end_halving(2)
        last.far()
        last.start_gathering(0)
        peers.end_gathering(2)
        kv_out[0] = kv_total[:cols]
        kv_out[1, 128:] = kv_total[cols : 2 * cols - 128]
        kv_out[1, :128] = kv_total[2 * cols - 128 :]
        last.end_gathering(0)
        last.start_gathering(1)
        cq_out[...] = cross_total[:cols]
        co_out[...] = cross_total[cols:]
        last.end_gathering(1)
        last.start_gathering(2)
        later.end_gathering(2)
        last.end_gathering(2)
        for c in range(3):
            qkv_out[c] = own_total[c * cols : (c + 1) * cols]
        so_out[...] = own_total[3 * cols :]


def self_backward(
    hidden, weights, gain, residue, grad_q, grad_t, q, k, v, p, ctx, kv, cross, pieces, gains, shifts,
    cols, ident, peers
):
    rows, width = hidden.shape
    block = min(rows, 256)
    half = block // 2
    full = pl.BlockSpec((block, width), lambda i: (i, 0))
    halves = pl.BlockSpec((half, width), lambda i: (i, 0))
    parts = cross_parts(kv.shape, cross.shape)
    far = (peers // PEERS - 1).bit_length()
    depth = kv.shape[1]
    own = (4 * cols, width)
    steps = 3 + far
    hbm = pl.BlockSpec(memory_space=pl.ANY)
    dma = pltpu.SemaphoreType.DMA
    count = PeerSum.copies(feed_parts(width), far)

    def whole(shape):
        return pl.BlockSpec(shape, lambda i: (0,) * len(shape), pipeline_mode=pl.Buffered(1))

    def wide(*shape):
        return jax.ShapeDtypeStruct(shape, WIDE)

    totals = [
        jax.ShapeDtypeStruct(dims, NARROW)
        for dims in ((2, cols, depth), (cols, width), (cols, width), (3, cols, width), (cols, width))
    ] + [wide(8, width)]
    return pl.pallas_call(
        self_backward_kernel,
        grid=(rows // block,),
        in_specs=[
            full,
            whole(weights.shape),
            pl.BlockSpec(gain.shape, lambda i: (0, 0)),
            full, halves, halves, full, full, full, full, full,
        ]
        + [whole(a.shape) for a in (kv, cross, *pieces, gains, shifts)],
        out_specs=[full] + [whole(t.shape) for t in totals] + [hbm],
        out_shape=[wide(rows, width)] + totals + [jax.ShapeDtypeStruct((4 * width, width), NARROW)],
        scratch_shapes=[pltpu.VMEM((block, width), NARROW)] * 5
        + [pltpu.VMEM((4, (cols + 64 + 127) // 128 * 128, width), WIDE)]
        + [pltpu.VMEM((1, width), WIDE)] * 2
        + [pltpu.VMEM(own, NARROW)]
        + peer_scratch(parts, [kv.shape, cross.shape], far)
        + [dma((count,)), dma((count,)), dma((4,))]
        + peer_scratch(self_parts(own), [own], far)
        + [pltpu.VMEM((steps, 8, width), WIDE)] * 2
        + [dma((steps,)), dma((steps,)), pltpu.VMEM((8, width), WIDE)],
        compiler_params=pltpu.CompilerParams(
            collective_id=ident, has_side_effects=True, vmem_limit_bytes=VMEM_BYTES
        ),
        name="self_backward",
    )(hidden, weights, gain, residue, grad_q, grad_t, q, k, v, p, ctx, kv, cross, *pieces, gains, shifts)


def feed_parts(width):
    return tuple((0, n * width, width // PIECES, 0, width, n // 2) for n in range(4))


LOADS = (
    "fq", "wq_own", "k", "v", "ft", "tin", "tout", "cotq", "tcot", "wo_own", "w_all", "tin2", "tout2",
)
STORES = ("outq", "outt", "gq", "gt", "grads", "kv", "piece0", "piece1", "piece2", "piece3")


def middle_kernel(names, *refs):
    r = types.SimpleNamespace(**dict(zip(names, refs)))
    cols = r.wq_own.shape[0]
    heads = cols // HEAD
    items, span = r.k.shape[:2]
    width = r.fq.shape[1]
    depth = r.visual.shape[2]
    chunks = r.win.shape[0]
    tensor = lax.axis_index("tensor")
    sources = dict(
        tin=r.ffn_in.at[1], tout=r.ffn_out.at[1],
        w_all=r.cross_o.at[:, pl.ds(cols, cols)], tin2=r.tin2_o, tout2=r.tout2_o,
        cotq=r.cot.at[:, pl.ds(0, NQ)], tcot=r.cot.at[:, pl.ds(NQ, TXT)],
    )
    rows = [slice(item * NQ, (item + 1) * NQ) for item in range(items)]
    tall = r.fq.shape

    def load(name, goal=None):
        return pltpu.make_async_copy(
            sources.get(name, getattr(r, name, None)),
            getattr(r, name + "_v") if goal is None else goal,
            r.load_sem.at[LOADS.index(name)],
        )

    def store(name, source):
        return pltpu.make_async_copy(source, getattr(r, name + "_o"), r.store_sem.at[STORES.index(name)])

    pair = (lax.axis_index("dp"), tensor + 1 - 2 * (tensor % 2))
    swaps = [remote(r.tpart.at[n], r.tland.at[n], r.swap_send.at[n], r.swap_recv.at[n], pair) for n in range(2)]
    forth = HeadGather(r.heads1, r.head_send1, r.head_recv1)
    gather = HeadGather(r.heads2, r.head_send2, r.head_recv2)
    base = Spread.COPIES * (chunks - 1)
    hops = range(1, chunks)
    first_out = Spread(eighth(r.wout_o), r.spread_send, r.spread_recv, base)
    text = [
        Spread(one_shard(ref), r.spread_send, r.spread_recv, n * base) for n, ref in ((3, r.tin2_o), (4, r.tout2_o))
    ]
    parts = feed_parts(width)
    kind_parts = ((0, 0, width // PIECES, 0, width, 0), (0, width, width // PIECES, 0, width, 1))
    feed_q = [None]
    pieces = (r.piece0, r.piece1, r.piece2, r.piece3)
    peers_q, peers_t = (
        PeerSum(
            kind_parts, source, (), r.land[kind::2], r.higher[kind::2], r.peer_send, r.peer_recv,
            kind * PeerSum.copies(kind_parts, len(PeerSum.far_bits())), pieces[kind::2],
        )
        for kind, source in enumerate((feed_q, (r.feed_t,)))
    )

    early = ("tin_v", "tout_v", "tin2_v", "tout2_v", "tslope", "tslope2", "cotq_v", "tcot_v")

    def to_feed_forward(*buffers):
        for name, buffer in zip(early, buffers):
            setattr(r, name, buffer)
        for name in LOADS[:11]:
            load(name).start()
        greet(first_out.along_targets() + peers_q.targets())
        for s in hops:
            first_out.start_across(s)
        for one in text:
            one.start_onward(FAR, True)
        for name in ("fq", "wq_own", "k", "v"):
            load(name).wait()
        r.q[...] = (
            mm_nt(r.fq_v[...].astype(NARROW), r.wq_own_v[...]).astype(NARROW).astype(WIDE) * SCALE
        ).astype(NARROW)
        for half in range(2):
            some = range(half * items // 2, (half + 1) * items // 2)
            scores = [mm_nt(r.k_v[item], spread_heads(r.q[rows[item]], heads)) for item in some]
            lows = []
            for item, value in zip(some, scores):
                lifted = jnp.exp(value - jnp.max(value, axis=0, keepdims=True))
                lows.append((lifted * (1.0 / jnp.sum(lifted, axis=0, keepdims=True))).astype(NARROW))
                r.p[item] = lows[-1]
            values = [mm_tn(low, r.v_v[item]) for item, low in zip(some, lows)]
            for item, value in zip(some, values):
                r.ctx[rows[item]] = gather_heads(value, heads).astype(NARROW)
            count = items // 2 * NQ
            here = slice(half * count, (half + 1) * count)
            forth.put(half, r.ctx[here])
            forth.start(half)
        def text_part(win, wout, slope_v, act_v):
            act, slope = gelu_parts(mm(r.ft_v[...].astype(NARROW), win[...]))
            slope_v[...] = slope.astype(NARROW)
            act = act.astype(NARROW)
            if act_v is not None:
                act_v[...] = act
            return mm(act, wout[...])

        for name in ("ft", "tin", "tout"):
            load(name).wait()
        r.gt_v[...] = text_part(r.tin_v, r.tout_v, r.tslope, r.tact)
        for s in hops:
            first_out.start_onward(s)
        for one in text:
            one.start_last(FAR)
        for one in text:
            one.finish(FAR, True)
        load("tin2").start()
        load("tout2").start()
        forth.wait(0)
        for s in hops:
            first_out.start_last(s)
        forth.wait(1)
        load("w_all").wait()
        r.gq_v[...] = forth.product(r.w_all_v)
        sources["w_all"] = r.cross_o.at[:, pl.ds(0, cols)]
        load("w_all").start()
        load("tin2").wait()
        load("tout2").wait()
        r.tpart[0] = (r.gt_v[...] + text_part(r.tin2_v, r.tout2_v, r.tslope2, None)).astype(NARROW)
        swaps[0].start()

        def text_rows():
            load("tcot").wait()
            unit, inverse = norm_parts(r.ft_v[...] + r.tpart[0].astype(WIDE) + r.tland[0].astype(WIDE))
            r.outt[...] = (unit * r.gain[3:4] + r.shift[3:4]).astype(NARROW)
            store("outt", r.outt).start()
            cotangent = r.tcot_v[...].astype(WIDE).reshape(tall)
            gain_sum, shift_sum = column_sums(unit, cotangent)
            r.gains[2:3] = gain_sum
            r.shifts[2:3] = shift_sum
            grad = norm_back(unit, inverse, r.gain[3:4], cotangent)
            r.gt_v[...] = grad
            r.ttop[...] = grad.astype(NARROW)
            r.tdpre[...] = (mm_nt(r.ttop[...], r.tout_v[...]) * r.tslope[...].astype(WIDE)).astype(NARROW)
            far = (mm_nt(r.ttop[...], r.tout2_v[...]) * r.tslope2[...].astype(WIDE)).astype(NARROW)
            r.tpart[1] = (mm_nt(r.tdpre[...], r.tin_v[...]) + mm_nt(far, r.tin2_v[...])).astype(NARROW)
            swaps[1].start()
            r.feed_t[:width] = mm_tn(r.ft_v[...].astype(NARROW), r.tdpre[...]).astype(NARROW)
            r.feed_t[width:] = mm_tn(r.tact[...], r.ttop[...]).astype(NARROW)
            peers_t.start_halving(0)

        def query_rows(slopes, total, weights, outq):
            def fetch(j):
                slot, chunk = j % 2, j % chunks
                return [
                    pltpu.make_async_copy(ref.at[chunk], weights.at[slot, n], r.weight_sem.at[slot, n])
                    for n, ref in enumerate((r.win_o, r.wout_o))
                ]

            unit, _ = norm_parts(r.fq_v[...] + r.gq_v[...])
            value = unit * r.gain[1:2] + r.shift[1:2]
            r.low[...] = value.astype(NARROW)
            total[...] = value
            for s in hops:
                first_out.finish(s)
            for made in fetch(0):
                made.start()

            def next_weights(j):
                for made in fetch(j):
                    made.wait()

                @pl.when(j + 1 < 2 * chunks)
                def _():
                    for made in fetch(j + 1):
                        made.start()

                return weights.at[j % 2, 0], weights.at[j % 2, 1]

            @pl.loop(0, chunks)
            def _(j):
                win, wout = next_weights(j)
                act, slope = gelu_parts(mm(r.low[...], win[...]))
                slopes[j] = slope.astype(NARROW)
                act = act.astype(NARROW)
                total[...] += mm(act, wout[...])

                @pl.when(j == tensor)
                def _():
                    r.act[...] = act


            unit, inverse = norm_parts(total[...])
            outq[...] = (unit * r.gain[2:3] + r.shift[2:3]).astype(NARROW)
            store("outq", outq).start()
            load("cotq").wait()
            cotangent = r.cotq_v[...].astype(WIDE).reshape(tall)
            gain_sum, shift_sum = column_sums(unit, cotangent)
            r.gains[1:2] = gain_sum
            r.shifts[1:2] = shift_sum
            grad = norm_back(unit, inverse, r.gain[2:3], cotangent)
            total[...] = grad
            r.top[...] = grad.astype(NARROW)

            @pl.loop(chunks, 2 * chunks)
            def _(j):
                win, wout = next_weights(j)
                chunk = j - chunks
                dpre = (mm_nt(r.top[...], wout[...]) * slopes[chunk].astype(WIDE)).astype(NARROW)
                total[...] += mm_nt(dpre, win[...])

                @pl.when(chunk == tensor)
                def _():
                    r.dpre[...] = dpre

                @pl.when(chunk == 2)
                def _():
                    swaps[0].wait()
                    text_rows()


            grad_second = total[...]
            unit, inverse = norm_parts(r.fq_v[...] + r.gq_v[...])
            gain_sum, shift_sum = column_sums(unit, grad_second)
            r.gains[0:1] = gain_sum
            r.shifts[0:1] = shift_sum
            grad = norm_back(unit, inverse, r.gain[1:2], grad_second)
            r.gq_v[...] = grad
            r.down[...] = grad.astype(NARROW)
            store("outq", outq).wait()

        pl.run_scoped(
            query_rows,
            pltpu.VMEM((chunks, tall[0], r.win.shape[2]), NARROW),
            pltpu.VMEM(tall, WIDE),
            pltpu.VMEM((2, 2) + r.win.shape[1:], NARROW),
            pltpu.VMEM(tall, NARROW),
        )

    inner, outer = r.ffn_in.shape[1:], r.ffn_out.shape[1:]
    pl.run_scoped(
        to_feed_forward,
        *[pltpu.VMEM(shape, NARROW) for shape in (inner, outer, inner, outer, (tall[0], inner[1]), (tall[0], inner[1]), (items, NQ, width), (items, TXT, width))],
    )

    def query_gradients(goal):
        feed_q[0] = goal
        goal[:width] = mm_tn(r.low[...], r.dpre[...]).astype(NARROW)
        goal[width:] = mm_tn(r.act[...], r.top[...]).astype(NARROW)
        peers_q.start_halving(0)

    def cross_rows(dctx, dq, score, dkv, acc, x, x_tail, kv, feed_v):
        group = items // 4
        steps = VISUAL_STEPS
        tail = span % steps
        block = (span - tail) // steps

        def fetch(j):
            return pltpu.make_async_copy(r.visual.at[pl.ds(j * block, block)], x.at[j % 2], r.x_sem.at[j % 2])

        rest = pltpu.make_async_copy(r.visual.at[pl.ds(span - tail, tail)], x_tail, r.x_sem.at[2])
        fetch(0).start()
        rest.start()
        query_gradients(feed_v)
        peers_t.end_halving(0)
        peers_t.start_halving(1)
        load("wo_own").wait()
        dctx[...] = mm_nt(r.down[...], r.wo_own_v[...]).astype(NARROW)
        for g in range(4):
            some = range(g * group, (g + 1) * group)
            spread = [spread_heads(dctx[rows[item]], heads) for item in some]
            grad_chances = [mm_nt(r.v_v[item], one) for item, one in zip(some, spread)]
            scores = []
            for item, value in zip(some, grad_chances):
                weighted = r.p[item].astype(WIDE)
                inner = jnp.sum(value * weighted, axis=0, keepdims=True)
                scores.append((weighted * (value - inner)).astype(NARROW))
                score[item] = scores[-1]
            values = [mm_tn(one, r.k_v[item]) for item, one in zip(some, scores)]
            for item, value in zip(some, values):
                dq[rows[item]] = (gather_heads(value, heads) * SCALE).astype(NARROW)
            if g % 2:
                count = 2 * group * NQ
                here = slice(g // 2 * count, (g // 2 + 1) * count)
                gather.put(g // 2, dq[here])
                gather.start(g // 2)
        peers_q.end_halving(0)
        peers_q.start_halving(1)
        none = jnp.zeros((QUAD * NQ, cols), NARROW)
        for g in range(4):
            some = range(g * group, (g + 1) * group)
            both = []
            for item in some:
                one = spread_heads(dctx[rows[item]], heads)
                both.append(
                    mm(
                        jnp.concatenate([score[item], r.p[item]], axis=1),
                        jnp.concatenate(
                            [
                                jnp.concatenate([spread_heads(r.q[rows[item]], heads), none], axis=1),
                                jnp.concatenate([none, one[:, 128:], one[:, :128]], axis=1),
                            ],
                            axis=0,
                        ),
                    )
                )
            for item, value in zip(some, both):
                for tile in range(dkv.shape[0]):
                    dkv[tile, pl.ds(item, span, stride=items)] = value[:, tile * 128 : (tile + 1) * 128]
        r.grads[:cols] = mm_tn(dq[...], r.fq_v[...].astype(NARROW)).astype(NARROW)
        r.grads[cols:] = mm_tn(r.ctx[...], r.down[...]).astype(NARROW)
        store("grads", r.grads).start()

        def product(first, count, value):
            grads = [dkv[tile, pl.ds(first, count)].astype(NARROW) for tile in range(dkv.shape[0])]
            return mm_tn(jnp.concatenate(grads, axis=1), value.reshape(count, depth))

        rest.wait()
        acc[...] = product((span - tail) * items, tail * items, x_tail[...])

        @pl.loop(0, steps)
        def _(j):
            fetch(j).wait()

            @pl.when(j + 1 < steps)
            def _():
                fetch(j + 1).start()

            acc[...] += product(pl.multiple_of(j * block * items, 16), block * items, x[j % 2])

            @pl.when(j == 1)
            def _():
                peers_t.end_halving(1)
                peers_t.start_halving(2)

            @pl.when(j == 4)
            def _():
                peers_q.end_halving(1)
                peers_q.start_halving(2)

        kv[...] = acc[...].astype(kv.dtype)
        store("kv", kv).start()
        gather.wait(0)
        gather.wait(1)
        load("w_all").wait()
        r.gq_v[...] += gather.product(r.w_all_v)
        store("gq", r.gq_v).start()
        swaps[1].wait()
        r.gt_v[...] += r.tpart[1].astype(WIDE) + r.tland[1].astype(WIDE)
        store("gt", r.gt_v).start()
        for one in (peers_t, peers_q):
            one.end_halving(2)
            one.far()
        for n, piece in enumerate(pieces):
            store("piece%d" % n, piece).start()
        store("kv", kv).wait()

    pl.run_scoped(
        cross_rows,
        pltpu.VMEM((tall[0], cols), NARROW),
        pltpu.VMEM((tall[0], cols), NARROW),
        pltpu.VMEM((items, span, QUAD * NQ), NARROW),
        pltpu.VMEM((2 * cols // 128, items * span, 128), WIDE),
        pltpu.VMEM((2 * cols, depth), WIDE),
        pltpu.VMEM((2, span // VISUAL_STEPS, items, depth), NARROW),
        pltpu.VMEM((span % VISUAL_STEPS, items, depth), NARROW),
        pltpu.VMEM((2 * cols, depth), NARROW),
        pltpu.VMEM((2 * width, width), NARROW),
    )
    for name, source in (
        ("outt", r.outt), ("gq", r.gq_v), ("gt", r.gt_v), ("grads", r.grads),
        ("piece0", r.piece0), ("piece1", r.piece1), ("piece2", r.piece2), ("piece3", r.piece3),
    ):
        store(name, source).wait()


def middle(arrays, ident, peers):
    rows, width = arrays["fq"].shape
    cols = arrays["wq_own"].shape[0]
    items, span = arrays["k"].shape[:2]
    hidden = arrays["ffn_in"].shape[2]
    depth = arrays["visual"].shape[2]
    shards = arrays["win"].shape[0]
    far = (peers // PEERS - 1).bit_length()
    parts = feed_parts(width)
    piece = (parts[0][2], width)
    dma = pltpu.SemaphoreType.DMA
    hbm, vmem = pl.BlockSpec(memory_space=pl.ANY), pl.BlockSpec(memory_space=pltpu.VMEM)

    def low(*dims):
        return pltpu.VMEM(dims, NARROW)

    def wide(*dims):
        return pltpu.VMEM(dims, WIDE)

    out = jax.ShapeDtypeStruct
    outs = dict(
        outq_o=out((rows, width), NARROW), outt_o=out((rows, width), NARROW),
        gq_o=out((rows, width), WIDE), gt_o=out((rows, width), WIDE),
        grads_o=out((2 * cols, width), NARROW), kv_o=out((2 * cols, depth), NARROW),
        piece0_o=out(piece, NARROW), piece1_o=out(piece, NARROW), piece2_o=out(piece, NARROW), piece3_o=out(piece, NARROW),
        gains=out((3, width), WIDE), shifts=out((3, width), WIDE),
        win_o=out(arrays["win"].shape, NARROW), wout_o=out(arrays["wout"].shape, NARROW),
        cross_o=out(arrays["cross_w"].shape, NARROW),
        tin2_o=out(arrays["tin2"].shape, NARROW), tout2_o=out(arrays["tout2"].shape, NARROW),
    )
    copies = feed_copies(shards)
    total = peer_scratch(parts, [], far)
    scratch = dict(
        fq_v=wide(rows, width), wq_own_v=low(cols, width), wo_own_v=low(cols, width),
        k_v=low(*arrays["k"].shape), v_v=low(*arrays["v"].shape), ft_v=wide(rows, width),
        w_all_v=low(shards, cols, width),
        q=low(rows, cols), ctx=low(rows, cols), p=low(items, span, QUAD * NQ),
        tact=low(rows, hidden),
        low=low(rows, width), top=low(rows, width), down=low(rows, width),
        act=low(rows, hidden), dpre=low(rows, hidden),
        ttop=low(rows, width), tdpre=low(rows, hidden), outt=low(rows, width),
        gq_v=wide(rows, width), gt_v=wide(rows, width), grads=low(2 * cols, width),
        tpart=low(2, rows, width), tland=low(2, rows, width), swap_send=dma((2,)), swap_recv=dma((2,)),
        heads1=low(shards, rows * cols // 128, 128), head_send1=dma((2, shards)), head_recv1=dma((2, shards)),
        heads2=low(shards, rows * cols // 128, 128), head_send2=dma((2, shards)), head_recv2=dma((2, shards)),
        spread_send=dma((copies,)), spread_recv=dma((copies,)),
        feed_t=low(2 * width, width), piece0=low(*piece), piece1=low(*piece), piece2=low(*piece), piece3=low(*piece),
        land=total[:4], higher=total[4:8], peer_send=total[8], peer_recv=total[9],
        load_sem=dma((len(LOADS),)), store_sem=dma((len(STORES),)), weight_sem=dma((2, 2)), x_sem=dma((3,)),
    )
    names = tuple(arrays) + tuple(outs) + tuple(scratch)
    return dict(
        zip(
            outs,
            pl.pallas_call(
                functools.partial(middle_kernel, names),
                in_specs=[vmem if name in ("gain", "shift") else hbm for name in arrays],
                out_specs=[vmem if name in ("gains", "shifts") else hbm for name in outs],
                out_shape=list(outs.values()),
                input_output_aliases={
                    list(arrays).index(a): list(outs).index(b)
                    for a, b in (
                        ("win", "win_o"), ("wout", "wout_o"), ("cross_w", "cross_o"), ("tin2", "tin2_o"), ("tout2", "tout2_o"),
                    )
                },
                scratch_shapes=list(scratch.values()),
                compiler_params=pltpu.CompilerParams(
                    collective_id=ident, has_side_effects=True, vmem_limit_bytes=62 * 2**20
                ),
                name="middle",
            )(*arrays.values()),
        )
    )


def on_device(
    hidden_in,
    visual_feats,
    caption_lengths,
    self_qkv,
    self_out,
    cross_query,
    cross_kv,
    cross_out,
    ffn_in,
    ffn_out,
    norm_gain,
    norm_shift,
    out_grad,
):
    items = visual_feats.shape[0]
    rows, width = hidden_in.shape
    span = rows // items
    cols = self_qkv.shape[2]
    shards = lax.axis_size("tensor")

    visual = jnp.swapaxes(visual_feats, 0, 1)
    cross_wq = jnp.swapaxes(cross_query, 0, 1)
    first = first_layer(
        hidden_in, jnp.swapaxes(caption_lengths, 0, 1), visual, jnp.swapaxes(cross_kv, 1, 2), jnp.swapaxes(self_qkv, 1, 2),
        self_out, cross_wq, cross_out, norm_gain, norm_shift, ffn_in, ffn_out, shards,
    )
    peers = lax.axis_size("dp")
    mid = middle(
        dict(
            fq=first.fq, wq_own=cross_wq, k=first.cross_k, v=first.cross_v, ft=first.ft,
            cot=out_grad.reshape(items, span, width), wo_own=cross_out, ffn_in=ffn_in, ffn_out=ffn_out, win=first.win,
            wout=first.wout, cross_w=first.cross, tin2=first.tin, tout2=first.tout, visual=visual,
            gain=norm_gain, shift=norm_shift,
        ),
        2, peers,
    )
    out_q, out_t, g_cross, g_kv = mid["outq_o"], mid["outt_o"], mid["grads_o"], mid["kv_o"]
    grad_hidden, g_kv, g_cq, g_co, g_qkv, g_so, gains, g_feed = self_backward(
        hidden_in, first.attn, norm_gain, first.res, mid["gq_o"], mid["gt_o"], first.q, first.k, first.v, first.p, first.ctx,
        g_kv, g_cross,
        [mid["piece%d_o" % n] for n in range(4)], mid["gains"], mid["shifts"], cols, 6, peers,
    )
    g_feed = g_feed.reshape(2, 2, width, width).astype(WIDE)
    g_in, g_out = g_feed[0], g_feed[1]
    g_kv, g_cq, g_co, g_qkv, g_so = [g.astype(WIDE) for g in (g_kv, g_cq, g_co, g_qkv, g_so)]
    out = jnp.concatenate(
        [out_q.reshape(items, NQ, width), out_t.reshape(items, TXT, width)], axis=1
    ).reshape(rows, width)
    return (
        out,
        grad_hidden,
        jnp.swapaxes(g_qkv, 1, 2),
        g_so,
        jnp.swapaxes(g_cq, 0, 1),
        jnp.swapaxes(g_kv, 1, 2),
        g_co,
        g_in,
        g_out,
        gains[:4],
        gains[4:],
    )


def solution(mesh):
    placed = (
        P("dp", None),
        P("dp", None, None),
        P("dp", None),
        P(None, None, "tensor"),
        P("tensor", None),
        P(None, "tensor"),
        P(None, None, "tensor"),
        P("tensor", None),
        P(None, None, "tensor"),
        P(None, "tensor", None),
        P(),
        P(),
        P("dp", None),
    )
    return jax.shard_map(
        on_device,
        mesh=mesh,
        in_specs=placed,
        out_specs=(
            P("dp", None),
            P("dp", None),
            P(None, None, "tensor"),
            P("tensor", None),
            P(None, "tensor"),
            P(None, None, "tensor"),
            P("tensor", None),
            P(None, None, "tensor"),
            P(None, "tensor", None),
            P(),
            P(),
        ),
        check_vma=False,
    )
```

```python
import functools
import math
import types

import jax
import jax.numpy as jnp
from jax import lax
from jax.experimental import pallas as pl
from jax.experimental.pallas import tpu as pltpu
from jax.sharding import PartitionSpec as P

HEAD = 64
NQ = 32
TXT = 32
QUAD = 4
UNITS = 12
VISUAL_STEPS = 8
EPSILON = 1e-06
MASKED_SCORE = -1e30
SCALE = 1.0 / math.sqrt(HEAD)
WIDE = jnp.float32
NARROW = jnp.bfloat16
VMEM_BYTES = 60 * 2**20


def mm(a, b):
    return lax.dot_general(a, b, (((1,), (0,)), ((), ())), preferred_element_type=WIDE)


def mm_nt(a, b):
    return lax.dot_general(a, b, (((1,), (1,)), ((), ())), preferred_element_type=WIDE)


def mm_tn(a, b):
    return lax.dot_general(a, b, (((0,), (0,)), ((), ())), preferred_element_type=WIDE)


def lane_group(rows, lanes, size):
    return lax.broadcasted_iota(jnp.int32, (rows, lanes), 1) // size


def spread_heads(block, count):
    group = lane_group(1, block.shape[1], HEAD)
    return jnp.concatenate(
        [block * jnp.where(group == h, 1.0, 0.0).astype(NARROW) for h in range(QUAD)], axis=0
    )


def gather_heads(block, count):
    rows, lanes = block.shape[0] // QUAD, block.shape[1]
    group = lane_group(rows, lanes, HEAD)
    out = block[:rows]
    for h in range(1, count):
        out = jnp.where(group == h, block[h * rows : (h + 1) * rows], out)
    return out


def norm_parts(residue):
    mean = jnp.mean(residue, axis=-1, keepdims=True)
    centered = residue - mean
    variance = jnp.mean(centered * centered, axis=-1, keepdims=True)
    inverse = lax.rsqrt(variance + EPSILON)
    return centered * inverse, inverse


def norm_back(unit, inverse, gain_row, cotangent):
    scaled = gain_row * cotangent
    first = jnp.mean(scaled, axis=-1, keepdims=True)
    second = jnp.mean(scaled * unit, axis=-1, keepdims=True)
    return inverse * (scaled - first - unit * second)


def column_sums(unit, cotangent):
    return (
        jnp.sum(cotangent * unit, axis=0, keepdims=True),
        jnp.sum(cotangent, axis=0, keepdims=True),
    )


def gelu_parts(pre):
    bell = jnp.exp(-0.5 * pre * pre)
    half = 0.5 * lax.erf(pre * math.sqrt(0.5)) + 0.5
    return pre * half, half + pre * bell * (1.0 / math.sqrt(2.0 * math.pi))


MESH = pl.DeviceIdType.MESH
PEERS = 8


def flip(index, bit):
    return index + bit - 2 * bit * ((index // bit) % 2)


def greet(targets):
    barrier = pltpu.get_barrier_semaphore()
    for target in targets:
        pl.semaphore_signal(barrier, inc=1, device_id=target, device_id_type=MESH)
    pl.semaphore_wait(barrier, len(targets))


def remote(src, dst, send, recv, target):
    return pltpu.make_async_remote_copy(
        src_ref=src, dst_ref=dst, send_sem=send, recv_sem=recv, device_id=target, device_id_type=MESH
    )


class Spread:
    COPIES = 9

    def __init__(self, at, send, recv, base):
        self.at, self.send, self.recv, self.base = at, send, recv, base
        self.dp, self.tensor = lax.axis_index("dp"), lax.axis_index("tensor")
        self.shards = lax.axis_size("tensor")
        self.peer = self.dp % PEERS

    def hop(self, slot, s, src, dst, target):
        index = self.base + (s - 1) * self.COPIES + slot
        return remote(src, dst, self.send.at[index], self.recv.at[index], target)

    def came(self, s):
        return (self.tensor + self.shards - s) % self.shards

    def along(self, s, own):
        return self.hop(0, s, own, self.at(self.tensor, self.peer, None), (self.dp, (self.tensor + s) % self.shards))

    def hand(self, slot, s, bit, peer, half):
        place = self.at(self.came(s), peer, half)
        return self.hop(slot, s, place, place, (flip(self.dp, bit), self.tensor))

    def across(self, s):
        return [self.hand(1, s, 2, self.peer, None), self.hand(2, s, 4, self.peer, None), self.hand(3, s, 1, self.peer, None)]

    def onward(self, s):
        x, y = flip(self.peer, 2), flip(self.peer, 4)
        return (
            [self.hand(4, s, 4, x, 0), self.hand(5, s, 1, x, None)],
            [self.hand(6, s, 2, y, 1), self.hand(7, s, 1, y, None)],
        )

    def last(self, s):
        return self.hand(8, s, 1, flip(flip(self.peer, 2), 4), None)

    def start_across(self, s):
        for made in self.across(s):
            made.start()

    def wait_across(self, s):
        for made in self.across(s):
            made.wait()

    def start_onward(self, s, arrived=False):
        over_x, over_y, _ = self.across(s)
        by_x, by_y = self.onward(s)
        if not arrived:
            over_x.wait_recv()
        for made in by_x:
            made.start()
        if not arrived:
            over_y.wait_recv()
        for made in by_y:
            made.start()

    def start_last(self, s):
        by_x, by_y = self.onward(s)
        by_x[0].wait_recv()
        by_y[0].wait_recv()
        self.last(s).start()

    def finish(self, s, arrived=False):
        over = self.across(s)
        by_x, by_y = self.onward(s)
        final = self.last(s)
        for made in ([] if arrived else [over[2]]) + [by_x[1], by_y[1], final]:
            made.wait_recv()
        for made in ([] if arrived else over) + by_x + by_y + [final]:
            made.wait_send()

    def targets(self):
        return self.along_targets() + self.peer_targets()

    def along_targets(self):
        return [(self.dp, (self.tensor + s) % self.shards) for s in range(1, self.shards)]

    def peer_targets(self):
        return [(flip(self.dp, bit), self.tensor) for bit in (2, 4, 1)]


FAR = 2


def one_shard(ref):
    rows = ref.shape[0] // PEERS

    def at(shard, peer, half):
        return ref.at[half_rows(peer * rows, rows, half)]

    return at


def half_rows(first, rows, half):
    split = (rows // 2 + 15) // 16 * 16
    start, count = {None: (0, rows), 0: (0, split), 1: (split, rows - split)}[half]
    return pl.ds(pl.multiple_of(first + start, 16), count)


def eighth(ref):
    rows = ref.shape[1] // PEERS

    def at(shard, peer, half):
        return ref.at[shard, half_rows(peer * rows, rows, half)]

    return at


class HeadGather:
    def __init__(self, buffer, send, recv):
        self.buffer, self.send, self.recv = buffer, send, recv
        self.dp, self.tensor = lax.axis_index("dp"), lax.axis_index("tensor")
        self.shards = lax.axis_size("tensor")

    def put(self, half, value):
        rows = value.shape[0]
        first = half * (rows + rows // 2)
        self.buffer[self.tensor, first : first + rows] = value[:, :128]
        self.buffer[self.tensor, first + rows : first + rows + rows // 2] = jnp.concatenate(
            [value[: rows // 2, 128:], value[rows // 2 :, 128:]], axis=1
        )

    def take(self, shard):
        count = self.buffer.shape[1] // 2
        rows = count * 2 // 3
        parts = []
        for half in range(2):
            low = self.buffer[shard, half * count : half * count + rows]
            rest = self.buffer[shard, half * count + rows : (half + 1) * count]
            high = jnp.concatenate([rest[:, :HEAD], rest[:, HEAD:]], axis=0)
            parts.append(jnp.concatenate([low, high], axis=1))
        return jnp.concatenate(parts, axis=0)

    def copies(self, half):
        count = self.buffer.shape[1] // 2
        place = self.buffer.at[self.tensor, pl.ds(half * count, count)]
        return [
            remote(place, place, self.send.at[half, s], self.recv.at[half, s], (self.dp, (self.tensor + s) % self.shards))
            for s in range(1, self.shards)
        ]

    def start(self, half):
        for made in self.copies(half):
            made.start()

    def wait(self, half):
        for made in self.copies(half):
            made.wait()

    def product(self, weights):
        total = mm(self.take(0), weights[0])
        for shard in range(1, self.shards):
            total += mm(self.take(shard), weights[shard])
        return total


PIECES = 8


class PeerSum:
    def __init__(self, parts, source, total, land, higher, send, recv, base=0, pieces=None):
        self.parts, self.source, self.total, self.land, self.higher = parts, source, total, land, higher
        self.pieces = pieces
        self.send, self.recv, self.base = send, recv, base
        self.dp, self.tensor = lax.axis_index("dp"), lax.axis_index("tensor")
        self.bits = [(self.dp // b) % 2 for b in (1, 2, 4)]

    @staticmethod
    def far_bits():
        return [PEERS << k for k in range((lax.axis_size("dp") // PEERS - 1).bit_length())]

    @staticmethod
    def copies(parts, far):
        return len(parts) * (6 + far)

    def way(self, part):
        order = ((2, self.bits[1]), (4, self.bits[2]))
        return order if part[5] == 0 else order[::-1]

    def rows(self, refs, part, piece, count):
        array, first, size, column, columns, _ = part
        start = pl.multiple_of(first + piece * size, 16)
        return refs[array].at[pl.ds(start, count * size), pl.ds(column, columns)]

    def hop(self, n, stage, src, dst, bit):
        index = self.base + n * (6 + len(self.far_bits())) + stage
        return remote(src, dst, self.send.at[index], self.recv.at[index], (flip(self.dp, bit), self.tensor))

    def landed(self, n, piece, count):
        size = self.parts[n][2]
        return self.land[n].at[pl.ds(pl.multiple_of(piece * size, 16), count * size)]

    def halving(self, n, stage):
        part = self.parts[n]
        core = self.bits[0]
        (bit_1, own_1), (bit_2, own_2) = self.way(part)
        if stage == 0:
            bit, place = 1, self.landed(n, 0, 4)
            out = self.rows(self.source, part, (1 - core) * 4, 4)
            kept = self.rows(self.source, part, core * 4, 4)
        elif stage == 1:
            bit, place = bit_1, self.landed(n, 4, 2)
            out, kept = self.landed(n, (1 - own_1) * 2, 2), self.landed(n, own_1 * 2, 2)
        else:
            bit, place = bit_2, self.landed(n, 6, 1)
            out, kept = self.landed(n, 4 + 1 - own_2, 1), self.landed(n, 4 + own_2, 1)
        goal = self.final_place(n) if stage == 2 else place
        return self.hop(n, stage, out, place, bit), kept, place, goal

    def final_place(self, n):
        if self.pieces is not None:
            return self.pieces[n]
        return self.rows(self.total, self.parts[n], self.final_piece(self.parts[n]), 1)

    def final_piece(self, part):
        (_, own_1), (_, own_2) = self.way(part)
        return self.bits[0] * 4 + own_1 * 2 + own_2

    def gathering(self, n, stage):
        part = self.parts[n]
        core = self.bits[0]
        (bit_1, own_1), (bit_2, _) = self.way(part)
        piece, count, bit = (
            (self.final_piece(part), 1, bit_2), (core * 4 + own_1 * 2, 2, bit_1), (core * 4, 4, 1),
        )[stage]
        place = self.rows(self.total, part, piece, count)
        return self.hop(n, 3 + stage, place, place, bit)

    def targets(self):
        return [(flip(self.dp, bit), self.tensor) for bit in [1, 2, 4] + self.far_bits()]

    def start_halving(self, stage):
        for n in range(len(self.parts)):
            self.halving(n, stage)[0].start()

    def end_halving(self, stage):
        for n in range(len(self.parts)):
            made, kept, place, goal = self.halving(n, stage)
            made.wait_recv()
            goal[...] = (kept[...].astype(WIDE) + place[...].astype(WIDE)).astype(goal.dtype)
        for n in range(len(self.parts)):
            self.halving(n, stage)[0].wait_send()

    def far(self):
        for k, bit in enumerate(self.far_bits()):
            for n in range(len(self.parts)):
                place = self.final_place(n)
                made = self.hop(n, 6 + k, place, self.higher[n].at[k], bit)
                made.start()
                made.wait()
                place[...] = (place[...].astype(WIDE) + self.higher[n][k].astype(WIDE)).astype(place.dtype)

    def start_gathering(self, stage):
        for n in range(len(self.parts)):
            self.gathering(n, stage).start()

    def end_gathering(self, stage):
        for n in range(len(self.parts)):
            self.gathering(n, stage).wait()


def peer_scratch(parts, shapes, far):
    dma = pltpu.SemaphoreType.DMA
    count = PeerSum.copies(parts, far)
    land = [pltpu.VMEM((7 * p[2], p[4]), NARROW) for p in parts]
    higher = [pltpu.VMEM((far, p[2], p[4]) if far else (1, 16, 128), NARROW) for p in parts]
    return [pltpu.VMEM(shape, NARROW) for shape in shapes] + land + higher + [dma((count,)), dma((count,))]


def sum_rows(values, out, land, send, recv):
    dp, tensor = lax.axis_index("dp"), lax.axis_index("tensor")
    bits = [1, 2, 4] + PeerSum.far_bits()

    def hop(k):
        source = values if k == 0 else out.at[k - 1]
        return remote(source, land.at[k], send.at[k], recv.at[k], (flip(dp, bits[k]), tensor))

    def run(k):
        if k > 0:
            hop(k - 1).wait()
            out[k - 1] = (values if k == 1 else out.at[k - 2])[...] + land[k - 1]
        if k < len(bits):
            hop(k).start()

    return [functools.partial(run, k) for k in range(len(bits) + 1)]


def cross_parts(kv, cross):
    width = cross[1]
    return (
        (0, 0, kv[0] // PIECES, 0, width, 0),
        (0, 0, kv[0] // PIECES, width, kv[1] - width, 1),
        (1, 0, cross[0] // PIECES, 0, width, 0),
    )


def self_parts(own):
    third, width = own[0] // 3, own[1]
    return ((0, 0, third // PIECES, 0, width, 0), (0, third, 2 * third // PIECES, 0, width, 1))


def feed_copies(shards):
    return 5 * Spread.COPIES * (shards - 1)


def labels_of(position, ends):
    place = position - NQ
    label = jnp.zeros_like(position)
    for end in ends:
        label = label + jnp.where(place >= end, 1, 0)
    return jnp.where(position < NQ, -1, label)


def allowed_pairs(lens_ref, item, span, lanes):
    ends = []
    total = jnp.int32(0)
    for c in range(lens_ref.shape[0]):
        total = total + lens_ref[c, item]
        ends.append(total)
    key_label = labels_of(lax.broadcasted_iota(jnp.int32, (span, lanes), 0), ends)
    query_label = labels_of(lax.broadcasted_iota(jnp.int32, (span, lanes), 1) % span, ends)
    return (key_label == query_label) | (key_label == -1)


VISUAL_BLOCKS = 4


def first_kernel(names, *refs):
    r = types.SimpleNamespace(**dict(zip(names, refs)))
    step = pl.program_id(0)
    last = pl.num_programs(0) - 1
    block, items, depth = r.visual.shape
    cols = r.so.shape[0]
    per = PEERS // 4
    rows = cols // per
    base = Spread.COPIES * (lax.axis_size("tensor") - 1)

    def at(shard, peer, half):
        return r.attn_v.at[peer // per, half_rows(shard * cols + (peer % per) * rows, rows, half)]

    def spread_to(where, n):
        return Spread(where, r.send, r.recv, n * base)

    attn = spread_to(at, 0)
    first_in, first_out, cross = (spread_to(eighth(ref), n + 1) for n, ref in enumerate((r.win, r.wout, r.cross)))
    text = [spread_to(one_shard(ref), n + 4) for n, ref in enumerate((r.tin, r.tout))]
    peer, tensor = attn.peer, attn.tensor
    hops = range(1, attn.shards)
    few = 2 * cols // PEERS

    def eighth_of(ref, first, count):
        return ref.at[pl.ds(pl.multiple_of(first, 16), count)]

    def start_attn(s):
        @pl.when(peer < 3 * per)
        def _():
            attn.along(s, eighth_of(r.qkv.at[peer // per], (peer % per) * rows, rows)).start()

        @pl.when(peer >= 3 * per)
        def _():
            attn.along(s, eighth_of(r.so, (peer - 3 * per) * rows, rows)).start()

    def start_cross(s):
        @pl.when(peer < PEERS // 2)
        def _():
            cross.along(s, eighth_of(r.cq, peer * few, few)).start()

        @pl.when(peer >= PEERS // 2)
        def _():
            cross.along(s, eighth_of(r.co, (peer - PEERS // 2) * few, few)).start()

    attn_any, cross_any = r.so.at[pl.ds(0, rows)], r.co.at[pl.ds(0, few)]
    in_mine, out_mine = (eighth(ref)(0, peer, None) for ref in (r.ffn_in_first, r.ffn_out_first))
    text_mine = [eighth(ref)(1, peer, None) for ref in (r.ffn_in, r.ffn_out)]
    here = pl.ds(pl.multiple_of(tensor * cols, 16), cols)
    own_copies = [
        pltpu.make_async_copy(source, goal, r.local.at[n])
        for n, (source, goal) in enumerate(
            [(r.qkv.at[c], r.attn_v.at[c, here]) for c in range(3)]
            + [
                (r.so, r.attn_v.at[3, here]),
                (r.cq, r.cross.at[tensor, pl.ds(0, cols)]),
                (r.co, r.cross.at[tensor, pl.ds(cols, cols)]),
                (r.ffn_in_first.at[0], r.win.at[tensor]),
                (r.ffn_out_first.at[0], r.wout.at[tensor]),
            ]
        )
    ]
    keep = pltpu.make_async_copy(r.attn_v, r.attn, r.local.at[len(own_copies)])

    @pl.when(step == 0)
    def _():
        greet(attn.targets())
        for s in hops:
            start_attn(s)
        for made in own_copies:
            made.start()
        low = 128
        r.w[:cols] = r.wkv[0]
        r.w[cols : 2 * cols - low] = r.wkv[1, low:]
        r.w[2 * cols - low :] = r.wkv[1, :low]

    def project(x, first, count):
        y = mm_nt(x, r.w[...])
        for tile in range(r.y.shape[0]):
            r.y[tile, : count * items] = y[:, tile * 128 : (tile + 1) * 128]
        for item in range(items):
            k_low, high, v_low = [
                r.y[tile, pl.ds(item, count, stride=items)].astype(NARROW) for tile in range(3)
            ]
            r.cross_k[item, first, :128] = k_low
            r.cross_k[item, first, 128:] = high[:, : cols - 128]
            r.cross_v[item, first, :128] = v_low
            r.cross_v[item, first, 128:] = high[:, cols - 128 :]

    @pl.when(step < VISUAL_BLOCKS)
    def _():
        project(
            r.visual[...].reshape(block * items, depth),
            pl.ds(pl.multiple_of(step * block, block), block),
            block,
        )

    @pl.when(step == VISUAL_BLOCKS - 1)
    def _():
        count = r.visual_tail.shape[0]
        project(
            r.visual_tail[...].reshape(count * items, depth),
            pl.ds(r.cross_k.shape[1] - count, count),
            count,
        )
        for s in hops:
            attn.along(s, attn_any).wait_recv()
            attn.start_across(s)
        for s in hops:
            start_cross(s)
        for s in hops:
            first_in.along(s, in_mine).start()
        for one, mine in zip(text, text_mine):
            one.along(FAR, mine).start()
        for s in hops:
            first_out.along(s, out_mine).start()
        for s in hops:
            attn.start_onward(s)
        for s in hops:
            attn.start_last(s)
        for s in hops:
            attn.finish(s)
            attn.along(s, attn_any).wait_send()
        for made in own_copies:
            made.wait()
        keep.start()

    @pl.when(step == VISUAL_BLOCKS + 1)
    def _():
        for s in hops:
            cross.along(s, cross_any).wait()
            cross.start_across(s)

    @pl.when(step == VISUAL_BLOCKS + 2)
    def _():
        for s in hops:
            first_in.along(s, in_mine).wait()
            first_in.start_across(s)

    @pl.when(step >= VISUAL_BLOCKS)
    def _():
        self_rows(r, step - VISUAL_BLOCKS)

    @pl.when(step == last)
    def _():
        for s in hops:
            cross.wait_across(s)
            cross.start_onward(s, True)
        for s in hops:
            first_in.wait_across(s)
            first_in.start_onward(s, True)
        for one, mine in zip(text, text_mine):
            one.along(FAR, mine).wait()
            one.start_across(FAR)
        for s in hops:
            cross.start_last(s)
        for s in hops:
            first_in.start_last(s)
        for s in hops:
            cross.finish(s, True)
            first_in.finish(s, True)
        for one in text:
            one.wait_across(FAR)
        for s in hops:
            first_out.along(s, out_mine).wait()
        keep.wait()


def self_rows(r, at):
    span = NQ + TXT
    items = r.hidden.shape[0] // span
    lanes = QUAD * HEAD
    x = r.hidden[...]
    r.q[...] = (mm_nt(x, r.attn_v[0]).astype(NARROW).astype(WIDE) * SCALE).astype(NARROW)
    r.k[...] = mm_nt(x, r.attn_v[1]).astype(NARROW)
    r.v[...] = mm_nt(x, r.attn_v[2]).astype(NARROW)

    units = []
    for item in range(items):
        rows = slice(item * span, (item + 1) * span)
        allowed = allowed_pairs(r.lens, at * items + item, span, lanes)
        for quad in range(r.hidden.shape[1] // lanes):
            units.append((rows, slice(quad * lanes, (quad + 1) * lanes), allowed))
    scores = [mm_nt(r.k[u, c], spread_heads(r.q[u, c], QUAD)) for u, c, _ in units]
    lows = []
    for value, (u, c, allowed) in zip(scores, units):
        value = jnp.where(allowed, value, MASKED_SCORE)
        lifted = jnp.exp(value - jnp.max(value, axis=0, keepdims=True))
        lows.append((lifted * (1.0 / jnp.sum(lifted, axis=0, keepdims=True))).astype(NARROW))
        r.p[u, c] = lows[-1]
    parts = [mm_tn(low, r.v[u, c]) for low, (u, c, _) in zip(lows, units)]
    for part, (u, c, _) in zip(parts, units):
        r.ctx[u, c] = gather_heads(part, QUAD).astype(NARROW)

    residue = x.astype(WIDE) + mm(r.ctx[...], r.attn_v[3])
    r.res[...] = residue
    unit, _ = norm_parts(residue)
    first = unit * r.gain[0:1] + r.shift[0:1]
    for item in range(items):
        r.fq[item * NQ : (item + 1) * NQ] = first[item * span : item * span + NQ]
        r.ft[item * TXT : (item + 1) * TXT] = first[item * span + NQ : (item + 1) * span]


def first_layer(hidden, lens, visual, wkv, qkv, so, cq, co, gain, shift, ffn_in, ffn_out, shards):
    rows, width = hidden.shape
    span, items, depth = visual.shape
    cols = so.shape[0]
    tail = span % (16 * VISUAL_BLOCKS)
    visual_block = (span - tail) // VISUAL_BLOCKS
    block = min(rows, 256)
    copies = 6 * Spread.COPIES * (shards - 1)
    dma = pltpu.SemaphoreType.DMA
    hbm = pl.BlockSpec(memory_space=pl.ANY)

    def later(i):
        return jnp.maximum(i - VISUAL_BLOCKS, 0)

    def whole(shape):
        return pl.BlockSpec(shape, lambda i: (0,) * len(shape), pipeline_mode=pl.Buffered(1))

    def by_rows(count, dtype=NARROW):
        return pl.BlockSpec((count, width), lambda i: (later(i), 0))

    def low(*shape):
        return jax.ShapeDtypeStruct(shape, NARROW)

    def wide(*shape):
        return jax.ShapeDtypeStruct(shape, WIDE)

    ins = dict(
        lens=(lens, pl.BlockSpec(memory_space=pltpu.SMEM)),
        hidden=(hidden, by_rows(block)),
        visual=(
            visual,
            pl.BlockSpec((visual_block, items, depth), lambda i: (jnp.minimum(i, VISUAL_BLOCKS - 1), 0, 0)),
        ),
        visual_tail=(visual, pl.BlockSpec((tail, items, depth), lambda i: (span // tail - 1, 0, 0))),
        wkv=(wkv, whole(wkv.shape)), qkv=(qkv, whole(qkv.shape)), so=(so, whole(so.shape)),
        cq=(cq, whole(cq.shape)), co=(co, whole(co.shape)), gain=(gain, whole(gain.shape)), shift=(shift, whole(shift.shape)),
        ffn_in_first=(ffn_in, whole((1,) + ffn_in.shape[1:])), ffn_out_first=(ffn_out, whole((1,) + ffn_out.shape[1:])),
        ffn_in=(ffn_in, hbm), ffn_out=(ffn_out, hbm),
    )
    kv = (items, span, cols)
    outs = dict(
        cross_k=(low(*kv), whole(kv)), cross_v=(low(*kv), whole(kv)),
        q=(low(rows, width), by_rows(block)), k=(low(rows, width), by_rows(block)), v=(low(rows, width), by_rows(block)),
        p=(low(rows, width), by_rows(block)), ctx=(low(rows, width), by_rows(block)),
        res=(wide(rows, width), by_rows(block)),
        fq=(wide(rows // 2, width), by_rows(block // 2)), ft=(wide(rows // 2, width), by_rows(block // 2)),
        attn=(low(4, shards * cols, width), hbm),
        win=(low(shards, *ffn_in.shape[1:]), hbm), wout=(low(shards, *ffn_out.shape[1:]), hbm),
        cross=(low(shards, 2 * cols, width), hbm),
        tin=(low(*ffn_in.shape[1:]), hbm), tout=(low(*ffn_out.shape[1:]), hbm),
    )
    scratch = dict(
        attn_v=pltpu.VMEM((4, shards * cols, width), NARROW),
        w=pltpu.VMEM((2 * cols, depth), NARROW),
        y=pltpu.VMEM((2 * cols // 128, visual_block * items, 128), WIDE),
        send=dma((copies,)), recv=dma((copies,)), local=dma((9,)),
    )
    names = tuple(ins) + tuple(outs) + tuple(scratch)
    values = pl.pallas_call(
        functools.partial(first_kernel, names),
        grid=(VISUAL_BLOCKS + rows // block,),
        in_specs=[spec for _, spec in ins.values()],
        out_specs=[spec for _, spec in outs.values()],
        out_shape=[shape for shape, _ in outs.values()],
        scratch_shapes=list(scratch.values()),
        compiler_params=pltpu.CompilerParams(
            collective_id=0, has_side_effects=True, vmem_limit_bytes=VMEM_BYTES
        ),
        name="first_layer",
    )(*[value for value, _ in ins.values()])
    return types.SimpleNamespace(**dict(zip(outs, values)))


def self_backward_kernel(
    x_ref, w_ref, gain_ref, res_ref, gq_ref, gt_ref, q_ref, k_ref, v_ref, p_ref, ctx_ref,
    kv_ref, cross_ref, piece0_ref, piece1_ref, piece2_ref, piece3_ref, other_gain, other_shift,
    grad_ref, kv_out, cq_out, co_out, qkv_out, so_out, rows_out, feed_total,
    down, dctx, dq, dk, dv, acc, gain_sums, shift_sums, grads_ref, *rest,
):
    parts = cross_parts(kv_ref.shape, cross_ref.shape)
    (kv_total, cross_total), land, higher = rest[:2], rest[2:5], rest[5:8]
    send, recv, feed_send, feed_recv, local = rest[8:13]
    own_total, own_land, own_higher, (own_send, own_recv) = rest[13], rest[14:16], rest[16:18], rest[18:20]
    few, few_land, few_send, few_recv, few_in = rest[20:]
    later = PeerSum(feed_parts(x_ref.shape[1]), (), (feed_total,), (), (), feed_send, feed_recv)
    peers = PeerSum(parts, (kv_ref, cross_ref), (kv_total, cross_total), land, higher, send, recv)
    last = PeerSum(
        self_parts(grads_ref.shape), (grads_ref,), (own_total,), own_land, own_higher, own_send, own_recv
    )
    span = NQ + TXT
    block = res_ref.shape[0]
    items = block // span
    lanes = QUAD * HEAD
    placed = [
        pltpu.make_async_copy(ref, later.rows((feed_total,), part, later.final_piece(part), 1), local.at[n])
        for n, (ref, part) in enumerate(zip((piece0_ref, piece1_ref, piece2_ref, piece3_ref), later.parts))
    ]
    step = pl.program_id(0)

    @pl.when(step == 0)
    def _():
        for made in placed:
            made.start()
        greet(peers.targets())
        peers.start_halving(0)
        for made in placed:
            made.wait()
        later.start_gathering(0)

    @pl.when(step == 1)
    def _():
        peers.end_halving(0)
        peers.start_halving(1)
        later.end_gathering(0)
        later.start_gathering(1)

    @pl.when(step == 2)
    def _():
        peers.end_halving(1)
        peers.start_halving(2)

    @pl.when(step == 3)
    def _():
        peers.end_halving(2)
        peers.far()
        peers.start_gathering(0)

    unit, inverse = norm_parts(res_ref[...])
    pieces = []
    for item in range(items):
        pieces.append(gq_ref[item * NQ : (item + 1) * NQ])
        pieces.append(gt_ref[item * TXT : (item + 1) * TXT])
    cotangent = jnp.concatenate(pieces, axis=0)
    grad_res = norm_back(unit, inverse, gain_ref[0:1], cotangent)
    gain_sum, shift_sum = column_sums(unit, cotangent)

    @pl.when(step == 0)
    def _():
        gain_sums[...] = gain_sum
        shift_sums[...] = shift_sum

    @pl.when(step > 0)
    def _():
        gain_sums[...] += gain_sum
        shift_sums[...] += shift_sum

    grad_ref[...] = grad_res
    low = grad_res.astype(NARROW)
    down[...] = low
    dctx[...] = mm_nt(low, w_ref[3]).astype(NARROW)

    units = [
        (slice(item * span, (item + 1) * span), slice(quad * lanes, (quad + 1) * lanes))
        for item in range(items)
        for quad in range(w_ref.shape[2] // lanes)
    ]
    for at in range(0, len(units), UNITS):
        some = units[at : at + UNITS]
        spread = [spread_heads(dctx[u], QUAD) for u in some]
        grad_chances = [mm_nt(v_ref[u], one) for u, one in zip(some, spread)]
        scores = []
        for u, value in zip(some, grad_chances):
            weighted = p_ref[u].astype(WIDE)
            inner = jnp.sum(value * weighted, axis=0, keepdims=True)
            scores.append((weighted * (value - inner)).astype(NARROW))
        for u, one in zip(some, spread):
            dv[u] = mm(p_ref[u], one).astype(NARROW)
        for u, one in zip(some, scores):
            dk[u] = mm(one, spread_heads(q_ref[u], QUAD)).astype(NARROW)
        values = [mm_tn(one, k_ref[u]) for u, one in zip(some, scores)]
        for u, value in zip(some, values):
            dq[u] = (gather_heads(value, QUAD) * SCALE).astype(NARROW)

    grad_ref[...] += mm(dq[...], w_ref[0]) + mm(dk[...], w_ref[1]) + mm(dv[...], w_ref[2])

    own = lax.axis_index("tensor")
    cols = grads_ref.shape[0] // 4
    window = acc.shape[1]
    start = pl.multiple_of((own * cols) // 128 * 128, 128)
    here = pl.ds(start, window)
    x = x_ref[...]
    products = (
        mm_tn(dq[:, here], x), mm_tn(dk[:, here], x), mm_tn(dv[:, here], x),
        mm_tn(ctx_ref[:, here], down[...]),
    )

    @pl.when(step == 0)
    def _():
        for c, product in enumerate(products):
            acc[c] = product

    @pl.when(step > 0)
    def _():
        for c, product in enumerate(products):
            acc[c] += product

    @pl.when(step == pl.num_programs(0) - 1)
    def _():
        offset = pl.multiple_of(own * cols - start, 64)
        for c in range(4):
            grads_ref[c * cols : (c + 1) * cols] = acc[c, pl.ds(offset, cols), :].astype(NARROW)
        last.start_halving(0)
        few_in[0:1] = gain_sums[...]
        few_in[1:4] = other_gain[...]
        few_in[4:5] = shift_sums[...]
        few_in[5:8] = other_shift[...]
        few_steps = sum_rows(few_in, few, few_land, few_send, few_recv)
        few_steps[0]()
        peers.end_gathering(0)
        last.end_halving(0)
        last.start_halving(1)
        peers.start_gathering(1)
        few_steps[1]()
        last.end_halving(1)
        last.start_halving(2)
        later.end_gathering(1)
        later.start_gathering(2)
        for run in few_steps[2:]:
            run()
        rows_out[...] = few[few.shape[0] - 1]
        peers.end_gathering(1)
        peers.start_gathering(2)
        last.end_halving(2)
        last.far()
        last.start_gathering(0)
        peers.end_gathering(2)
        kv_out[0] = kv_total[:cols]
        kv_out[1, 128:] = kv_total[cols : 2 * cols - 128]
        kv_out[1, :128] = kv_total[2 * cols - 128 :]
        last.end_gathering(0)
        last.start_gathering(1)
        cq_out[...] = cross_total[:cols]
        co_out[...] = cross_total[cols:]
        last.end_gathering(1)
        last.start_gathering(2)
        later.end_gathering(2)
        last.end_gathering(2)
        for c in range(3):
            qkv_out[c] = own_total[c * cols : (c + 1) * cols]
        so_out[...] = own_total[3 * cols :]


def self_backward(
    hidden, weights, gain, residue, grad_q, grad_t, q, k, v, p, ctx, kv, cross, pieces, gains, shifts,
    cols, ident, peers
):
    rows, width = hidden.shape
    block = min(rows, 256)
    half = block // 2
    full = pl.BlockSpec((block, width), lambda i: (i, 0))
    halves = pl.BlockSpec((half, width), lambda i: (i, 0))
    parts = cross_parts(kv.shape, cross.shape)
    far = (peers // PEERS - 1).bit_length()
    depth = kv.shape[1]
    own = (4 * cols, width)
    steps = 3 + far
    hbm = pl.BlockSpec(memory_space=pl.ANY)
    dma = pltpu.SemaphoreType.DMA
    count = PeerSum.copies(feed_parts(width), far)

    def whole(shape):
        return pl.BlockSpec(shape, lambda i: (0,) * len(shape), pipeline_mode=pl.Buffered(1))

    def wide(*shape):
        return jax.ShapeDtypeStruct(shape, WIDE)

    totals = [
        jax.ShapeDtypeStruct(dims, NARROW)
        for dims in ((2, cols, depth), (cols, width), (cols, width), (3, cols, width), (cols, width))
    ] + [wide(8, width)]
    return pl.pallas_call(
        self_backward_kernel,
        grid=(rows // block,),
        in_specs=[
            full,
            whole(weights.shape),
            pl.BlockSpec(gain.shape, lambda i: (0, 0)),
            full, halves, halves, full, full, full, full, full,
        ]
        + [whole(a.shape) for a in (kv, cross, *pieces, gains, shifts)],
        out_specs=[full] + [whole(t.shape) for t in totals] + [hbm],
        out_shape=[wide(rows, width)] + totals + [jax.ShapeDtypeStruct((4 * width, width), NARROW)],
        scratch_shapes=[pltpu.VMEM((block, width), NARROW)] * 5
        + [pltpu.VMEM((4, (cols + 64 + 127) // 128 * 128, width), WIDE)]
        + [pltpu.VMEM((1, width), WIDE)] * 2
        + [pltpu.VMEM(own, NARROW)]
        + peer_scratch(parts, [kv.shape, cross.shape], far)
        + [dma((count,)), dma((count,)), dma((4,))]
        + peer_scratch(self_parts(own), [own], far)
        + [pltpu.VMEM((steps, 8, width), WIDE)] * 2
        + [dma((steps,)), dma((steps,)), pltpu.VMEM((8, width), WIDE)],
        compiler_params=pltpu.CompilerParams(
            collective_id=ident, has_side_effects=True, vmem_limit_bytes=VMEM_BYTES
        ),
        name="self_backward",
    )(hidden, weights, gain, residue, grad_q, grad_t, q, k, v, p, ctx, kv, cross, *pieces, gains, shifts)


def feed_parts(width):
    return tuple((0, n * width, width // PIECES, 0, width, n // 2) for n in range(4))


LOADS = (
    "fq", "wq_own", "k", "v", "ft", "tin", "tout", "cotq", "tcot", "wo_own", "w_all", "tin2", "tout2",
)
STORES = ("outq", "outt", "gq", "gt", "grads", "kv", "piece0", "piece1", "piece2", "piece3")


def middle_kernel(names, *refs):
    r = types.SimpleNamespace(**dict(zip(names, refs)))
    cols = r.wq_own.shape[0]
    heads = cols // HEAD
    items, span = r.k.shape[:2]
    width = r.fq.shape[1]
    depth = r.visual.shape[2]
    chunks = r.win.shape[0]
    tensor = lax.axis_index("tensor")
    sources = dict(
        tin=r.ffn_in.at[1], tout=r.ffn_out.at[1],
        w_all=r.cross_o.at[:, pl.ds(cols, cols)], tin2=r.tin2_o, tout2=r.tout2_o,
        cotq=r.cot.at[:, pl.ds(0, NQ)], tcot=r.cot.at[:, pl.ds(NQ, TXT)],
    )
    rows = [slice(item * NQ, (item + 1) * NQ) for item in range(items)]
    tall = r.fq.shape

    def load(name, goal=None):
        return pltpu.make_async_copy(
            sources.get(name, getattr(r, name, None)),
            getattr(r, name + "_v") if goal is None else goal,
            r.load_sem.at[LOADS.index(name)],
        )

    def store(name, source):
        return pltpu.make_async_copy(source, getattr(r, name + "_o"), r.store_sem.at[STORES.index(name)])

    pair = (lax.axis_index("dp"), tensor + 1 - 2 * (tensor % 2))
    swaps = [remote(r.tpart.at[n], r.tland.at[n], r.swap_send.at[n], r.swap_recv.at[n], pair) for n in range(2)]
    forth = HeadGather(r.heads1, r.head_send1, r.head_recv1)
    gather = HeadGather(r.heads2, r.head_send2, r.head_recv2)
    base = Spread.COPIES * (chunks - 1)
    hops = range(1, chunks)
    first_out = Spread(eighth(r.wout_o), r.spread_send, r.spread_recv, base)
    text = [
        Spread(one_shard(ref), r.spread_send, r.spread_recv, n * base) for n, ref in ((3, r.tin2_o), (4, r.tout2_o))
    ]
    parts = feed_parts(width)
    kind_parts = ((0, 0, width // PIECES, 0, width, 0), (0, width, width // PIECES, 0, width, 1))
    feed_q = [None]
    pieces = (r.piece0, r.piece1, r.piece2, r.piece3)
    peers_q, peers_t = (
        PeerSum(
            kind_parts, source, (), r.land[kind::2], r.higher[kind::2], r.peer_send, r.peer_recv,
            kind * PeerSum.copies(kind_parts, len(PeerSum.far_bits())), pieces[kind::2],
        )
        for kind, source in enumerate((feed_q, (r.feed_t,)))
    )

    early = ("tin_v", "tout_v", "tin2_v", "tout2_v", "tslope", "tslope2", "cotq_v", "tcot_v")

    def to_feed_forward(*buffers):
        for name, buffer in zip(early, buffers):
            setattr(r, name, buffer)
        for name in LOADS[:11]:
            load(name).start()
        greet(first_out.along_targets() + peers_q.targets())
        for s in hops:
            first_out.start_across(s)
        for one in text:
            one.start_onward(FAR, True)
        for name in ("fq", "wq_own", "k", "v"):
            load(name).wait()
        r.q[...] = (
            mm_nt(r.fq_v[...].astype(NARROW), r.wq_own_v[...]).astype(NARROW).astype(WIDE) * SCALE
        ).astype(NARROW)
        for half in range(2):
            some = range(half * items // 2, (half + 1) * items // 2)
            scores = [mm_nt(r.k_v[item], spread_heads(r.q[rows[item]], heads)) for item in some]
            lows = []
            for item, value in zip(some, scores):
                lifted = jnp.exp(value - jnp.max(value, axis=0, keepdims=True))
                lows.append((lifted * (1.0 / jnp.sum(lifted, axis=0, keepdims=True))).astype(NARROW))
                r.p[item] = lows[-1]
            values = [mm_tn(low, r.v_v[item]) for item, low in zip(some, lows)]
            for item, value in zip(some, values):
                r.ctx[rows[item]] = gather_heads(value, heads).astype(NARROW)
            count = items // 2 * NQ
            here = slice(half * count, (half + 1) * count)
            forth.put(half, r.ctx[here])
            forth.start(half)
        def text_part(win, wout, slope_v, act_v):
            act, slope = gelu_parts(mm(r.ft_v[...].astype(NARROW), win[...]))
            slope_v[...] = slope.astype(NARROW)
            act = act.astype(NARROW)
            if act_v is not None:
                act_v[...] = act
            return mm(act, wout[...])

        for name in ("ft", "tin", "tout"):
            load(name).wait()
        r.gt_v[...] = text_part(r.tin_v, r.tout_v, r.tslope, r.tact)
        for s in hops:
            first_out.start_onward(s)
        for one in text:
            one.start_last(FAR)
        for one in text:
            one.finish(FAR, True)
        load("tin2").start()
        load("tout2").start()
        forth.wait(0)
        for s in hops:
            first_out.start_last(s)
        forth.wait(1)
        load("w_all").wait()
        r.gq_v[...] = forth.product(r.w_all_v)
        sources["w_all"] = r.cross_o.at[:, pl.ds(0, cols)]
        load("w_all").start()
        load("tin2").wait()
        load("tout2").wait()
        r.tpart[0] = (r.gt_v[...] + text_part(r.tin2_v, r.tout2_v, r.tslope2, None)).astype(NARROW)
        swaps[0].start()

        def text_rows():
            load("tcot").wait()
            unit, inverse = norm_parts(r.ft_v[...] + r.tpart[0].astype(WIDE) + r.tland[0].astype(WIDE))
            r.outt[...] = (unit * r.gain[3:4] + r.shift[3:4]).astype(NARROW)
            store("outt", r.outt).start()
            cotangent = r.tcot_v[...].astype(WIDE).reshape(tall)
            gain_sum, shift_sum = column_sums(unit, cotangent)
            r.gains[2:3] = gain_sum
            r.shifts[2:3] = shift_sum
            grad = norm_back(unit, inverse, r.gain[3:4], cotangent)
            r.gt_v[...] = grad
            r.ttop[...] = grad.astype(NARROW)
            r.tdpre[...] = (mm_nt(r.ttop[...], r.tout_v[...]) * r.tslope[...].astype(WIDE)).astype(NARROW)
            far = (mm_nt(r.ttop[...], r.tout2_v[...]) * r.tslope2[...].astype(WIDE)).astype(NARROW)
            r.tpart[1] = (mm_nt(r.tdpre[...], r.tin_v[...]) + mm_nt(far, r.tin2_v[...])).astype(NARROW)
            swaps[1].start()
            r.feed_t[:width] = mm_tn(r.ft_v[...].astype(NARROW), r.tdpre[...]).astype(NARROW)
            r.feed_t[width:] = mm_tn(r.tact[...], r.ttop[...]).astype(NARROW)
            peers_t.start_halving(0)

        def query_rows(slopes, total, weights, outq):
            def fetch(j):
                slot, chunk = j % 2, j % chunks
                return [
                    pltpu.make_async_copy(ref.at[chunk], weights.at[slot, n], r.weight_sem.at[slot, n])
                    for n, ref in enumerate((r.win_o, r.wout_o))
                ]

            unit, _ = norm_parts(r.fq_v[...] + r.gq_v[...])
            value = unit * r.gain[1:2] + r.shift[1:2]
            r.low[...] = value.astype(NARROW)
            total[...] = value
            for s in hops:
                first_out.finish(s)
            for made in fetch(0):
                made.start()

            def next_weights(j):
                for made in fetch(j):
                    made.wait()

                @pl.when(j + 1 < 2 * chunks)
                def _():
                    for made in fetch(j + 1):
                        made.start()

                return weights.at[j % 2, 0], weights.at[j % 2, 1]

            @pl.loop(0, chunks)
            def _(j):
                win, wout = next_weights(j)
                act, slope = gelu_parts(mm(r.low[...], win[...]))
                slopes[j] = slope.astype(NARROW)
                act = act.astype(NARROW)
                total[...] += mm(act, wout[...])

                @pl.when(j == tensor)
                def _():
                    r.act[...] = act


            unit, inverse = norm_parts(total[...])
            outq[...] = (unit * r.gain[2:3] + r.shift[2:3]).astype(NARROW)
            store("outq", outq).start()
            load("cotq").wait()
            cotangent = r.cotq_v[...].astype(WIDE).reshape(tall)
            gain_sum, shift_sum = column_sums(unit, cotangent)
            r.gains[1:2] = gain_sum
            r.shifts[1:2] = shift_sum
            grad = norm_back(unit, inverse, r.gain[2:3], cotangent)
            total[...] = grad
            r.top[...] = grad.astype(NARROW)

            @pl.loop(chunks, 2 * chunks)
            def _(j):
                win, wout = next_weights(j)
                chunk = j - chunks
                dpre = (mm_nt(r.top[...], wout[...]) * slopes[chunk].astype(WIDE)).astype(NARROW)
                total[...] += mm_nt(dpre, win[...])

                @pl.when(chunk == tensor)
                def _():
                    r.dpre[...] = dpre

                @pl.when(chunk == 2)
                def _():
                    swaps[0].wait()
                    text_rows()


            grad_second = total[...]
            unit, inverse = norm_parts(r.fq_v[...] + r.gq_v[...])
            gain_sum, shift_sum = column_sums(unit, grad_second)
            r.gains[0:1] = gain_sum
            r.shifts[0:1] = shift_sum
            grad = norm_back(unit, inverse, r.gain[1:2], grad_second)
            r.gq_v[...] = grad
            r.down[...] = grad.astype(NARROW)
            store("outq", outq).wait()

        pl.run_scoped(
            query_rows,
            pltpu.VMEM((chunks, tall[0], r.win.shape[2]), NARROW),
            pltpu.VMEM(tall, WIDE),
            pltpu.VMEM((2, 2) + r.win.shape[1:], NARROW),
            pltpu.VMEM(tall, NARROW),
        )

    inner, outer = r.ffn_in.shape[1:], r.ffn_out.shape[1:]
    pl.run_scoped(
        to_feed_forward,
        *[pltpu.VMEM(shape, NARROW) for shape in (inner, outer, inner, outer, (tall[0], inner[1]), (tall[0], inner[1]), (items, NQ, width), (items, TXT, width))],
    )

    def query_gradients(goal):
        feed_q[0] = goal
        goal[:width] = mm_tn(r.low[...], r.dpre[...]).astype(NARROW)
        goal[width:] = mm_tn(r.act[...], r.top[...]).astype(NARROW)
        peers_q.start_halving(0)

    def cross_rows(dctx, dq, score, dkv, acc, x, x_tail, kv, feed_v):
        group = items // 4
        steps = VISUAL_STEPS
        tail = span % steps
        block = (span - tail) // steps

        def fetch(j):
            return pltpu.make_async_copy(r.visual.at[pl.ds(j * block, block)], x.at[j % 2], r.x_sem.at[j % 2])

        rest = pltpu.make_async_copy(r.visual.at[pl.ds(span - tail, tail)], x_tail, r.x_sem.at[2])
        fetch(0).start()
        rest.start()
        query_gradients(feed_v)
        peers_t.end_halving(0)
        peers_t.start_halving(1)
        load("wo_own").wait()
        dctx[...] = mm_nt(r.down[...], r.wo_own_v[...]).astype(NARROW)
        for g in range(4):
            some = range(g * group, (g + 1) * group)
            spread = [spread_heads(dctx[rows[item]], heads) for item in some]
            grad_chances = [mm_nt(r.v_v[item], one) for item, one in zip(some, spread)]
            scores = []
            for item, value in zip(some, grad_chances):
                weighted = r.p[item].astype(WIDE)
                inner = jnp.sum(value * weighted, axis=0, keepdims=True)
                scores.append((weighted * (value - inner)).astype(NARROW))
                score[item] = scores[-1]
            values = [mm_tn(one, r.k_v[item]) for item, one in zip(some, scores)]
            for item, value in zip(some, values):
                dq[rows[item]] = (gather_heads(value, heads) * SCALE).astype(NARROW)
            if g % 2:
                count = 2 * group * NQ
                here = slice(g // 2 * count, (g // 2 + 1) * count)
                gather.put(g // 2, dq[here])
                gather.start(g // 2)
        peers_q.end_halving(0)
        peers_q.start_halving(1)
        none = jnp.zeros((QUAD * NQ, cols), NARROW)
        for g in range(4):
            some = range(g * group, (g + 1) * group)
            both = []
            for item in some:
                one = spread_heads(dctx[rows[item]], heads)
                both.append(
                    mm(
                        jnp.concatenate([score[item], r.p[item]], axis=1),
                        jnp.concatenate(
                            [
                                jnp.concatenate([spread_heads(r.q[rows[item]], heads), none], axis=1),
                                jnp.concatenate([none, one[:, 128:], one[:, :128]], axis=1),
                            ],
                            axis=0,
                        ),
                    )
                )
            for item, value in zip(some, both):
                for tile in range(dkv.shape[0]):
                    dkv[tile, pl.ds(item, span, stride=items)] = value[:, tile * 128 : (tile + 1) * 128]
        r.grads[:cols] = mm_tn(dq[...], r.fq_v[...].astype(NARROW)).astype(NARROW)
        r.grads[cols:] = mm_tn(r.ctx[...], r.down[...]).astype(NARROW)
        store("grads", r.grads).start()

        def product(first, count, value):
            grads = [dkv[tile, pl.ds(first, count)].astype(NARROW) for tile in range(dkv.shape[0])]
            return mm_tn(jnp.concatenate(grads, axis=1), value.reshape(count, depth))

        rest.wait()
        acc[...] = product((span - tail) * items, tail * items, x_tail[...])

        @pl.loop(0, steps)
        def _(j):
            fetch(j).wait()

            @pl.when(j + 1 < steps)
            def _():
                fetch(j + 1).start()

            acc[...] += product(pl.multiple_of(j * block * items, 16), block * items, x[j % 2])

            @pl.when(j == 1)
            def _():
                peers_t.end_halving(1)
                peers_t.start_halving(2)

            @pl.when(j == 4)
            def _():
                peers_q.end_halving(1)
                peers_q.start_halving(2)

        kv[...] = acc[...].astype(kv.dtype)
        store("kv", kv).start()
        gather.wait(0)
        gather.wait(1)
        load("w_all").wait()
        r.gq_v[...] += gather.product(r.w_all_v)
        store("gq", r.gq_v).start()
        swaps[1].wait()
        r.gt_v[...] += r.tpart[1].astype(WIDE) + r.tland[1].astype(WIDE)
        store("gt", r.gt_v).start()
        for one in (peers_t, peers_q):
            one.end_halving(2)
            one.far()
        for n, piece in enumerate(pieces):
            store("piece%d" % n, piece).start()
        store("kv", kv).wait()

    pl.run_scoped(
        cross_rows,
        pltpu.VMEM((tall[0], cols), NARROW),
        pltpu.VMEM((tall[0], cols), NARROW),
        pltpu.VMEM((items, span, QUAD * NQ), NARROW),
        pltpu.VMEM((2 * cols // 128, items * span, 128), WIDE),
        pltpu.VMEM((2 * cols, depth), WIDE),
        pltpu.VMEM((2, span // VISUAL_STEPS, items, depth), NARROW),
        pltpu.VMEM((span % VISUAL_STEPS, items, depth), NARROW),
        pltpu.VMEM((2 * cols, depth), NARROW),
        pltpu.VMEM((2 * width, width), NARROW),
    )
    for name, source in (
        ("outt", r.outt), ("gq", r.gq_v), ("gt", r.gt_v), ("grads", r.grads),
        ("piece0", r.piece0), ("piece1", r.piece1), ("piece2", r.piece2), ("piece3", r.piece3),
    ):
        store(name, source).wait()


def middle(arrays, ident, peers):
    rows, width = arrays["fq"].shape
    cols = arrays["wq_own"].shape[0]
    items, span = arrays["k"].shape[:2]
    hidden = arrays["ffn_in"].shape[2]
    depth = arrays["visual"].shape[2]
    shards = arrays["win"].shape[0]
    far = (peers // PEERS - 1).bit_length()
    parts = feed_parts(width)
    piece = (parts[0][2], width)
    dma = pltpu.SemaphoreType.DMA
    hbm, vmem = pl.BlockSpec(memory_space=pl.ANY), pl.BlockSpec(memory_space=pltpu.VMEM)

    def low(*dims):
        return pltpu.VMEM(dims, NARROW)

    def wide(*dims):
        return pltpu.VMEM(dims, WIDE)

    out = jax.ShapeDtypeStruct
    outs = dict(
        outq_o=out((rows, width), NARROW), outt_o=out((rows, width), NARROW),
        gq_o=out((rows, width), WIDE), gt_o=out((rows, width), WIDE),
        grads_o=out((2 * cols, width), NARROW), kv_o=out((2 * cols, depth), NARROW),
        piece0_o=out(piece, NARROW), piece1_o=out(piece, NARROW), piece2_o=out(piece, NARROW), piece3_o=out(piece, NARROW),
        gains=out((3, width), WIDE), shifts=out((3, width), WIDE),
        win_o=out(arrays["win"].shape, NARROW), wout_o=out(arrays["wout"].shape, NARROW),
        cross_o=out(arrays["cross_w"].shape, NARROW),
        tin2_o=out(arrays["tin2"].shape, NARROW), tout2_o=out(arrays["tout2"].shape, NARROW),
    )
    copies = feed_copies(shards)
    total = peer_scratch(parts, [], far)
    scratch = dict(
        fq_v=wide(rows, width), wq_own_v=low(cols, width), wo_own_v=low(cols, width),
        k_v=low(*arrays["k"].shape), v_v=low(*arrays["v"].shape), ft_v=wide(rows, width),
        w_all_v=low(shards, cols, width),
        q=low(rows, cols), ctx=low(rows, cols), p=low(items, span, QUAD * NQ),
        tact=low(rows, hidden),
        low=low(rows, width), top=low(rows, width), down=low(rows, width),
        act=low(rows, hidden), dpre=low(rows, hidden),
        ttop=low(rows, width), tdpre=low(rows, hidden), outt=low(rows, width),
        gq_v=wide(rows, width), gt_v=wide(rows, width), grads=low(2 * cols, width),
        tpart=low(2, rows, width), tland=low(2, rows, width), swap_send=dma((2,)), swap_recv=dma((2,)),
        heads1=low(shards, rows * cols // 128, 128), head_send1=dma((2, shards)), head_recv1=dma((2, shards)),
        heads2=low(shards, rows * cols // 128, 128), head_send2=dma((2, shards)), head_recv2=dma((2, shards)),
        spread_send=dma((copies,)), spread_recv=dma((copies,)),
        feed_t=low(2 * width, width), piece0=low(*piece), piece1=low(*piece), piece2=low(*piece), piece3=low(*piece),
        land=total[:4], higher=total[4:8], peer_send=total[8], peer_recv=total[9],
        load_sem=dma((len(LOADS),)), store_sem=dma((len(STORES),)), weight_sem=dma((2, 2)), x_sem=dma((3,)),
    )
    names = tuple(arrays) + tuple(outs) + tuple(scratch)
    return dict(
        zip(
            outs,
            pl.pallas_call(
                functools.partial(middle_kernel, names),
                in_specs=[vmem if name in ("gain", "shift") else hbm for name in arrays],
                out_specs=[vmem if name in ("gains", "shifts") else hbm for name in outs],
                out_shape=list(outs.values()),
                input_output_aliases={
                    list(arrays).index(a): list(outs).index(b)
                    for a, b in (
                        ("win", "win_o"), ("wout", "wout_o"), ("cross_w", "cross_o"), ("tin2", "tin2_o"), ("tout2", "tout2_o"),
                    )
                },
                scratch_shapes=list(scratch.values()),
                compiler_params=pltpu.CompilerParams(
                    collective_id=ident, has_side_effects=True, vmem_limit_bytes=62 * 2**20
                ),
                name="middle",
            )(*arrays.values()),
        )
    )


def on_device(
    hidden_in,
    visual_feats,
    caption_lengths,
    self_qkv,
    self_out,
    cross_query,
    cross_kv,
    cross_out,
    ffn_in,
    ffn_out,
    norm_gain,
    norm_shift,
    out_grad,
):
    items = visual_feats.shape[0]
    rows, width = hidden_in.shape
    span = rows // items
    cols = self_qkv.shape[2]
    shards = lax.axis_size("tensor")

    visual = jnp.swapaxes(visual_feats, 0, 1)
    cross_wq = jnp.swapaxes(cross_query, 0, 1)
    first = first_layer(
        hidden_in, jnp.swapaxes(caption_lengths, 0, 1), visual, jnp.swapaxes(cross_kv, 1, 2), jnp.swapaxes(self_qkv, 1, 2),
        self_out, cross_wq, cross_out, norm_gain, norm_shift, ffn_in, ffn_out, shards,
    )
    peers = lax.axis_size("dp")
    mid = middle(
        dict(
            fq=first.fq, wq_own=cross_wq, k=first.cross_k, v=first.cross_v, ft=first.ft,
            cot=out_grad.reshape(items, span, width), wo_own=cross_out, ffn_in=ffn_in, ffn_out=ffn_out, win=first.win,
            wout=first.wout, cross_w=first.cross, tin2=first.tin, tout2=first.tout, visual=visual,
            gain=norm_gain, shift=norm_shift,
        ),
        2, peers,
    )
    out_q, out_t, g_cross, g_kv = mid["outq_o"], mid["outt_o"], mid["grads_o"], mid["kv_o"]
    grad_hidden, g_kv, g_cq, g_co, g_qkv, g_so, gains, g_feed = self_backward(
        hidden_in, first.attn, norm_gain, first.res, mid["gq_o"], mid["gt_o"], first.q, first.k, first.v, first.p, first.ctx,
        g_kv, g_cross,
        [mid["piece%d_o" % n] for n in range(4)], mid["gains"], mid["shifts"], cols, 6, peers,
    )
    g_feed = g_feed.reshape(2, 2, width, width).astype(WIDE)
    g_in, g_out = g_feed[0], g_feed[1]
    g_kv, g_cq, g_co, g_qkv, g_so = [g.astype(WIDE) for g in (g_kv, g_cq, g_co, g_qkv, g_so)]
    out = jnp.concatenate(
        [out_q.reshape(items, NQ, width), out_t.reshape(items, TXT, width)], axis=1
    ).reshape(rows, width)
    return (
        out,
        grad_hidden,
        jnp.swapaxes(g_qkv, 1, 2),
        g_so,
        jnp.swapaxes(g_cq, 0, 1),
        jnp.swapaxes(g_kv, 1, 2),
        g_co,
        g_in,
        g_out,
        gains[:4],
        gains[4:],
    )


def solution(mesh):
    placed = (
        P("dp", None),
        P("dp", None, None),
        P("dp", None),
        P(None, None, "tensor"),
        P("tensor", None),
        P(None, "tensor"),
        P(None, None, "tensor"),
        P("tensor", None),
        P(None, None, "tensor"),
        P(None, "tensor", None),
        P(),
        P(),
        P("dp", None),
    )
    return jax.shard_map(
        on_device,
        mesh=mesh,
        in_specs=placed,
        out_specs=(
            P("dp", None),
            P("dp", None),
            P(None, None, "tensor"),
            P("tensor", None),
            P(None, "tensor"),
            P(None, None, "tensor"),
            P("tensor", None),
            P(None, None, "tensor"),
            P(None, "tensor", None),
            P(),
            P(),
        ),
        check_vma=False,
    )
```
